32 devices in a mesh: batch: 8 (over y, x, core), seq: 4 (over z).
Axes of the slice: x: 2, y: 2, z: 4, core: 2. Of those that a mesh axis runs over, the one named last changes fastest.
Arguments:
- inputs: bfloat16 [16, 1728, 1024], P('batch', 'seq'), may hold values from -6 to 6
- timesteps: int32 [16], P('batch'), may hold values from 0 to 4999
- segments: int32 [16, 1728], P('batch'), may hold values from 0 to 13, as said below
- cotangent: bfloat16 [16, 1728, 1024], P('batch', 'seq'), may hold values from -6 to 6
- w_qkv: bfloat16 [1024, 3072], replicated, may hold values from -0.1875 to 0.1875
- b_query: bfloat16 [1024], replicated, may hold values from -3 to 3
- b_value: bfloat16 [1024], replicated, may hold values from -3 to 3
- w_out: bfloat16 [1024, 1024], replicated, may hold values from -1.5 to 1.5
- b_out: bfloat16 [1024], replicated, may hold values from -3 to 3
- ln1_gain: bfloat16 [1024], replicated, may hold values from 0.25 to 1.75
- ln1_bias: bfloat16 [1024], replicated, may hold values from -3 to 3
- w_up: bfloat16 [1024, 4096], replicated, may hold values from -0.1875 to 0.1875
- b_up: bfloat16 [4096], replicated, may hold values from -3 to 3
- w_down: bfloat16 [4096, 1024], replicated, may hold values from -0.09375 to 0.09375
- b_down: bfloat16 [1024], replicated, may hold values from -3 to 3
- ln2_gain: bfloat16 [1024], replicated, may hold values from 0.25 to 1.75
- ln2_bias: bfloat16 [1024], replicated, may hold values from -3 to 3
- w_time: bfloat16 [1024], replicated, may hold values from -4 to 4
- b_time: bfloat16 [1024], replicated, may hold values from -3 to 3
Outputs:
- output: bfloat16 [16, 1728, 1024], P('batch', 'seq')
- grad_inputs: bfloat16 [16, 1728, 1024], P('batch', 'seq')
- grad_w_qkv: float32 [1024, 3072], P(('batch', 'seq'))
- grad_b_query: float32 [1024], P(('batch', 'seq'))
- grad_b_value: float32 [1024], P(('batch', 'seq'))
- grad_w_out: float32 [1024, 1024], P(('batch', 'seq'))
- grad_b_out: float32 [1024], P(('batch', 'seq'))
- grad_ln1_gain: float32 [1024], P(('batch', 'seq'))
- grad_ln1_bias: float32 [1024], P(('batch', 'seq'))
- grad_w_up: float32 [1024, 4096], P(('batch', 'seq'))
- grad_b_up: float32 [4096], P(('batch', 'seq'))
- grad_w_down: float32 [4096, 1024], P(('batch', 'seq'))
- grad_b_down: float32 [1024], P(('batch', 'seq'))
- grad_ln2_gain: float32 [1024], P(('batch', 'seq'))
- grad_ln2_bias: float32 [1024], P(('batch', 'seq'))
- grad_w_time: float32 [1024], P(('batch', 'seq'))
- grad_b_time: float32 [1024], P(('batch', 'seq'))
The draws below stay inside these ranges and needn't reach their ends.
Inputs may be any that keep to these rules, and one draw needn't show every extreme that they name: `segments`: in each sequence the ids rise by one from item to item, starting at 1 at position 0, over the first 1664 positions; the last 64 positions carry 0. Items are 512 or 128 positions long, except that in each index of batch one sequence is a single item. Padding positions attend only to padding.
All inputs are finite; a program needn't handle non-finite values.
Results may differ from the reference program's by a relative error of at most 0.014.
Values may be sent and summed in bfloat16 or wider, within the bound.
No kernel may reach another device: no remote copies, remote signals or barrier semaphores. Data moves between devices by JAX's collectives and lax.ppermute only.
A program may use at most 256 MiB of HBM per device.

```python
import jax
import jax.numpy as jnp
from jax import lax

D = 1024
HEADS = 16
FF = 4096
GROUP_SEQS = 2
LONG = 512
SHORT = 128
PAD = 64
TSTEPS = 5000
SEQ_LEN = 1728
SEQUENCES = 16


def draw_segments(key, part):
    key = jax.random.fold_in(key, 7)
    item_slots = (3 * LONG + SHORT) // SHORT
    filled = 3 * LONG + SHORT
    length = filled + PAD
    groups = SEQUENCES // GROUP_SEQS
    row_count = SEQUENCES
    key_pick, key_longs, key_order = jax.random.split(key, 3)
    chosen = jax.random.randint(key_pick, (groups, 1), 0, GROUP_SEQS)
    member = jnp.arange(GROUP_SEQS)[None, :]
    single = (member == chosen).reshape(-1)
    forced_many = (member == (chosen + 1) % GROUP_SEQS).reshape(-1)
    long_count = jax.random.randint(key_longs, (row_count,), 0, 4)
    long_count = jnp.where(forced_many, 0, long_count)
    item_count = long_count + (3 - long_count) * 4 + 1
    slot_index = jnp.arange(item_slots)[None, :]
    order_values = jax.random.randint(key_order, (row_count, item_slots), 0, 1 << 20) * item_slots + slot_index
    slot_live = slot_index < item_count[:, None]
    slot_rank = jnp.sum((order_values[:, None, :] < order_values[:, :, None]) & slot_live[:, None, :], axis=2)
    is_long = slot_live & (slot_rank < long_count[:, None])
    item_sizes = jnp.where(slot_live, jnp.where(is_long, LONG, SHORT), 0)
    item_starts = jnp.cumsum(item_sizes, axis=1) - item_sizes
    position = jnp.arange(length)
    segment_ids = jnp.sum((item_starts[:, None, :] <= position[None, :, None]) & slot_live[:, None, :], axis=2)
    inside = position[None, :] < filled
    segment_ids = jnp.where(inside, segment_ids, 0)
    segment_ids = jnp.where(single[:, None] & inside, 1, segment_ids)
    return segment_ids.astype(jnp.int32)


def touch_ends(values, rng, smallest, high):
    spot = [jax.random.randint(jax.random.fold_in(rng, axis), (), 0, length) for axis, length in enumerate(values.shape)]
    widest = values.shape.index(max(values.shape))
    neighbour = spot[:widest] + [(spot[widest] + 1) % values.shape[widest]] + spot[widest + 1:]
    return values.at[tuple(spot)].set(smallest).at[tuple(neighbour)].set(high)


def strengthened(values, rng, source, target, shards_of, factor):
    owner, partner = [(jnp.arange(values.shape[axis_at]) // (values.shape[axis_at] // shards_of)).reshape([-1 if axis == axis_at else 1 for axis in range(values.ndim)]) for axis_at in (source, target)]
    chosen = jax.random.permutation(rng, shards_of)[partner]
    strong = (owner == chosen) | (owner == (partner + shards_of // 2) % shards_of)
    return jnp.where(strong, factor * values, values)


def level_of(stream_key, shape, cuts, smallest, largest):
    factor_of = 1.0
    for axis_at, shards_of in cuts:
        steps = jax.random.uniform(jax.random.fold_in(jax.random.fold_in(stream_key, 6), axis_at), (shards_of,), jnp.float32, smallest / len(cuts), largest / len(cuts))
        factor_of = factor_of * jnp.repeat(jnp.exp(steps), shape[axis_at] // shards_of).reshape((-1,) + (1,) * (len(shape) - 1 - axis_at))
    return factor_of


def gaussian(own_key, shape, spread, most, cuts=(), held_as=jnp.bfloat16):
    loudness = level_of(own_key, shape, cuts, -0.22, 0.18) if cuts else 1.0
    values = jax.random.normal(own_key, shape, jnp.float32) * spread * loudness
    return jnp.minimum(jnp.maximum(values, -most), most).astype(held_as)


def bell_draw_with(stream_key, extent, width, reach, cuts, heavy, kind=jnp.bfloat16):
    values = width * jax.random.normal(stream_key, extent, jnp.float32)
    if cuts:
        values = values * level_of(stream_key, extent, cuts, -0.22, 0.18)
    return jnp.clip(strengthened(values, jax.random.fold_in(stream_key, 3), *heavy), -reach, reach).astype(kind)


def setup_inputs(seed: int = 0) -> dict:
    streams_of = jax.random.split(jax.random.key(seed), 20)
    return {
        "inputs": gaussian(streams_of[0], (SEQUENCES, SEQ_LEN, D), 1.0, 6.0, ((0, 8), (1, 4))),
        "timesteps": touch_ends(jax.random.randint(streams_of[1], (SEQUENCES,), 0, TSTEPS), jax.random.fold_in(streams_of[1], 1), 0, TSTEPS - 1).astype(jnp.int32),
        "segments": draw_segments(jax.random.fold_in(streams_of[19], 71), 0),
        "cotangent": bell_draw_with(streams_of[3], (SEQUENCES, SEQ_LEN, D), 1.0, 6.0, ((0, 8), (1, 4)), (0, 2, 8, 2.0)),
        "w_qkv": gaussian(streams_of[4], (D, 3 * D), D ** -0.5, 0.1875),
        "b_query": gaussian(streams_of[5], (D,), 0.5, 3.0),
        "b_value": gaussian(streams_of[6], (D,), 0.5, 3.0),
        "w_out": gaussian(streams_of[7], (D, D), (D // 64) ** -0.5, 1.5),
        "b_out": gaussian(streams_of[8], (D,), 0.5, 3.0),
        "ln1_gain": jnp.clip(1.0 + 0.15 * jax.random.normal(streams_of[9], (D,), jnp.float32), 0.25, 1.75).astype(jnp.bfloat16),
        "ln1_bias": gaussian(streams_of[10], (D,), 0.5, 3.0),
        "w_up": gaussian(streams_of[11], (D, FF), D ** -0.5, 0.1875),
        "b_up": gaussian(streams_of[12], (FF,), 0.5, 3.0),
        "w_down": gaussian(streams_of[13], (FF, D), FF ** -0.5, 0.09375),
        "b_down": gaussian(streams_of[14], (D,), 0.5, 3.0),
        "ln2_gain": jnp.clip(1.0 + 0.15 * jax.random.normal(streams_of[15], (D,), jnp.float32), 0.25, 1.75).astype(jnp.bfloat16),
        "ln2_bias": gaussian(streams_of[16], (D,), 0.5, 3.0),
        "w_time": gaussian(streams_of[17], (D,), 1.0, 4.0),
        "b_time": gaussian(streams_of[18], (D,), 0.5, 3.0),
    }


@jax.custom_vjp
def low(v):
    return lax.optimization_barrier(v.astype(jnp.bfloat16)).astype(jnp.float32)

@jax.custom_vjp
def low_back(v):
    return v

def low_keep(v):
    return (low(v), None)

def low_pass(kept, grad):
    return (grad,)

def back_keep(v):
    return (v, None)

def back_low(kept, grad):
    return (low(grad),)
low.defvjp(low_keep, low_pass)
low_back.defvjp(back_keep, back_low)
highest = lax.Precision.HIGHEST

def rounded_both(values):
    return low(low_back(values))

def layer_norm(values, gain, shift):
    centered = values - lax.optimization_barrier(jnp.mean(values, axis=-1, keepdims=True))
    variance = lax.optimization_barrier(jnp.mean(centered * centered, axis=-1, keepdims=True))
    return centered * lax.rsqrt(variance + 1e-05) * gain + shift

def attend(queries, key_rows, value_rows, segments):
    seq_count, length, model_width = queries.shape
    head_dim = model_width // HEADS
    block_len = length // 3
    query_blocks = jnp.moveaxis(queries.reshape(seq_count, 3, block_len, HEADS, head_dim), 1, 0)
    segment_blocks = jnp.moveaxis(segments.reshape(seq_count, 3, block_len), 1, 0)
    key_heads = key_rows.reshape(seq_count, length, HEADS, head_dim)
    value_heads = value_rows.reshape(seq_count, length, HEADS, head_dim)

    def one_block(pieces):
        query_part, segment_part = pieces
        scores = low_back(jnp.einsum('bqhd,bkhd->bhqk', query_part, key_heads, precision=highest) * head_dim ** (-0.5))
        allowed = segment_part[:, None, :, None] == segments[:, None, None, :]
        masked = jnp.where(allowed, scores, -1e+30)
        maxima = lax.optimization_barrier(jnp.max(masked, axis=-1, keepdims=True))
        exp_scores = jnp.exp(masked - maxima)
        prob_weights = exp_scores / lax.optimization_barrier(jnp.sum(exp_scores, axis=-1, keepdims=True))
        return jnp.einsum('bhqk,bkhd->bqhd', low(prob_weights), value_heads, precision=highest)
    contexts = lax.map(jax.checkpoint(one_block), (query_blocks, segment_blocks))
    return jnp.moveaxis(contexts, 0, 1).reshape(seq_count, length, model_width)

def forward(weight_list, inputs, fraction, segments):
    w_qkv, b_query, b_value, w_out, b_out, ln1_gain, ln1_bias, w_up, b_up, w_down, b_down, ln2_gain, ln2_bias, w_time, b_time = weight_list
    model_width = inputs.shape[-1]
    start_sum = inputs + fraction[:, None, None] * w_time + b_time
    start_low = low(start_sum)
    projected = jnp.einsum('bld,de->ble', start_low, w_qkv, precision=highest)
    queries = rounded_both(projected[..., :model_width] + b_query)
    key_rows = rounded_both(projected[..., model_width:2 * model_width])
    value_rows = rounded_both(projected[..., 2 * model_width:] + b_value)
    context = rounded_both(attend(queries, key_rows, value_rows, segments))
    attn_out = low_back(jnp.einsum('bld,de->ble', context, w_out, precision=highest)) + b_out
    normed = layer_norm(start_sum + attn_out, ln1_gain, ln1_bias)
    hidden_pre = low_back(jnp.einsum('bld,df->blf', low(normed), w_up, precision=highest)) + b_up
    activated = low(jax.nn.gelu(hidden_pre, approximate=False))
    ffn_out = low_back(jnp.einsum('blf,fd->bld', activated, w_down, precision=highest)) + b_down
    return layer_norm(normed + ffn_out, ln2_gain, ln2_bias)

def reference(inputs, timesteps, segments, cotangent, w_qkv, b_query, b_value, w_out, b_out, ln1_gain, ln1_bias, w_up, b_up, w_down, b_down, ln2_gain, ln2_bias, w_time, b_time):
    weights = tuple((item.astype(jnp.float32) for item in (w_qkv, b_query, b_value, w_out, b_out, ln1_gain, ln1_bias, w_up, b_up, w_down, b_down, ln2_gain, ln2_bias, w_time, b_time)))
    pair_count = SEQUENCES // 2

    def stacked(array):
        return array.reshape((pair_count, 2) + array.shape[1:])

    def scan_step(totals, block_data):
        block_inputs, block_times, block_segments, block_cotangent = block_data
        fraction = block_times.astype(jnp.float32) / TSTEPS

        def layer_run(weight_list, layer_inputs):
            return forward(weight_list, layer_inputs, fraction, block_segments)
        result, pull_back = jax.vjp(layer_run, weights, block_inputs.astype(jnp.float32))
        weight_grads, input_grads = pull_back(block_cotangent.astype(jnp.float32))
        totals = jax.tree.map(jnp.add, totals, weight_grads)
        return (totals, (result.astype(jnp.bfloat16), input_grads.astype(jnp.bfloat16)))
    zero_grads = jax.tree.map(jnp.zeros_like, weights)
    totals, (outputs, input_grads) = lax.scan(scan_step, zero_grads, (stacked(inputs), stacked(timesteps), stacked(segments), stacked(cotangent)))
    grad_w_qkv, grad_b_query, grad_b_value, grad_w_out, grad_b_out, grad_ln1_gain, grad_ln1_bias, grad_w_up, grad_b_up, grad_w_down, grad_b_down, grad_ln2_gain, grad_ln2_bias, grad_w_time, grad_b_time = totals
    full_shape = inputs.shape
    return (outputs.reshape(full_shape), input_grads.reshape(full_shape), grad_w_qkv, grad_b_query, grad_b_value, grad_w_out, grad_b_out, grad_ln1_gain, grad_ln1_bias, grad_w_up, grad_b_up, grad_w_down, grad_b_down, grad_ln2_gain, grad_ln2_bias, grad_w_time, grad_b_time)
```

```python
import functools

import jax
import jax.numpy as jnp
from jax import lax
from jax.experimental import pallas as pl
from jax.experimental.pallas import tpu as pltpu
from jax.sharding import PartitionSpec as P

D = 1024
HEADS = 16
TSTEPS = 5000
AXES = ("batch", "seq")


BF=jnp.bfloat16; F32=jnp.float32
NT=(((1,),(1,)),((),())); NN=(((1,),(0,)),((),())); TN=(((0,),(0,)),((),()))
def dot(a,b,d): return lax.dot_general(a,b,d,preferred_element_type=F32)
FILLED=1664; PAD=64
def lanes(rows):
    return lax.broadcasted_iota(jnp.int32,(rows,128),1)
def parts3(x):
    a=x.astype(BF).astype(F32); r=x-a; b=r.astype(BF).astype(F32); c=r-b
    return a,b,c
def augment(base,h,x,lane):
    a,b,c=parts3(x)
    o=(1-h)*64
    f=base.astype(F32)
    f=jnp.where((lane>=o)&(lane<o+64),jnp.where(lane==o,a,jnp.where(lane==o+1,b,jnp.where(lane==o+2,c,0.0))),f)
    return f.astype(BF)
def ones3(base,h,lane,n=3):
    o=(1-h)*64
    f=base.astype(F32)
    f=jnp.where((lane>=o)&(lane<o+64),jnp.where(lane<o+n,1.0,0.0),f)
    return f.astype(BF)
def fwd_item(q_ref,k_ref,v_ref,o_ref,ol_ref,qa_ref,off,n,bq):
    k=k_ref[pl.ds(off,n),:]
    v=v_ref[pl.ds(off,n),:]
    lk=lanes(n)
    vs=[ones3(v,h,lk,1) for h in (0,1)]
    lq=lanes(bq)
    for r in range(n//bq):
        rows=pl.ds(off+r*bq,bq)
        q=q_ref[rows,:]
        outs=[]
        for h in (0,1):
            qh=jnp.where((lq//64)==h,q.astype(F32),0.0).astype(BF)
            s=dot(qh,k,NT)
            m=jnp.max(s,axis=1,keepdims=True)
            p=jnp.exp2(s-m).astype(BF)
            o=dot(p,vs[h],NN)
            l=o[:,(1-h)*64:(1-h)*64+1]
            outs.append(o/l)
            qa_ref[h,rows,:]=augment(q,h,-(m+jnp.log2(l)),lq)
        o=jnp.where(lq<64,outs[0],outs[1])
        o_ref[rows,:]=o.astype(BF)
        ol_ref[rows,:]=(o-o.astype(BF).astype(F32)).astype(BF)
def walk(seg_ref,item,bs):
    single=seg_ref[0]==seg_ref[12]
    @pl.when(single)
    def _():
        item(0,FILLED,bs[0])
    @pl.when(jnp.logical_not(single))
    def _():
        def step(i,c):
            me=seg_ref[i]
            first=(i==0)|(seg_ref[jnp.maximum(i-1,0)]!=me)
            last3=jnp.minimum(i+3,12)
            long=first&(i+3<=12)&(seg_ref[last3]==me)
            off=pl.multiple_of(i*128,128)
            @pl.when(long)
            def _(): item(off,512,bs[1])
            @pl.when(first&jnp.logical_not(long))
            def _(): item(off,128,bs[2])
            return c
        lax.fori_loop(0,13,step,0)
    item(FILLED,PAD,PAD)
def fwd_kernel(bs,seg_ref,q_ref,k_ref,v_ref,o_ref,ol_ref,qa_ref):
    walk(seg_ref,functools.partial(fwd_item,q_ref,k_ref,v_ref,o_ref,ol_ref,qa_ref),bs)
def attn_fwd(seg13,qkv,bs=(832,256,128)):
    L,W3=qkv.shape; W=W3//3; n=W//128
    spec=lambda j: pl.BlockSpec((L,128),lambda p,s,j=j:(0,p+j*n))
    return pl.pallas_call(functools.partial(fwd_kernel,bs),
        out_shape=(jax.ShapeDtypeStruct((L,W),BF),)*2+(jax.ShapeDtypeStruct((2*n,L,128),BF),),
        grid_spec=pltpu.PrefetchScalarGridSpec(num_scalar_prefetch=1,grid=(n,),
            in_specs=[spec(0),spec(1),spec(2)],
            out_specs=(pl.BlockSpec((L,128),lambda p,s:(0,p)),pl.BlockSpec((L,128),lambda p,s:(0,p)),pl.BlockSpec((2,L,128),lambda p,s:(p,0,0)))),
        compiler_params=pltpu.CompilerParams(vmem_limit_bytes=50<<20),name="attn_forward",
        cost_estimate=pl.CostEstimate(flops=2*2*2*n*L*L*256,bytes_accessed=10*L*W,transcendentals=2*n*L*L))(seg13,qkv,qkv,qkv)
def bwd_item(mode,qa_ref,k_ref,v_ref,o_ref,ol_ref,g_ref,dq_ref,dk_ref,dv_ref,acc,off,n,bk):
    item=pl.ds(off,n)
    ln=lanes(n)
    g=g_ref[item,:]
    prod=g.astype(F32)*(o_ref[item,:].astype(F32)+ol_ref[item,:].astype(F32))
    lb=lanes(bk)
    nb=n//bk
    gas=[augment(g,h,-jnp.sum(jnp.where((ln//64)==h,prod,0.0),axis=1,keepdims=True),ln) for h in (0,1)]
    for b in range(nb):
        rows=pl.ds(off+b*bk,bk)
        k=k_ref[rows,:]; v=v_ref[rows,:]
        dks=[];dvs=[]
        for h in (0,1):
            ga=gas[h]
            qa=qa_ref[h,item,:]
            kh=ones3(k,h,lb); vh=ones3(v,h,lb)
            p=jnp.exp2(dot(kh,qa,NT))
            d=dot(vh,ga,NT)
            ds=(p*d).astype(BF)
            dvs.append(dot(p.astype(BF),ga,NN))
            dks.append(dot(ds,qa,NN))
            if mode=='TN':
                dq=dot(ds,kh,TN)
                if b==0: acc[h,item,:]=dq
                else: acc[h,item,:]+=dq
        dk_ref[rows,:]=(jnp.where(lb<64,dks[0],dks[1])*0.6931471805599453).astype(BF)
        dv_ref[rows,:]=jnp.where(lb<64,dvs[0],dvs[1]).astype(BF)
    dq_ref[item,:]=(jnp.where(ln<64,acc[0,item,:],acc[1,item,:])*0.125).astype(BF)
def bwd_kernel(bs,mode,seg_ref,qa_ref,k_ref,v_ref,o_ref,ol_ref,g_ref,dq_ref,dk_ref,dv_ref,acc):
    walk(seg_ref,functools.partial(bwd_item,mode,qa_ref,k_ref,v_ref,o_ref,ol_ref,g_ref,dq_ref,dk_ref,dv_ref,acc),bs)
def attn_bwd(seg13,qa,qkv,o,ol,g,bs=(832,256,128),mode='TN'):
    L,W3=qkv.shape; W=W3//3; n=W//128
    spec=lambda j: pl.BlockSpec((L,128),lambda p,s,j=j:(0,p+j*n))
    one=pl.BlockSpec((L,128),lambda p,s:(0,p))
    return pl.pallas_call(functools.partial(bwd_kernel,bs,mode),
        out_shape=(jax.ShapeDtypeStruct((L,W),BF),)*3,
        grid_spec=pltpu.PrefetchScalarGridSpec(num_scalar_prefetch=1,grid=(n,),
            in_specs=[pl.BlockSpec((2,L,128),lambda p,s:(p,0,0)),spec(1),spec(2),one,one,one],
            out_specs=(one,one,one),
            scratch_shapes=[pltpu.VMEM((2,L,128),F32)]),
        compiler_params=pltpu.CompilerParams(vmem_limit_bytes=50<<20),name="attn_backward",
        cost_estimate=pl.CostEstimate(flops=5*2*2*n*L*L*256,bytes_accessed=16*L*W,transcendentals=2*n*L*L))(seg13,qa,qkv,qkv,o,ol,g)


def gelu_exact(values):
    return jax.nn.gelu(values, approximate=False)


def norm_forward(values, gain, shift):
    centered = values - jnp.mean(values, axis=-1, keepdims=True)
    inverse = lax.rsqrt(jnp.mean(centered * centered, axis=-1, keepdims=True) + 1e-05)
    unit_part = centered * inverse
    return (unit_part * gain + shift, unit_part, inverse)


def norm_backward(grad_out, unit_part, inverse, gain):
    scaled = grad_out * gain
    centered = scaled - jnp.mean(scaled, axis=-1, keepdims=True)
    grad_in = inverse * (
        centered - unit_part * jnp.mean(scaled * unit_part, axis=-1, keepdims=True)
    )
    return (grad_in, jnp.sum(grad_out * unit_part, axis=0), jnp.sum(grad_out, axis=0))


def attention_forward(query_all, key_all, value_all, segments, head_dim):
    length, local_width = (query_all.shape[1], query_all.shape[2])
    head_count = local_width // head_dim
    block_len = length // 3
    score_scale = head_dim ** (-0.5)

    def per_sequence(pieces):
        queries, key_rows, value_rows, seq_ids = pieces
        key_heads = key_rows.reshape(length, head_count, head_dim)
        value_heads = value_rows.reshape(length, head_count, head_dim)

        def per_block(block_pieces):
            query_part, id_part = block_pieces
            query_heads = query_part.reshape(block_len, head_count, head_dim)
            scores = (
                jnp.einsum(
                    "qhd,khd->hqk", query_heads, key_heads, preferred_element_type=jnp.float32
                )
                * score_scale
            )
            masked = jnp.where(id_part[None, :, None] == seq_ids[None, None, :], scores, -1e30)
            maxima = jnp.max(masked, axis=-1, keepdims=True)
            exp_scores = jnp.exp(masked - maxima)
            totals = jnp.sum(exp_scores, axis=-1, keepdims=True)
            weights_low = (exp_scores / totals).astype(jnp.bfloat16)
            context = jnp.einsum(
                "hqk,khd->qhd", weights_low, value_heads, preferred_element_type=jnp.float32
            )
            return (
                context.astype(jnp.bfloat16).reshape(block_len, local_width),
                (maxima + jnp.log(totals))[..., 0],
            )

        contexts, logsums = lax.map(
            per_block, (queries.reshape(3, block_len, local_width), seq_ids.reshape(3, block_len))
        )
        return (contexts.reshape(length, local_width), logsums)

    return lax.map(per_sequence, (query_all, key_all, value_all, segments))


def attention_backward(query_all, key_all, value_all, segments, logsums, grad_all, head_dim):
    length, local_width = (query_all.shape[1], query_all.shape[2])
    head_count = local_width // head_dim
    block_len = length // 3
    score_scale = head_dim ** (-0.5)

    def per_sequence(pieces):
        queries, key_rows, value_rows, seq_ids, sum_rows, grad_rows = pieces
        key_heads = key_rows.reshape(length, head_count, head_dim)
        value_heads = value_rows.reshape(length, head_count, head_dim)

        def per_block(carry, block_pieces):
            key_total, value_total = carry
            query_part, id_part, sum_part, grad_part = block_pieces
            query_heads = query_part.reshape(block_len, head_count, head_dim)
            grad_heads = grad_part.reshape(block_len, head_count, head_dim)
            scores = (
                jnp.einsum(
                    "qhd,khd->hqk", query_heads, key_heads, preferred_element_type=jnp.float32
                )
                * score_scale
            )
            allowed = id_part[None, :, None] == seq_ids[None, None, :]
            prob_weights = jnp.where(allowed, jnp.exp(scores - sum_part[:, :, None]), 0.0)
            grad_probs = jnp.einsum(
                "qhd,khd->hqk", grad_heads, value_heads, preferred_element_type=jnp.float32
            )
            delta = jnp.sum(prob_weights * grad_probs, axis=-1, keepdims=True)
            grad_scores = (prob_weights * (grad_probs - delta)).astype(jnp.bfloat16)
            query_grad = (
                jnp.einsum(
                    "hqk,khd->qhd", grad_scores, key_heads, preferred_element_type=jnp.float32
                )
                * score_scale
            )
            key_total = (
                key_total
                + jnp.einsum(
                    "hqk,qhd->khd", grad_scores, query_heads, preferred_element_type=jnp.float32
                )
                * score_scale
            )
            value_total = value_total + jnp.einsum(
                "hqk,qhd->khd",
                prob_weights.astype(jnp.bfloat16),
                grad_heads,
                preferred_element_type=jnp.float32,
            )
            return (
                (key_total, value_total),
                query_grad.astype(jnp.bfloat16).reshape(block_len, local_width),
            )

        zero_heads = jnp.zeros((length, head_count, head_dim), jnp.float32)
        (key_total, value_total), query_grads = lax.scan(
            per_block,
            (zero_heads, zero_heads),
            (
                queries.reshape(3, block_len, local_width),
                seq_ids.reshape(3, block_len),
                sum_rows,
                grad_rows.reshape(3, block_len, local_width),
            ),
        )
        return (
            query_grads.reshape(length, local_width),
            key_total.astype(jnp.bfloat16).reshape(length, local_width),
            value_total.astype(jnp.bfloat16).reshape(length, local_width),
        )

    return lax.map(per_sequence, (query_all, key_all, value_all, segments, logsums, grad_all))


def per_device(
    inputs,
    timesteps,
    segments,
    cotangent,
    w_qkv,
    b_query,
    b_value,
    w_out,
    b_out,
    ln1_gain,
    ln1_bias,
    w_up,
    b_up,
    w_down,
    b_down,
    ln2_gain,
    ln2_bias,
    w_time,
    b_time,
):
    groups, local_len, model_width = inputs.shape
    row_count = groups * local_len
    head_dim = D // HEADS
    fraction = timesteps.astype(jnp.float32) / TSTEPS
    start_sum = (
        inputs.astype(jnp.float32)
        + fraction[:, None, None] * w_time.astype(jnp.float32)
        + b_time.astype(jnp.float32)
    )
    start_low = start_sum.astype(jnp.bfloat16)
    projected = jnp.einsum("bld,de->ble", start_low, w_qkv, preferred_element_type=jnp.float32)
    query_low = (projected[..., :model_width] + b_query.astype(jnp.float32)).astype(jnp.bfloat16)
    key_low = projected[..., model_width : 2 * model_width].astype(jnp.bfloat16)
    value_low = (projected[..., 2 * model_width :] + b_value.astype(jnp.float32)).astype(
        jnp.bfloat16
    )
    query_all, key_all, value_all = (
        lax.all_to_all(query_low, "seq", split_axis=2, concat_axis=1, tiled=True),
        lax.all_to_all(key_low, "seq", split_axis=2, concat_axis=1, tiled=True),
        lax.all_to_all(value_low, "seq", split_axis=2, concat_axis=1, tiled=True),
    )
    context_heads, logsums = attention_forward(query_all, key_all, value_all, segments, head_dim)
    context = lax.all_to_all(context_heads, "seq", split_axis=1, concat_axis=2, tiled=True)
    context_rows = context.reshape(row_count, model_width)
    start_rows = start_sum.reshape(row_count, model_width)
    residual_one = (
        start_rows
        + jnp.dot(context_rows, w_out, preferred_element_type=jnp.float32)
        + b_out.astype(jnp.float32)
    )
    normed, unit_one, inverse_one = norm_forward(
        residual_one, ln1_gain.astype(jnp.float32), ln1_bias.astype(jnp.float32)
    )
    normed_low = normed.astype(jnp.bfloat16)
    hidden_pre = jnp.dot(normed_low, w_up, preferred_element_type=jnp.float32) + b_up.astype(
        jnp.float32
    )
    activated, gelu_pull = jax.vjp(gelu_exact, hidden_pre)
    activated_low = activated.astype(jnp.bfloat16)
    residual_two = (
        normed
        + jnp.dot(activated_low, w_down, preferred_element_type=jnp.float32)
        + b_down.astype(jnp.float32)
    )
    result, unit_two, inverse_two = norm_forward(
        residual_two, ln2_gain.astype(jnp.float32), ln2_bias.astype(jnp.float32)
    )
    output = result.astype(jnp.bfloat16).reshape(groups, local_len, model_width)
    grad_result = cotangent.reshape(row_count, model_width).astype(jnp.float32)
    grad_two, grad_ln2_gain, grad_ln2_bias = norm_backward(
        grad_result, unit_two, inverse_two, ln2_gain.astype(jnp.float32)
    )
    grad_b_down = jnp.sum(grad_two, axis=0)
    grad_two_low = grad_two.astype(jnp.bfloat16)
    grad_w_down = jnp.einsum(
        "rf,rd->fd", activated_low, grad_two_low, preferred_element_type=jnp.float32
    )
    grad_activated = jnp.einsum(
        "rd,fd->rf", grad_two_low, w_down, preferred_element_type=jnp.float32
    )
    grad_hidden = gelu_pull(grad_activated)[0]
    grad_b_up = jnp.sum(grad_hidden, axis=0)
    grad_hidden_low = grad_hidden.astype(jnp.bfloat16)
    grad_w_up = jnp.einsum(
        "rd,rf->df", normed_low, grad_hidden_low, preferred_element_type=jnp.float32
    )
    grad_normed = grad_two + jnp.einsum(
        "rf,df->rd", grad_hidden_low, w_up, preferred_element_type=jnp.float32
    )
    grad_one, grad_ln1_gain, grad_ln1_bias = norm_backward(
        grad_normed, unit_one, inverse_one, ln1_gain.astype(jnp.float32)
    )
    grad_b_out = jnp.sum(grad_one, axis=0)
    grad_one_low = grad_one.astype(jnp.bfloat16)
    grad_w_out = jnp.einsum(
        "rd,re->de", context_rows, grad_one_low, preferred_element_type=jnp.float32
    )
    grad_context = (
        jnp.einsum("re,de->rd", grad_one_low, w_out, preferred_element_type=jnp.float32)
        .astype(jnp.bfloat16)
        .reshape(groups, local_len, model_width)
    )
    grad_context_heads = lax.all_to_all(
        grad_context, "seq", split_axis=2, concat_axis=1, tiled=True
    )
    query_grads, key_grads, value_grads = attention_backward(
        query_all, key_all, value_all, segments, logsums, grad_context_heads, head_dim
    )
    grad_query, grad_key, grad_value = (
        lax.all_to_all(query_grads, "seq", split_axis=1, concat_axis=2, tiled=True),
        lax.all_to_all(key_grads, "seq", split_axis=1, concat_axis=2, tiled=True),
        lax.all_to_all(value_grads, "seq", split_axis=1, concat_axis=2, tiled=True),
    )
    grad_projected = jnp.concatenate((grad_query, grad_key, grad_value), axis=2).reshape(
        row_count, 3 * model_width
    )
    grad_w_qkv = jnp.einsum(
        "rd,re->de",
        start_low.reshape(row_count, model_width),
        grad_projected,
        preferred_element_type=jnp.float32,
    )
    grad_b_query = jnp.sum(grad_query.astype(jnp.float32), axis=(0, 1))
    grad_b_value = jnp.sum(grad_value.astype(jnp.float32), axis=(0, 1))
    grad_start = grad_one + jnp.einsum(
        "re,de->rd", grad_projected, w_qkv, preferred_element_type=jnp.float32
    )
    grad_inputs = grad_start.astype(jnp.bfloat16).reshape(groups, local_len, model_width)
    per_sequence_grad = jnp.sum(grad_start.reshape(groups, local_len, model_width), axis=1)
    grad_w_time = jnp.einsum("g,gd->d", fraction, per_sequence_grad)
    grad_b_time = jnp.sum(per_sequence_grad, axis=0)
    (
        sum_w_qkv,
        sum_b_query,
        sum_b_value,
        sum_w_out,
        sum_b_out,
        sum_ln1_gain,
        sum_ln1_bias,
        sum_w_up,
        sum_b_up,
        sum_w_down,
        sum_b_down,
        sum_ln2_gain,
        sum_ln2_bias,
        sum_w_time,
        sum_b_time,
    ) = (
        lax.psum_scatter(grad_w_qkv, ("batch", "seq"), scatter_dimension=0, tiled=True),
        lax.psum_scatter(grad_b_query, ("batch", "seq"), scatter_dimension=0, tiled=True),
        lax.psum_scatter(grad_b_value, ("batch", "seq"), scatter_dimension=0, tiled=True),
        lax.psum_scatter(grad_w_out, ("batch", "seq"), scatter_dimension=0, tiled=True),
        lax.psum_scatter(grad_b_out, ("batch", "seq"), scatter_dimension=0, tiled=True),
        lax.psum_scatter(grad_ln1_gain, ("batch", "seq"), scatter_dimension=0, tiled=True),
        lax.psum_scatter(grad_ln1_bias, ("batch", "seq"), scatter_dimension=0, tiled=True),
        lax.psum_scatter(grad_w_up, ("batch", "seq"), scatter_dimension=0, tiled=True),
        lax.psum_scatter(grad_b_up, ("batch", "seq"), scatter_dimension=0, tiled=True),
        lax.psum_scatter(grad_w_down, ("batch", "seq"), scatter_dimension=0, tiled=True),
        lax.psum_scatter(grad_b_down, ("batch", "seq"), scatter_dimension=0, tiled=True),
        lax.psum_scatter(grad_ln2_gain, ("batch", "seq"), scatter_dimension=0, tiled=True),
        lax.psum_scatter(grad_ln2_bias, ("batch", "seq"), scatter_dimension=0, tiled=True),
        lax.psum_scatter(grad_w_time, ("batch", "seq"), scatter_dimension=0, tiled=True),
        lax.psum_scatter(grad_b_time, ("batch", "seq"), scatter_dimension=0, tiled=True),
    )
    return (
        output,
        grad_inputs,
        sum_w_qkv,
        sum_b_query,
        sum_b_value,
        sum_w_out,
        sum_b_out,
        sum_ln1_gain,
        sum_ln1_bias,
        sum_w_up,
        sum_b_up,
        sum_w_down,
        sum_b_down,
        sum_ln2_gain,
        sum_ln2_bias,
        sum_w_time,
        sum_b_time,
    )


LOG2E = 1.4426950408889634


class Plan:
    def __init__(self, mesh):
        sizes = dict(mesh.shape)
        self.batch, self.depth = sizes["batch"], sizes["seq"]
        chips = self.batch // 2
        side = 1
        while side * side < chips:
            side *= 2
        self.nx, self.ny = side, chips // side

    def perm(self, target):
        pairs = []
        for y in range(self.ny):
            for x in range(self.nx):
                for c in range(2):
                    for z in range(self.depth):
                        to = target(y, x, c, z)
                        if to is not None:
                            pairs.append((self.index(y, x, c, z), self.index(*to)))
        return pairs

    def index(self, y, x, c, z):
        return ((y * self.nx + x) * 2 + c) * self.depth + z

    def send(self, value, target):
        return lax.ppermute(value, AXES, self.perm(target))

    def sibling(self, value):
        return self.send(value, lambda y, x, c, z: (y, x, 1 - c, z))


def pick(array, index, axis):
    return lax.dynamic_index_in_dim(array, index, axis, keepdims=False)


def scatter_sum(plan, terms, order, where):
    y, x, z = where
    for axis in order:
        if axis == "x":
            if plan.nx == 1:
                terms = terms[:, 0]
                continue
            at = terms.ndim - 4
            total = pick(terms, x, at).astype(F32)
            for r in range(1, plan.nx):
                got = plan.send(
                    pick(terms, (x + r) % plan.nx, at),
                    lambda y, x, c, z, r=r: (y, (x + r) % plan.nx, c, z),
                )
                total = total + got.astype(F32)
        else:
            total = pick(terms, y, 0).astype(F32)
            for r in range(1, plan.ny):
                got = plan.send(
                    pick(terms, (y + r) % plan.ny, 0),
                    lambda y, x, c, z, r=r: ((y + r) % plan.ny, x, c, z),
                )
                total = total + got.astype(F32)
        terms = total.astype(terms.dtype)
    total = pick(terms, z, 0).astype(F32)
    for r in range(1, plan.depth):
        got = plan.send(
            pick(terms, (z + r) % plan.depth, 0),
            lambda y, x, c, z, r=r: (y, x, c, (z + r) % plan.depth),
        )
        total = total + got.astype(F32)
    return total


def per_chip(
    plan,
    inputs,
    timesteps,
    segments,
    cotangent,
    w_qkv,
    b_query,
    b_value,
    w_out,
    b_out,
    ln1_gain,
    ln1_bias,
    w_up,
    b_up,
    w_down,
    b_down,
    ln2_gain,
    ln2_bias,
    w_time,
    b_time,
):
    local_len = inputs.shape[1]
    rows = 2 * local_len
    length = segments.shape[1]
    b = lax.axis_index("batch")
    z = lax.axis_index("seq")
    c, x, y = b % 2, (b // 2) % plan.nx, b // 2 // plan.nx
    part = z % 2
    where = (y, x, z)
    first = (segments[1, 0] == segments[1, 128 * 12]).astype(jnp.int32)
    which = lambda s: (first + s) % 2
    facts = jnp.concatenate(
        [segments[:, : 128 * 13 : 128], timesteps[:, None], jnp.zeros((2, 2), jnp.int32)], axis=1
    )
    facts = jnp.stack([pick(facts, which(0), 0), pick(facts, which(1), 0)])
    other_facts = plan.sibling(facts)
    facts = jnp.where(z // 2 == c, facts, other_facts)
    mine = pick(facts, z % 2, 0)
    seg13 = mine[:13]
    fraction = mine[13].astype(F32) / TSTEPS

    def gather_rows(array):
        got = [
            plan.send(
                pick(array, which((part + j) % 2), 0),
                lambda y, x, c, z, j=j: (y, x, z // 2, 2 * c + (z + j) % 2),
            )
            for j in (0, 1)
        ]
        return jnp.concatenate(
            [jnp.where(part == 0, got[0], got[1]), jnp.where(part == 0, got[1], got[0])], axis=0
        )

    def spread_rows(array):
        array = array.reshape(2, local_len, array.shape[-1])
        got = [
            plan.send(
                pick(array, (part + j) % 2, 0),
                lambda y, x, c, z, j=j: (y, x, z // 2, 2 * c + (z + j) % 2),
            )
            for j in (0, 1)
        ]
        swap = (part + first) % 2
        return jnp.stack(
            [jnp.where(swap == 0, got[0], got[1]), jnp.where(swap == 0, got[1], got[0])], axis=0
        )

    def whole(own, other):
        return jnp.where(c == 0, jnp.concatenate([own, other]), jnp.concatenate([other, own]))

    def halves(array, axis):
        shape = array.shape
        cut = shape[:axis] + (plan.ny * plan.nx, 2, -1) + shape[axis + 1 :]
        flat = shape[:axis] + (-1,) + shape[axis + 1 :]
        split = array.reshape(cut)
        return (
            pick(split, c, axis + 1).reshape(flat),
            pick(split, 1 - c, axis + 1).reshape(flat),
        )

    def blocks(array):
        return array.reshape(plan.ny, plan.nx, plan.depth, -1, array.shape[-1])

    model = inputs.shape[-1]
    own_inputs = gather_rows(inputs)
    own_cotangent = gather_rows(cotangent)
    start = (
        own_inputs.astype(F32) + fraction * w_time.astype(F32)[None] + b_time.astype(F32)[None]
    )
    start_low = start.astype(BF)
    start_full = whole(start_low, plan.sibling(start_low))
    w_three = w_qkv.reshape(model, 3, model)
    w_own = jnp.concatenate([halves(w_three[:, i], 1)[0] for i in range(3)], axis=1)
    w_oth = jnp.concatenate([halves(w_three[:, i], 1)[1] for i in range(3)], axis=1)
    half = model // 2
    bias = jnp.concatenate(
        [
            halves(b_query.astype(F32), 0)[0],
            jnp.zeros((half,), F32),
            halves(b_value.astype(F32), 0)[0],
        ]
    )
    scale = jnp.where(jnp.arange(3 * half) < half, 0.125 * LOG2E, 1.0)
    qkv = ((jnp.dot(start_full, w_own, preferred_element_type=F32) + bias) * scale).astype(BF)
    context, context_rest, query_rows = attn_fwd(seg13, qkv)
    my_ctx, away_ctx = pick(context.reshape(2, rows, half), c, 0), pick(
        context.reshape(2, rows, half), 1 - c, 0
    )
    ctx_rows = jnp.concatenate([my_ctx, plan.sibling(away_ctx)], axis=1)
    w_out_own, w_out_oth = halves(w_out, 0)
    w_out_cat = jnp.concatenate([w_out_own, w_out_oth])
    residual_one = (
        start + jnp.dot(ctx_rows, w_out_cat, preferred_element_type=F32) + b_out.astype(F32)
    )
    normed, unit_one, inverse_one = norm_forward(
        residual_one, ln1_gain.astype(F32), ln1_bias.astype(F32)
    )
    normed_low = normed.astype(BF)
    hidden_pre = jnp.dot(normed_low, w_up, preferred_element_type=F32) + b_up.astype(F32)
    activated, gelu_pull = jax.vjp(gelu_exact, hidden_pre)
    activated_low = activated.astype(BF)
    residual_two = (
        normed
        + jnp.dot(activated_low, w_down, preferred_element_type=F32)
        + b_down.astype(F32)
    )
    result, unit_two, inverse_two = norm_forward(
        residual_two, ln2_gain.astype(F32), ln2_bias.astype(F32)
    )
    output = spread_rows(result.astype(BF))
    grad_result = own_cotangent.astype(F32)
    grad_two, grad_ln2_gain, grad_ln2_bias = norm_backward(
        grad_result, unit_two, inverse_two, ln2_gain.astype(F32)
    )
    grad_b_down = jnp.sum(grad_two, axis=0)
    grad_two_low = grad_two.astype(BF)
    act_own, act_oth = halves(activated_low, 1)
    down_away = lax.dot_general(act_oth, grad_two_low, TN, preferred_element_type=F32).astype(BF)
    down_got = plan.sibling(down_away)
    grad_activated = lax.dot_general(grad_two_low, w_down, NT, preferred_element_type=F32)
    grad_hidden = gelu_pull(grad_activated)[0]
    grad_b_up = jnp.sum(grad_hidden, axis=0)
    grad_hidden_low = grad_hidden.astype(BF)
    grad_normed = grad_two + lax.dot_general(
        grad_hidden_low, w_up, NT, preferred_element_type=F32
    )
    nl_own, nl_oth = halves(normed_low, 1)
    up_away = lax.dot_general(nl_oth, grad_hidden_low, TN, preferred_element_type=F32).astype(BF)
    up_got = plan.sibling(up_away)
    grad_one, grad_ln1_gain, grad_ln1_bias = norm_backward(
        grad_normed, unit_one, inverse_one, ln1_gain.astype(F32)
    )
    grad_b_out = jnp.sum(grad_one, axis=0)
    grad_one_low = grad_one.astype(BF)
    grad_one_full = whole(grad_one_low, plan.sibling(grad_one_low))
    down_sum = (
        lax.dot_general(act_own, grad_two_low, TN, preferred_element_type=F32)
        + down_got.astype(F32)
    ).astype(BF)
    sum_w_down = scatter_sum(plan, blocks(down_sum), "xy", where)
    up_sum = (
        lax.dot_general(nl_own, grad_hidden_low, TN, preferred_element_type=F32)
        + up_got.astype(F32)
    ).astype(BF)
    sum_w_up = scatter_sum(plan, blocks(up_sum), "yx", where)
    out_sum = lax.dot_general(context, grad_one_full, TN, preferred_element_type=F32).astype(BF)
    sum_w_out = scatter_sum(plan, blocks(out_sum), "xy", where)
    grad_context = lax.dot_general(
        grad_one_full, w_out_own, NT, preferred_element_type=F32
    ).astype(BF)
    grads = attn_bwd(seg13, query_rows, qkv, context, context_rest, grad_context)
    grad_qkv = jnp.concatenate(grads, axis=1)
    both = grad_qkv.reshape(2, rows, 3 * half)
    qkv_mine = pick(both, c, 0)
    qkv_got = plan.sibling(pick(both, 1 - c, 0))
    grad_start = (
        grad_one
        + lax.dot_general(qkv_mine, w_own, NT, preferred_element_type=F32)
        + lax.dot_general(qkv_got, w_oth, NT, preferred_element_type=F32)
    )
    grad_inputs = spread_rows(grad_start.astype(BF))
    sf_own, sf_oth = halves(start_full, 1)
    qkv_away = lax.dot_general(sf_oth, grad_qkv, TN, preferred_element_type=F32).astype(BF)
    qkv_keep = lax.dot_general(sf_own, grad_qkv, TN, preferred_element_type=F32).astype(BF)
    qkv_cross = plan.sibling(qkv_away)
    sum_own = scatter_sum(plan, blocks(qkv_keep), "xy", where)
    sum_oth = scatter_sum(plan, blocks(qkv_cross), "yx", where)
    quads = plan.ny * plan.nx
    pair = jnp.where(c == 0, jnp.stack([sum_own, sum_oth]), jnp.stack([sum_oth, sum_own]))
    sum_w_qkv = (
        pair.reshape(2, -1, 3, quads, half // quads).transpose(1, 2, 3, 0, 4).reshape(-1, 3 * model)
    )
    grad_b_own = jnp.sum(grad_qkv.astype(F32), axis=0)
    grad_b_time = jnp.sum(grad_start, axis=0)
    grad_w_time = fraction * grad_b_time
    zero = jnp.zeros((quads, 2, half // quads), F32)

    def placed(v):
        return lax.dynamic_update_index_in_dim(zero, v.reshape(quads, half // quads), c, 1).reshape(-1)

    vectors = [
        placed(grad_b_own[:half]),
        placed(grad_b_own[2 * half :]),
        grad_b_out,
        grad_ln1_gain,
        grad_ln1_bias,
        grad_b_down,
        grad_ln2_gain,
        grad_ln2_bias,
        grad_w_time,
        grad_b_time,
    ]
    small = jnp.concatenate([v[:, None] for v in vectors] + [grad_b_up.reshape(model, -1)], axis=1)
    small_own, small_oth = halves(small, 0)
    small_own = small_own + plan.sibling(small_oth)
    small_sum = scatter_sum(plan, blocks(small_own), "xy", where)
    v = [small_sum[:, i] for i in range(10)]
    return (
        output,
        grad_inputs,
        sum_w_qkv,
        v[0],
        v[1],
        sum_w_out,
        v[2],
        v[3],
        v[4],
        sum_w_up,
        small_sum[:, 10:].reshape(-1),
        sum_w_down,
        v[5],
        v[6],
        v[7],
        v[8],
        v[9],
    )


def solution(mesh):
    placed = (
        P("batch", "seq", None),
        P("batch"),
        P("batch", None),
        P("batch", "seq", None),
        P(),
        P(),
        P(),
        P(),
        P(),
        P(),
        P(),
        P(),
        P(),
        P(),
        P(),
        P(),
        P(),
        P(),
        P(),
    )
    sizes = dict(mesh.shape)
    body = per_device
    if sizes["seq"] == 4 and sizes["batch"] % 2 == 0:
        body = functools.partial(per_chip, Plan(mesh))
    return jax.shard_map(
        body,
        mesh=mesh,
        in_specs=placed,
        out_specs=(
            P("batch", "seq", None),
            P("batch", "seq", None),
            P(("batch", "seq"), None),
            P(("batch", "seq")),
            P(("batch", "seq")),
            P(("batch", "seq"), None),
            P(("batch", "seq")),
            P(("batch", "seq")),
            P(("batch", "seq")),
            P(("batch", "seq"), None),
            P(("batch", "seq")),
            P(("batch", "seq"), None),
            P(("batch", "seq")),
            P(("batch", "seq")),
            P(("batch", "seq")),
            P(("batch", "seq")),
            P(("batch", "seq")),
        ),
        check_vma=False,
    )
```

```python
import functools

import jax
import jax.numpy as jnp
from jax import lax
from jax.experimental import pallas as pl
from jax.experimental.pallas import tpu as pltpu
from jax.sharding import PartitionSpec as P

D = 1024
HEADS = 16
TSTEPS = 5000
AXES = ("batch", "seq")


BF=jnp.bfloat16; F32=jnp.float32
NT=(((1,),(1,)),((),())); NN=(((1,),(0,)),((),())); TN=(((0,),(0,)),((),()))
def dot(a,b,d): return lax.dot_general(a,b,d,preferred_element_type=F32)
FILLED=1664; PAD=64
def lanes(rows):
    return lax.broadcasted_iota(jnp.int32,(rows,128),1)
def parts3(x):
    a=x.astype(BF).astype(F32); r=x-a; b=r.astype(BF).astype(F32); c=r-b
    return a,b,c
def augment(base,h,x,lane):
    a,b,c=parts3(x)
    o=(1-h)*64
    f=base.astype(F32)
    f=jnp.where((lane>=o)&(lane<o+64),jnp.where(lane==o,a,jnp.where(lane==o+1,b,jnp.where(lane==o+2,c,0.0))),f)
    return f.astype(BF)
def ones3(base,h,lane,n=3):
    o=(1-h)*64
    f=base.astype(F32)
    f=jnp.where((lane>=o)&(lane<o+64),jnp.where(lane<o+n,1.0,0.0),f)
    return f.astype(BF)
def fwd_tile(q,k,vs,lane,keep):
    outs=[];augs=[]
    for h in (0,1):
        qh=jnp.where((lane//64)==h,q.astype(F32),0.0).astype(BF)
        s=dot(qh,k,NT)
        if keep is not None: s=jnp.where(keep,s,-1e30)
        m=jnp.max(s,axis=1,keepdims=True)
        p=jnp.exp2(s-m).astype(BF)
        o=dot(p,vs[h],NN)
        l=o[:,(1-h)*64:(1-h)*64+1]
        outs.append(o/l)
        augs.append(augment(q,h,-(m+jnp.log2(l)),lane))
    return jnp.where(lane<64,outs[0],outs[1]),augs
def fwd_store(refs,rows,o,augs):
    o_ref,ol_ref,qa_ref=refs
    o_ref[rows,:]=o.astype(BF)
    ol_ref[rows,:]=(o-o.astype(BF).astype(F32)).astype(BF)
    for h in (0,1): qa_ref[h,rows,:]=augs[h]
def fwd_kernel(bq,info,q_ref,k_ref,v_ref,*refs):
    single=info[0]==1
    @pl.when(single)
    def _():
        k=k_ref[0:FILLED,:]; v=v_ref[0:FILLED,:]
        vs=[ones3(v,h,lanes(FILLED),1) for h in (0,1)]
        for r in range(0,FILLED,bq):
            n=min(bq,FILLED-r)
            o,augs=fwd_tile(q_ref[r:r+n,:],k,vs,lanes(n),None)
            fwd_store(refs,slice(r,r+n),o,augs)
    @pl.when(jnp.logical_not(single))
    def _():
        col=lax.broadcasted_iota(jnp.int32,(128,512),1)
        lw=lanes(512); lq=lanes(128)
        for i in range(13):
            lo=info[1+i]; hi=info[14+i]
            at=jnp.minimum(lo,9)
            window=pl.ds(pl.multiple_of(at*128,128),512)
            k=k_ref[window,:]; v=v_ref[window,:]
            vs=[ones3(v,h,lw,1) for h in (0,1)]
            keep=(col>=(lo-at)*128)&(col<(hi-at)*128)
            rows=slice(i*128,i*128+128)
            o,augs=fwd_tile(q_ref[rows,:],k,vs,lq,keep)
            fwd_store(refs,rows,o,augs)
    rows=slice(FILLED,FILLED+PAD)
    lp=lanes(PAD)
    v=v_ref[rows,:]
    o,augs=fwd_tile(q_ref[rows,:],k_ref[rows,:],[ones3(v,h,lp,1) for h in (0,1)],lp,None)
    fwd_store(refs,rows,o,augs)
def attn_fwd(info,qkv,first,count,bq=832):
    L,W3=qkv.shape; n=W3//384
    spec=lambda j: pl.BlockSpec((L,128),lambda p,s,j=j:(0,p+first+j*n))
    one=pl.BlockSpec((L,128),lambda p,s:(0,p))
    return pl.pallas_call(functools.partial(fwd_kernel,bq),
        out_shape=(jax.ShapeDtypeStruct((L,count*128),BF),)*2+(jax.ShapeDtypeStruct((2*count,L,128),BF),),
        grid_spec=pltpu.PrefetchScalarGridSpec(num_scalar_prefetch=1,grid=(count,),
            in_specs=[spec(0),spec(1),spec(2)],
            out_specs=(one,one,pl.BlockSpec((2,L,128),lambda p,s:(p,0,0)))),
        compiler_params=pltpu.CompilerParams(vmem_limit_bytes=50<<20),name="attn_forward",
        cost_estimate=pl.CostEstimate(flops=8*count*L*L*256,bytes_accessed=10*L*count*128,transcendentals=2*count*L*L))(info,qkv,qkv,qkv)
def deltas(g,o,ol,lane):
    prod=g.astype(F32)*(o.astype(F32)+ol.astype(F32))
    return [augment(g,h,-jnp.sum(jnp.where((lane//64)==h,prod,0.0),axis=1,keepdims=True),lane) for h in (0,1)]
def bwd_tile(qa,k,v,ga,h,lane,keep):
    kh=ones3(k,h,lane); vh=ones3(v,h,lane)
    p=jnp.exp2(dot(kh,qa,NT))
    d=dot(vh,ga,NT)
    if keep is not None: p=jnp.where(keep,p,0.0)
    ds=(p*d).astype(BF)
    return dot(ds,kh,TN),dot(ds,qa,NN),dot(p.astype(BF),ga,NN)
LN2=0.6931471805599453
def both(a,lane): return jnp.where(lane<64,a[0],a[1])
def bwd_kernel(bk,info,qa_ref,k_ref,v_ref,o_ref,ol_ref,g_ref,dq_ref,dk_ref,dv_ref,sum_ref,acc,acc_k,acc_v):
    single=info[0]==1
    @pl.when(single)
    def _():
        lf=lanes(FILLED)
        gas=deltas(g_ref[0:FILLED,:],o_ref[0:FILLED,:],ol_ref[0:FILLED,:],lf)
        for r in range(0,FILLED,bk):
            n=min(bk,FILLED-r)
            rows=slice(r,r+n); lb=lanes(n)
            k=k_ref[rows,:]; v=v_ref[rows,:]
            dks=[];dvs=[]
            for h in (0,1):
                dq,dk,dv=bwd_tile(qa_ref[h,0:FILLED,:],k,v,gas[h],h,lb,None)
                if r==0: acc[h,0:FILLED,:]=dq
                else: acc[h,0:FILLED,:]+=dq
                dks.append(dk); dvs.append(dv)
            dk_ref[rows,:]=(both(dks,lb)*LN2).astype(BF)
            dv_ref[rows,:]=both(dvs,lb).astype(BF)
        dq_ref[0:FILLED,:]=(jnp.where(lf<64,acc[0,0:FILLED,:],acc[1,0:FILLED,:])*0.125).astype(BF)
    @pl.when(jnp.logical_not(single))
    def _():
        row=lax.broadcasted_iota(jnp.int32,(512,128),0)
        lw=lanes(512); lq=lanes(128)
        acc_k[...]=jnp.zeros_like(acc_k); acc_v[...]=jnp.zeros_like(acc_v)
        for i in range(13):
            lo=info[1+i]; hi=info[14+i]
            at=jnp.minimum(lo,9)
            window=pl.ds(pl.multiple_of(at*128,128),512)
            k=k_ref[window,:]; v=v_ref[window,:]
            keep=(row>=(lo-at)*128)&(row<(hi-at)*128)
            rows=slice(i*128,i*128+128)
            gas=deltas(g_ref[rows,:],o_ref[rows,:],ol_ref[rows,:],lq)
            dqs=[]
            for h in (0,1):
                dq,dk,dv=bwd_tile(qa_ref[h,rows,:],k,v,gas[h],h,lw,keep)
                dqs.append(dq)
                acc_k[h,window,:]+=dk
                acc_v[h,window,:]+=dv
            dq_ref[rows,:]=(both(dqs,lq)*0.125).astype(BF)
        lf=lanes(FILLED)
        dk_ref[0:FILLED,:]=(jnp.where(lf<64,acc_k[0],acc_k[1])*LN2).astype(BF)
        dv_ref[0:FILLED,:]=jnp.where(lf<64,acc_v[0],acc_v[1]).astype(BF)
    rows=slice(FILLED,FILLED+PAD)
    lp=lanes(PAD)
    gas=deltas(g_ref[rows,:],o_ref[rows,:],ol_ref[rows,:],lp)
    t=[bwd_tile(qa_ref[h,rows,:],k_ref[rows,:],v_ref[rows,:],gas[h],h,lp,None) for h in (0,1)]
    dq_ref[rows,:]=(both([a[0] for a in t],lp)*0.125).astype(BF)
    dk_ref[rows,:]=(both([a[1] for a in t],lp)*LN2).astype(BF)
    dv_ref[rows,:]=both([a[2] for a in t],lp).astype(BF)
    sum_ref[0:1,:]=jnp.sum(dq_ref[...].astype(F32),axis=0,keepdims=True)
    sum_ref[1:2,:]=jnp.sum(dv_ref[...].astype(F32),axis=0,keepdims=True)
def attn_bwd(info,qa,qkv,o,ol,g,first,count,inner,bk=832):
    L,W3=qkv.shape; n=W3//384
    spec=lambda j: pl.BlockSpec((L,128),lambda p,s,j=j:(0,p+first+j*n))
    one=pl.BlockSpec((L,128),lambda p,s:(0,p))
    part=pl.BlockSpec((L,128),lambda p,s:(0,p+inner))
    every=pl.BlockSpec((L,128),lambda p,s:(0,p+first))
    return pl.pallas_call(functools.partial(bwd_kernel,bk),
        out_shape=(jax.ShapeDtypeStruct((L,count*128),BF),)*3+(jax.ShapeDtypeStruct((2,count*128),F32),),
        grid_spec=pltpu.PrefetchScalarGridSpec(num_scalar_prefetch=1,grid=(count,),
            in_specs=[pl.BlockSpec((2,L,128),lambda p,s:(p+inner,0,0)),spec(1),spec(2),part,part,every],
            out_specs=(one,one,one,pl.BlockSpec((2,128),lambda p,s:(0,p))),
            scratch_shapes=[pltpu.VMEM((2,FILLED,128),F32)]*3),
        compiler_params=pltpu.CompilerParams(vmem_limit_bytes=56<<20),name="attn_backward",
        cost_estimate=pl.CostEstimate(flops=20*count*L*L*256,bytes_accessed=16*L*count*128,transcendentals=2*count*L*L))(info,qa,qkv,qkv,o,ol,g)


def gelu_exact(values):
    return jax.nn.gelu(values, approximate=False)


def norm_forward(values, gain, shift):
    centered = values - jnp.mean(values, axis=-1, keepdims=True)
    inverse = lax.rsqrt(jnp.mean(centered * centered, axis=-1, keepdims=True) + 1e-05)
    unit_part = centered * inverse
    return (unit_part * gain + shift, unit_part, inverse)


def norm_backward(grad_out, unit_part, inverse, gain):
    scaled = grad_out * gain
    centered = scaled - jnp.mean(scaled, axis=-1, keepdims=True)
    grad_in = inverse * (
        centered - unit_part * jnp.mean(scaled * unit_part, axis=-1, keepdims=True)
    )
    return (grad_in, jnp.sum(grad_out * unit_part, axis=0), jnp.sum(grad_out, axis=0))


def attention_forward(query_all, key_all, value_all, segments, head_dim):
    length, local_width = (query_all.shape[1], query_all.shape[2])
    head_count = local_width // head_dim
    block_len = length // 3
    score_scale = head_dim ** (-0.5)

    def per_sequence(pieces):
        queries, key_rows, value_rows, seq_ids = pieces
        key_heads = key_rows.reshape(length, head_count, head_dim)
        value_heads = value_rows.reshape(length, head_count, head_dim)

        def per_block(block_pieces):
            query_part, id_part = block_pieces
            query_heads = query_part.reshape(block_len, head_count, head_dim)
            scores = (
                jnp.einsum(
                    "qhd,khd->hqk", query_heads, key_heads, preferred_element_type=jnp.float32
                )
                * score_scale
            )
            masked = jnp.where(id_part[None, :, None] == seq_ids[None, None, :], scores, -1e30)
            maxima = jnp.max(masked, axis=-1, keepdims=True)
            exp_scores = jnp.exp(masked - maxima)
            totals = jnp.sum(exp_scores, axis=-1, keepdims=True)
            weights_low = (exp_scores / totals).astype(jnp.bfloat16)
            context = jnp.einsum(
                "hqk,khd->qhd", weights_low, value_heads, preferred_element_type=jnp.float32
            )
            return (
                context.astype(jnp.bfloat16).reshape(block_len, local_width),
                (maxima + jnp.log(totals))[..., 0],
            )

        contexts, logsums = lax.map(
            per_block, (queries.reshape(3, block_len, local_width), seq_ids.reshape(3, block_len))
        )
        return (contexts.reshape(length, local_width), logsums)

    return lax.map(per_sequence, (query_all, key_all, value_all, segments))


def attention_backward(query_all, key_all, value_all, segments, logsums, grad_all, head_dim):
    length, local_width = (query_all.shape[1], query_all.shape[2])
    head_count = local_width // head_dim
    block_len = length // 3
    score_scale = head_dim ** (-0.5)

    def per_sequence(pieces):
        queries, key_rows, value_rows, seq_ids, sum_rows, grad_rows = pieces
        key_heads = key_rows.reshape(length, head_count, head_dim)
        value_heads = value_rows.reshape(length, head_count, head_dim)

        def per_block(carry, block_pieces):
            key_total, value_total = carry
            query_part, id_part, sum_part, grad_part = block_pieces
            query_heads = query_part.reshape(block_len, head_count, head_dim)
            grad_heads = grad_part.reshape(block_len, head_count, head_dim)
            scores = (
                jnp.einsum(
                    "qhd,khd->hqk", query_heads, key_heads, preferred_element_type=jnp.float32
                )
                * score_scale
            )
            allowed = id_part[None, :, None] == seq_ids[None, None, :]
            prob_weights = jnp.where(allowed, jnp.exp(scores - sum_part[:, :, None]), 0.0)
            grad_probs = jnp.einsum(
                "qhd,khd->hqk", grad_heads, value_heads, preferred_element_type=jnp.float32
            )
            delta = jnp.sum(prob_weights * grad_probs, axis=-1, keepdims=True)
            grad_scores = (prob_weights * (grad_probs - delta)).astype(jnp.bfloat16)
            query_grad = (
                jnp.einsum(
                    "hqk,khd->qhd", grad_scores, key_heads, preferred_element_type=jnp.float32
                )
                * score_scale
            )
            key_total = (
                key_total
                + jnp.einsum(
                    "hqk,qhd->khd", grad_scores, query_heads, preferred_element_type=jnp.float32
                )
                * score_scale
            )
            value_total = value_total + jnp.einsum(
                "hqk,qhd->khd",
                prob_weights.astype(jnp.bfloat16),
                grad_heads,
                preferred_element_type=jnp.float32,
            )
            return (
                (key_total, value_total),
                query_grad.astype(jnp.bfloat16).reshape(block_len, local_width),
            )

        zero_heads = jnp.zeros((length, head_count, head_dim), jnp.float32)
        (key_total, value_total), query_grads = lax.scan(
            per_block,
            (zero_heads, zero_heads),
            (
                queries.reshape(3, block_len, local_width),
                seq_ids.reshape(3, block_len),
                sum_rows,
                grad_rows.reshape(3, block_len, local_width),
            ),
        )
        return (
            query_grads.reshape(length, local_width),
            key_total.astype(jnp.bfloat16).reshape(length, local_width),
            value_total.astype(jnp.bfloat16).reshape(length, local_width),
        )

    return lax.map(per_sequence, (query_all, key_all, value_all, segments, logsums, grad_all))


def per_device(
    inputs,
    timesteps,
    segments,
    cotangent,
    w_qkv,
    b_query,
    b_value,
    w_out,
    b_out,
    ln1_gain,
    ln1_bias,
    w_up,
    b_up,
    w_down,
    b_down,
    ln2_gain,
    ln2_bias,
    w_time,
    b_time,
):
    groups, local_len, model_width = inputs.shape
    row_count = groups * local_len
    head_dim = D // HEADS
    fraction = timesteps.astype(jnp.float32) / TSTEPS
    start_sum = (
        inputs.astype(jnp.float32)
        + fraction[:, None, None] * w_time.astype(jnp.float32)
        + b_time.astype(jnp.float32)
    )
    start_low = start_sum.astype(jnp.bfloat16)
    projected = jnp.einsum("bld,de->ble", start_low, w_qkv, preferred_element_type=jnp.float32)
    query_low = (projected[..., :model_width] + b_query.astype(jnp.float32)).astype(jnp.bfloat16)
    key_low = projected[..., model_width : 2 * model_width].astype(jnp.bfloat16)
    value_low = (projected[..., 2 * model_width :] + b_value.astype(jnp.float32)).astype(
        jnp.bfloat16
    )
    query_all, key_all, value_all = (
        lax.all_to_all(query_low, "seq", split_axis=2, concat_axis=1, tiled=True),
        lax.all_to_all(key_low, "seq", split_axis=2, concat_axis=1, tiled=True),
        lax.all_to_all(value_low, "seq", split_axis=2, concat_axis=1, tiled=True),
    )
    context_heads, logsums = attention_forward(query_all, key_all, value_all, segments, head_dim)
    context = lax.all_to_all(context_heads, "seq", split_axis=1, concat_axis=2, tiled=True)
    context_rows = context.reshape(row_count, model_width)
    start_rows = start_sum.reshape(row_count, model_width)
    residual_one = (
        start_rows
        + jnp.dot(context_rows, w_out, preferred_element_type=jnp.float32)
        + b_out.astype(jnp.float32)
    )
    normed, unit_one, inverse_one = norm_forward(
        residual_one, ln1_gain.astype(jnp.float32), ln1_bias.astype(jnp.float32)
    )
    normed_low = normed.astype(jnp.bfloat16)
    hidden_pre = jnp.dot(normed_low, w_up, preferred_element_type=jnp.float32) + b_up.astype(
        jnp.float32
    )
    activated, gelu_pull = jax.vjp(gelu_exact, hidden_pre)
    activated_low = activated.astype(jnp.bfloat16)
    residual_two = (
        normed
        + jnp.dot(activated_low, w_down, preferred_element_type=jnp.float32)
        + b_down.astype(jnp.float32)
    )
    result, unit_two, inverse_two = norm_forward(
        residual_two, ln2_gain.astype(jnp.float32), ln2_bias.astype(jnp.float32)
    )
    output = result.astype(jnp.bfloat16).reshape(groups, local_len, model_width)
    grad_result = cotangent.reshape(row_count, model_width).astype(jnp.float32)
    grad_two, grad_ln2_gain, grad_ln2_bias = norm_backward(
        grad_result, unit_two, inverse_two, ln2_gain.astype(jnp.float32)
    )
    grad_b_down = jnp.sum(grad_two, axis=0)
    grad_two_low = grad_two.astype(jnp.bfloat16)
    grad_w_down = jnp.einsum(
        "rf,rd->fd", activated_low, grad_two_low, preferred_element_type=jnp.float32
    )
    grad_activated = jnp.einsum(
        "rd,fd->rf", grad_two_low, w_down, preferred_element_type=jnp.float32
    )
    grad_hidden = gelu_pull(grad_activated)[0]
    grad_b_up = jnp.sum(grad_hidden, axis=0)
    grad_hidden_low = grad_hidden.astype(jnp.bfloat16)
    grad_w_up = jnp.einsum(
        "rd,rf->df", normed_low, grad_hidden_low, preferred_element_type=jnp.float32
    )
    grad_normed = grad_two + jnp.einsum(
        "rf,df->rd", grad_hidden_low, w_up, preferred_element_type=jnp.float32
    )
    grad_one, grad_ln1_gain, grad_ln1_bias = norm_backward(
        grad_normed, unit_one, inverse_one, ln1_gain.astype(jnp.float32)
    )
    grad_b_out = jnp.sum(grad_one, axis=0)
    grad_one_low = grad_one.astype(jnp.bfloat16)
    grad_w_out = jnp.einsum(
        "rd,re->de", context_rows, grad_one_low, preferred_element_type=jnp.float32
    )
    grad_context = (
        jnp.einsum("re,de->rd", grad_one_low, w_out, preferred_element_type=jnp.float32)
        .astype(jnp.bfloat16)
        .reshape(groups, local_len, model_width)
    )
    grad_context_heads = lax.all_to_all(
        grad_context, "seq", split_axis=2, concat_axis=1, tiled=True
    )
    query_grads, key_grads, value_grads = attention_backward(
        query_all, key_all, value_all, segments, logsums, grad_context_heads, head_dim
    )
    grad_query, grad_key, grad_value = (
        lax.all_to_all(query_grads, "seq", split_axis=1, concat_axis=2, tiled=True),
        lax.all_to_all(key_grads, "seq", split_axis=1, concat_axis=2, tiled=True),
        lax.all_to_all(value_grads, "seq", split_axis=1, concat_axis=2, tiled=True),
    )
    grad_projected = jnp.concatenate((grad_query, grad_key, grad_value), axis=2).reshape(
        row_count, 3 * model_width
    )
    grad_w_qkv = jnp.einsum(
        "rd,re->de",
        start_low.reshape(row_count, model_width),
        grad_projected,
        preferred_element_type=jnp.float32,
    )
    grad_b_query = jnp.sum(grad_query.astype(jnp.float32), axis=(0, 1))
    grad_b_value = jnp.sum(grad_value.astype(jnp.float32), axis=(0, 1))
    grad_start = grad_one + jnp.einsum(
        "re,de->rd", grad_projected, w_qkv, preferred_element_type=jnp.float32
    )
    grad_inputs = grad_start.astype(jnp.bfloat16).reshape(groups, local_len, model_width)
    per_sequence_grad = jnp.sum(grad_start.reshape(groups, local_len, model_width), axis=1)
    grad_w_time = jnp.einsum("g,gd->d", fraction, per_sequence_grad)
    grad_b_time = jnp.sum(per_sequence_grad, axis=0)
    (
        sum_w_qkv,
        sum_b_query,
        sum_b_value,
        sum_w_out,
        sum_b_out,
        sum_ln1_gain,
        sum_ln1_bias,
        sum_w_up,
        sum_b_up,
        sum_w_down,
        sum_b_down,
        sum_ln2_gain,
        sum_ln2_bias,
        sum_w_time,
        sum_b_time,
    ) = (
        lax.psum_scatter(grad_w_qkv, ("batch", "seq"), scatter_dimension=0, tiled=True),
        lax.psum_scatter(grad_b_query, ("batch", "seq"), scatter_dimension=0, tiled=True),
        lax.psum_scatter(grad_b_value, ("batch", "seq"), scatter_dimension=0, tiled=True),
        lax.psum_scatter(grad_w_out, ("batch", "seq"), scatter_dimension=0, tiled=True),
        lax.psum_scatter(grad_b_out, ("batch", "seq"), scatter_dimension=0, tiled=True),
        lax.psum_scatter(grad_ln1_gain, ("batch", "seq"), scatter_dimension=0, tiled=True),
        lax.psum_scatter(grad_ln1_bias, ("batch", "seq"), scatter_dimension=0, tiled=True),
        lax.psum_scatter(grad_w_up, ("batch", "seq"), scatter_dimension=0, tiled=True),
        lax.psum_scatter(grad_b_up, ("batch", "seq"), scatter_dimension=0, tiled=True),
        lax.psum_scatter(grad_w_down, ("batch", "seq"), scatter_dimension=0, tiled=True),
        lax.psum_scatter(grad_b_down, ("batch", "seq"), scatter_dimension=0, tiled=True),
        lax.psum_scatter(grad_ln2_gain, ("batch", "seq"), scatter_dimension=0, tiled=True),
        lax.psum_scatter(grad_ln2_bias, ("batch", "seq"), scatter_dimension=0, tiled=True),
        lax.psum_scatter(grad_w_time, ("batch", "seq"), scatter_dimension=0, tiled=True),
        lax.psum_scatter(grad_b_time, ("batch", "seq"), scatter_dimension=0, tiled=True),
    )
    return (
        output,
        grad_inputs,
        sum_w_qkv,
        sum_b_query,
        sum_b_value,
        sum_w_out,
        sum_b_out,
        sum_ln1_gain,
        sum_ln1_bias,
        sum_w_up,
        sum_b_up,
        sum_w_down,
        sum_b_down,
        sum_ln2_gain,
        sum_ln2_bias,
        sum_w_time,
        sum_b_time,
    )


GROUPS = 2
SLOPE = F32
LOG2E = 1.4426950408889634


def layer_norm(values):
    centered = values - jnp.mean(values, axis=1, keepdims=True)
    inverse = lax.rsqrt(jnp.mean(centered * centered, axis=1, keepdims=True) + 1e-05)
    return centered * inverse, inverse


def layer_norm_back(scaled, unit_part, inverse):
    return inverse * (
        scaled
        - jnp.mean(scaled, axis=1, keepdims=True)
        - unit_part * jnp.mean(scaled * unit_part, axis=1, keepdims=True)
    )


def gelu_pair(v):
    bell = jnp.exp2(v * v * (-0.5 * LOG2E))
    base = 1.0 + 0.2316418882663604 * jnp.abs(v)
    t = pltpu.reciprocal(base, approx=True)
    t = t * (2.0 - base * t)
    tail = t * (
        0.127414796
        + t * (-0.142248368 + t * (0.7107068705 + t * (-0.7265760135 + t * 0.5307027145)))
    )
    tail = tail * bell
    cover = jnp.where(v >= 0, 1.0 - tail, tail)
    return v * cover, cover + v * bell * 0.3989422804014327


def middle_kernel(
    fc,
    sel_ref,
    frac_ref,
    inp_ref,
    ctx_a_ref,
    ctx_b_ref,
    cot_ref,
    vec_ref,
    b_up_ref,
    wo_a_ref,
    wo_b_ref,
    w_up_hbm,
    w_down_hbm,
    out_ref,
    norm_ref,
    act_ref,
    two_ref,
    hid_ref,
    one_ref,
    onel_ref,
    small_ref,
    smallup_ref,
    w_up,
    w_down,
    slope,
    sems,
):
    step = pl.program_id(0)
    up_copy = pltpu.make_async_copy(w_up_hbm, w_up, sems.at[0])
    down_copy = pltpu.make_async_copy(w_down_hbm, w_down, sems.at[1])

    @pl.when(step == 0)
    def _():
        up_copy.start()
        down_copy.start()
        small_ref[...] = jnp.zeros_like(small_ref)
        smallup_ref[...] = jnp.zeros_like(smallup_ref)

    vec = lambda i: vec_ref[i : i + 1, :]
    start = inp_ref[...].astype(F32) + (frac_ref[0] * vec(0) + vec(1))
    residual = (
        start
        + dot(ctx_a_ref[...], wo_a_ref[...].reshape(-1, wo_a_ref.shape[-1]), NN)
        + dot(ctx_b_ref[...], wo_b_ref[...].reshape(-1, wo_b_ref.shape[-1]), NN)
        + vec(2)
    )
    unit_one, inverse_one = layer_norm(residual)
    normed = unit_one * vec(3) + vec(4)
    low = normed.astype(BF)
    norm_ref[...] = low

    @pl.when(step == 0)
    def _():
        up_copy.wait()
        down_copy.wait()

    width = w_up.shape[1]
    total = normed + vec(5)
    for f in range(0, width, fc):
        cols = slice(f, f + fc)
        v = dot(low, w_up[:, cols], NN) + b_up_ref[:, cols]
        a, g = gelu_pair(v)
        a = a.astype(BF)
        act_ref[:, cols] = a
        slope[:, cols] = g.astype(slope.dtype)
        total = total + dot(a, w_down[cols, :], NN)
    unit_two, inverse_two = layer_norm(total)
    out_ref[...] = (unit_two * vec(6) + vec(7)).astype(BF)
    cot = cot_ref[...].astype(F32)
    two = layer_norm_back(cot * vec(6), unit_two, inverse_two)
    add = lambda v: jnp.sum(v, axis=0, keepdims=True)
    small_ref[3:4, :] += add(two)
    small_ref[4:5, :] += add(cot * unit_two)
    small_ref[5:6, :] += add(cot)
    two_low = two.astype(BF)
    two_ref[...] = two_low
    total = two
    for f in range(0, width, fc):
        cols = slice(f, f + fc)
        d = dot(two_low, w_down[cols, :], NT) * slope[:, cols].astype(F32)
        smallup_ref[:, cols] += add(d)
        d = d.astype(BF)
        hid_ref[:, cols] = d
        total = total + dot(d, w_up[:, cols], NT)
    small_ref[1:2, :] += add(total * unit_one)
    small_ref[2:3, :] += add(total)
    one = layer_norm_back(total * vec(3), unit_one, inverse_one)
    small_ref[0:1, :] += add(one)
    one_ref[...] = one
    onel_ref[...] = one.astype(BF)


def middle(core, fraction, inp, ctx_a, ctx_b, cot, vecs, b_up, w_out, w_up, w_down, br=288, fc=2048):
    rows, model = inp.shape
    width = w_up.shape[1]
    half = model // 2
    quads = w_out.shape[0]
    row = lambda w: pl.BlockSpec((br, w), lambda i, s: (i, 0))
    fixed = lambda shape: pl.BlockSpec(shape, lambda i, s: (0,) * len(shape))
    wo = lambda flip: pl.BlockSpec(
        (quads, 1, model // quads // 2, model),
        (lambda i, s: (0, s[0], 0, 0)) if not flip else (lambda i, s: (0, 1 - s[0], 0, 0)),
    )
    out = lambda w, t: jax.ShapeDtypeStruct((rows, w), t)
    return pl.pallas_call(
        functools.partial(middle_kernel, fc),
        out_shape=(
            out(model, BF),
            out(model, BF),
            out(width, BF),
            out(model, BF),
            out(width, BF),
            out(model, F32),
            out(model, BF),
            jax.ShapeDtypeStruct((8, model), F32),
            jax.ShapeDtypeStruct((1, width), F32),
        ),
        grid_spec=pltpu.PrefetchScalarGridSpec(
            num_scalar_prefetch=1,
            grid=(rows // br,),
            in_specs=[
                pl.BlockSpec(memory_space=pltpu.SMEM),
                row(model),
                row(half),
                row(half),
                row(model),
                fixed((8, model)),
                fixed((1, width)),
                wo(False),
                wo(True),
                pl.BlockSpec(memory_space=pl.ANY),
                pl.BlockSpec(memory_space=pl.ANY),
            ],
            out_specs=(
                row(model),
                row(model),
                row(width),
                row(model),
                row(width),
                row(model),
                row(model),
                fixed((8, model)),
                fixed((1, width)),
            ),
            scratch_shapes=[
                pltpu.VMEM(w_up.shape, BF),
                pltpu.VMEM(w_down.shape, BF),
                pltpu.VMEM((br, width), SLOPE),
                pltpu.SemaphoreType.DMA((2,)),
            ],
        ),
        compiler_params=pltpu.CompilerParams(vmem_limit_bytes=60 << 20),
        cost_estimate=pl.CostEstimate(
            flops=4 * rows * model * (model // 2 + 2 * width),
            bytes_accessed=4 * model * width + rows * (16 * model + 4 * width),
            transcendentals=rows * width * 2,
        ),
        name="middle",
    )(core, fraction, inp, ctx_a, ctx_b, cot, vecs, b_up, w_out, w_out, w_up, w_down)


def grad_kernel(count, extra, *refs):
    lhs = [r[...] for r in refs[1 : 1 + count]]
    rhs_ref = refs[1 + count]
    out_ref = refs[-1]
    left = lhs[0] if count == 1 else jnp.concatenate(lhs, axis=1)
    total = dot(left, rhs_ref[...], TN)
    if extra:
        total = total + refs[2 + count][...].astype(F32)
    out_ref[...] = total.astype(BF)


def weight_grad(sel, lhs, rhs, add=None, cols=1024, quads=4, pairs=2):
    depth, width = lhs.shape
    n = rhs.shape[1]
    w = width // (quads * pairs)
    extra = add is not None
    if w >= 512:
        grid, count = (quads,), 1
        ins = [
            pl.BlockSpec((depth, w), lambda i, s: (0, pairs * i + s[0])),
            pl.BlockSpec((depth, n), lambda i, s: (0, 0)),
        ]
        out = pl.BlockSpec((w, n), lambda i, s: (i, 0))
        args = [lhs, rhs]
    else:
        grid, count = (n // cols,), quads
        ins = [
            pl.BlockSpec((depth, w), lambda i, s, q=q: (0, pairs * q + s[0])) for q in range(quads)
        ] + [pl.BlockSpec((depth, cols), lambda i, s: (0, i))]
        out = pl.BlockSpec((quads * w, cols), lambda i, s: (0, i))
        args = [lhs] * quads + [rhs]
    if extra:
        ins.append(out)
        args.append(add)
    total = quads * w
    return pl.pallas_call(
        functools.partial(grad_kernel, count, extra),
        out_shape=jax.ShapeDtypeStruct((total, n), BF),
        grid_spec=pltpu.PrefetchScalarGridSpec(
            num_scalar_prefetch=1, grid=grid, in_specs=ins, out_specs=out
        ),
        compiler_params=pltpu.CompilerParams(vmem_limit_bytes=48 << 20),
        cost_estimate=pl.CostEstimate(
            flops=2 * depth * total * n,
            bytes_accessed=2 * depth * (total + n) + (4 if extra else 2) * total * n,
            transcendentals=0,
        ),
        name="weight_grad",
    )(sel, *args)


class Plan:
    def __init__(self, mesh):
        sizes = dict(mesh.shape)
        self.batch, self.depth = sizes["batch"], sizes["seq"]
        chips = self.batch // 2
        side = 1
        while side * side < chips:
            side *= 2
        self.nx, self.ny = side, chips // side

    def perm(self, target):
        pairs = []
        for y in range(self.ny):
            for x in range(self.nx):
                for c in range(2):
                    for z in range(self.depth):
                        to = target(y, x, c, z)
                        if to is not None:
                            pairs.append((self.index(y, x, c, z), self.index(*to)))
        return pairs

    def index(self, y, x, c, z):
        return ((y * self.nx + x) * 2 + c) * self.depth + z

    def send(self, value, target):
        return lax.ppermute(value, AXES, self.perm(target))

    def sibling(self, value):
        return self.send(value, lambda y, x, c, z: (y, x, 1 - c, z))


def pick(array, index, axis):
    return lax.dynamic_index_in_dim(array, index, axis, keepdims=False)


def scatter_sum(plan, terms, order, where):
    y, x, z = where
    for axis in order:
        if axis == "x":
            if plan.nx == 1:
                terms = terms[:, 0]
                continue
            at = terms.ndim - 4
            total = pick(terms, x, at).astype(F32)
            for r in range(1, plan.nx):
                got = plan.send(
                    pick(terms, (x + r) % plan.nx, at),
                    lambda y, x, c, z, r=r: (y, (x + r) % plan.nx, c, z),
                )
                total = total + got.astype(F32)
        else:
            total = pick(terms, y, 0).astype(F32)
            for r in range(1, plan.ny):
                got = plan.send(
                    pick(terms, (y + r) % plan.ny, 0),
                    lambda y, x, c, z, r=r: ((y + r) % plan.ny, x, c, z),
                )
                total = total + got.astype(F32)
        terms = total.astype(terms.dtype)
    total = pick(terms, z, 0).astype(F32)
    for r in range(1, plan.depth):
        got = plan.send(
            pick(terms, (z + r) % plan.depth, 0),
            lambda y, x, c, z, r=r: (y, x, c, (z + r) % plan.depth),
        )
        total = total + got.astype(F32)
    return total


def per_chip(
    plan,
    inputs,
    timesteps,
    segments,
    cotangent,
    w_qkv,
    b_query,
    b_value,
    w_out,
    b_out,
    ln1_gain,
    ln1_bias,
    w_up,
    b_up,
    w_down,
    b_down,
    ln2_gain,
    ln2_bias,
    w_time,
    b_time,
):
    local_len = inputs.shape[1]
    rows = 2 * local_len
    length = segments.shape[1]
    b = lax.axis_index("batch")
    z = lax.axis_index("seq")
    c, x, y = b % 2, (b // 2) % plan.nx, b // 2 // plan.nx
    part = z % 2
    where = (y, x, z)
    first = (segments[1, 0] == segments[1, 128 * 12]).astype(jnp.int32)
    which = lambda s: (first + s) % 2
    facts = jnp.concatenate(
        [segments[:, : 128 * 13 : 128], timesteps[:, None], jnp.zeros((2, 2), jnp.int32)], axis=1
    )
    facts = jnp.stack([pick(facts, which(0), 0), pick(facts, which(1), 0)])
    other_facts = plan.sibling(facts)
    facts = jnp.where(z // 2 == c, facts, other_facts)
    mine = pick(facts, z % 2, 0)
    marks = mine[:13]
    info = jnp.concatenate(
        [
            (marks[:1] == marks[12:]).astype(jnp.int32),
            jnp.sum((marks[None, :] < marks[:, None]).astype(jnp.int32), axis=1),
            jnp.sum((marks[None, :] <= marks[:, None]).astype(jnp.int32), axis=1),
        ]
    )
    fraction = mine[13].astype(F32) / TSTEPS

    def gather_rows(array):
        got = [
            plan.send(
                pick(array, which((part + j) % 2), 0),
                lambda y, x, c, z, j=j: (y, x, z // 2, 2 * c + (z + j) % 2),
            )
            for j in (0, 1)
        ]
        return jnp.concatenate(
            [jnp.where(part == 0, got[0], got[1]), jnp.where(part == 0, got[1], got[0])], axis=0
        )

    def spread_rows(array):
        array = array.reshape(2, local_len, array.shape[-1])
        got = [
            plan.send(
                pick(array, (part + j) % 2, 0),
                lambda y, x, c, z, j=j: (y, x, z // 2, 2 * c + (z + j) % 2),
            )
            for j in (0, 1)
        ]
        swap = (part + first) % 2
        return jnp.stack(
            [jnp.where(swap == 0, got[0], got[1]), jnp.where(swap == 0, got[1], got[0])], axis=0
        )

    def whole(own, other):
        return jnp.where(c == 0, jnp.concatenate([own, other]), jnp.concatenate([other, own]))

    def halves(array, axis):
        shape = array.shape
        cut = shape[:axis] + (plan.ny * plan.nx, 2, -1) + shape[axis + 1 :]
        flat = shape[:axis] + (-1,) + shape[axis + 1 :]
        split = array.reshape(cut)
        return (
            pick(split, c, axis + 1).reshape(flat),
            pick(split, 1 - c, axis + 1).reshape(flat),
        )

    def blocks(array):
        return array.reshape(plan.ny, plan.nx, plan.depth, -1, array.shape[-1])

    model = inputs.shape[-1]
    half = model // 2
    quads = plan.ny * plan.nx
    core = jnp.stack([c]).astype(jnp.int32)
    away = 1 - core
    w_four = w_qkv.reshape(model, 3, quads, 2, half // quads)
    w_own, w_oth = pick(w_four, c, 3), pick(w_four, 1 - c, 3)
    bias = jnp.concatenate(
        [
            halves(b_query.astype(F32), 0)[0],
            jnp.zeros((half,), F32),
            halves(b_value.astype(F32), 0)[0],
        ]
    )
    w_out_own = halves(w_out, 0)[0]
    w_all = w_own.reshape(model, 3 * half)
    groups = [range(g * (quads // GROUPS), (g + 1) * (quads // GROUPS)) for g in range(GROUPS)]
    cut = lambda w: [w[:, :, g.start : g.stop].reshape(model, -1) for g in groups]
    w_cut, w_cut_oth = cut(w_own), cut(w_oth)
    own_inputs = gather_rows(inputs)
    own_inputs, w_all, w_cut, w_cut_oth, w_out_own = lax.optimization_barrier(
        (own_inputs, w_all, w_cut, w_cut_oth, w_out_own)
    )
    start = (
        own_inputs.astype(F32) + fraction * w_time.astype(F32)[None] + b_time.astype(F32)[None]
    )
    start_low = start.astype(BF)
    start_sib = plan.sibling(start_low)
    cotangent, _ = lax.optimization_barrier((cotangent, start_low))
    own_cotangent = gather_rows(cotangent)
    start_full = whole(start_low, start_sib)
    scale = jnp.where(jnp.arange(3 * half) < half, 0.125 * LOG2E, 1.0)
    qkv = ((jnp.dot(start_full, w_all, preferred_element_type=F32) + bias) * scale).astype(BF)
    fwd = [attn_fwd(info, qkv, g.start, len(g)) for g in groups]
    mine_of, away_of = [], []
    for g in range(GROUPS):
        split = fwd[g][0].reshape(2, rows, -1)
        mine_of.append(pick(split, c, 0))
        away_of.append(plan.sibling(pick(split, 1 - c, 0)))
    vecs = jnp.stack(
        [v.astype(F32) for v in (w_time, b_time, b_out, ln1_gain, ln1_bias, b_down, ln2_gain, ln2_bias)]
    )
    result, normed_low, act, two_low, hid, grad_one, one_low, small_sums, up_sums = middle(
        core,
        fraction[None],
        own_inputs,
        jnp.concatenate(mine_of, axis=1),
        jnp.concatenate(away_of, axis=1),
        own_cotangent,
        vecs,
        b_up.astype(F32)[None],
        w_out.reshape(quads, 2, -1, model),
        w_up,
        w_down,
    )
    grad_one_full = whole(one_low, plan.sibling(one_low))
    down_got = plan.sibling(weight_grad(away, act, two_low, quads=quads))
    up_got = plan.sibling(weight_grad(away, normed_low, hid, quads=quads))
    output = spread_rows(result)
    grad_context = lax.dot_general(
        grad_one_full, w_out_own, NT, preferred_element_type=F32
    ).astype(BF)
    down_sum = weight_grad(core, act, two_low, down_got, quads=quads)
    up_sum = weight_grad(core, normed_low, hid, up_got, quads=quads)
    grad_context, down_sum, up_sum = lax.optimization_barrier((grad_context, down_sum, up_sum))
    sum_w_down = scatter_sum(plan, blocks(down_sum), "xy", where)
    sum_w_up = scatter_sum(plan, blocks(up_sum), "yx", where)
    context = jnp.concatenate([f[0] for f in fwd], axis=1)
    out_sum = weight_grad(0 * core, context, grad_one_full, quads=quads, pairs=1, cols=512)
    sum_w_out = scatter_sum(plan, blocks(out_sum), "yx", where)
    grad_start = grad_one
    keeps, crosses, b_sums = [], [], []
    for g in range(GROUPS):
        heads = groups[g]
        dq, dk, dv, b_sum = attn_bwd(
            info, fwd[g][2], qkv, fwd[g][0], fwd[g][1], grad_context, heads.start, len(heads), 0
        )
        b_sums.append(b_sum)
        grad_qkv = jnp.concatenate([dq, dk, dv], axis=1)
        both_halves = grad_qkv.reshape(2, rows, -1)
        got = plan.sibling(pick(both_halves, 1 - c, 0))
        cols = grad_qkv.shape[1]
        cross = plan.sibling(weight_grad(away, start_full, grad_qkv, quads=quads, cols=cols))
        keep = weight_grad(core, start_full, grad_qkv, quads=quads, cols=cols)
        keeps.append(scatter_sum(plan, blocks(keep), "xy", where))
        crosses.append(scatter_sum(plan, blocks(cross), "yx", where))
        grad_start = (
            grad_start
            + lax.dot_general(pick(both_halves, c, 0), w_cut[g], NT, preferred_element_type=F32)
            + lax.dot_general(got, w_cut_oth[g], NT, preferred_element_type=F32)
        )
        if g + 1 < GROUPS:
            grad_context, grad_qkv = lax.optimization_barrier((grad_context, grad_qkv))
    grad_inputs = spread_rows(grad_start.astype(BF))
    split3 = lambda parts: jnp.concatenate(
        [p.reshape(p.shape[0], 3, quads // GROUPS, -1) for p in parts], axis=2
    )
    sum_own, sum_oth = split3(keeps), split3(crosses)
    b_sum = jnp.concatenate(b_sums, axis=1)
    grad_b_query, grad_b_value = b_sum[0], b_sum[1]
    pair = jnp.where(c == 0, jnp.stack([sum_own, sum_oth]), jnp.stack([sum_oth, sum_own]))
    sum_w_qkv = (
        pair.transpose(1, 2, 3, 0, 4).reshape(-1, 3 * model)
    )
    grad_b_time = jnp.sum(grad_start, axis=0)
    grad_w_time = fraction * grad_b_time
    zero = jnp.zeros((quads, 2, half // quads), F32)

    def placed(v):
        return lax.dynamic_update_index_in_dim(zero, v.reshape(quads, half // quads), c, 1).reshape(-1)

    vectors = [
        placed(grad_b_query),
        placed(grad_b_value),
        small_sums[0],
        small_sums[1],
        small_sums[2],
        small_sums[3],
        small_sums[4],
        small_sums[5],
        grad_w_time,
        grad_b_time,
    ]
    small = jnp.concatenate([v[:, None] for v in vectors] + [up_sums.reshape(model, -1)], axis=1)
    small_own, small_oth = halves(small, 0)
    small_own = small_own + plan.sibling(small_oth)
    small_sum = scatter_sum(plan, blocks(small_own), "xy", where)
    v = [small_sum[:, i] for i in range(10)]
    return (
        output,
        grad_inputs,
        sum_w_qkv,
        v[0],
        v[1],
        sum_w_out,
        v[2],
        v[3],
        v[4],
        sum_w_up,
        small_sum[:, 10:].reshape(-1),
        sum_w_down,
        v[5],
        v[6],
        v[7],
        v[8],
        v[9],
    )


def solution(mesh):
    placed = (
        P("batch", "seq", None),
        P("batch"),
        P("batch", None),
        P("batch", "seq", None),
        P(),
        P(),
        P(),
        P(),
        P(),
        P(),
        P(),
        P(),
        P(),
        P(),
        P(),
        P(),
        P(),
        P(),
        P(),
    )
    sizes = dict(mesh.shape)
    body = per_device
    if sizes["seq"] == 4 and sizes["batch"] % 2 == 0:
        body = functools.partial(per_chip, Plan(mesh))
    return jax.shard_map(
        body,
        mesh=mesh,
        in_specs=placed,
        out_specs=(
            P("batch", "seq", None),
            P("batch", "seq", None),
            P(("batch", "seq"), None),
            P(("batch", "seq")),
            P(("batch", "seq")),
            P(("batch", "seq"), None),
            P(("batch", "seq")),
            P(("batch", "seq")),
            P(("batch", "seq")),
            P(("batch", "seq"), None),
            P(("batch", "seq")),
            P(("batch", "seq"), None),
            P(("batch", "seq")),
            P(("batch", "seq")),
            P(("batch", "seq")),
            P(("batch", "seq")),
            P(("batch", "seq")),
        ),
        check_vma=False,
    )
```

```python
import functools

import jax
import jax.numpy as jnp
from jax import lax
from jax.experimental import pallas as pl
from jax.experimental.pallas import tpu as pltpu
from jax.sharding import PartitionSpec as P

D = 1024
HEADS = 16
TSTEPS = 5000
AXES = ("batch", "seq")


BF=jnp.bfloat16; F32=jnp.float32
NT=(((1,),(1,)),((),())); NN=(((1,),(0,)),((),())); TN=(((0,),(0,)),((),()))
def dot(a,b,d): return lax.dot_general(a,b,d,preferred_element_type=F32)
PHASE=1
FILLED=1664; PAD=64
def lanes(rows):
    return lax.broadcasted_iota(jnp.int32,(rows,128),1)
def parts3(x):
    a=x.astype(BF).astype(F32); r=x-a; b=r.astype(BF).astype(F32); c=r-b
    return a,b,c
def augment(base,h,x,lane):
    a,b,c=parts3(x)
    o=(1-h)*64
    f=base.astype(F32)
    f=jnp.where((lane>=o)&(lane<o+64),jnp.where(lane==o,a,jnp.where(lane==o+1,b,jnp.where(lane==o+2,c,0.0))),f)
    return f.astype(BF)
def ones3(base,h,lane,n=3):
    o=(1-h)*64
    f=base.astype(F32)
    f=jnp.where((lane>=o)&(lane<o+64),jnp.where(lane<o+n,1.0,0.0),f)
    return f.astype(BF)
def spread(base,h,x,lane):
    a=x.astype(BF).astype(F32); r=x-a; b=r.astype(BF).astype(F32); c=r-b
    o=(1-h)*64
    f=jnp.where(lane==o,a,jnp.where(lane==o+1,b,jnp.where(lane==o+2,c,0.0)))
    return jnp.where((lane//64)==h,base.astype(F32),f).astype(BF)
def fwd_tiles(tasks,lane):
    scores=[]
    for q,k,vs,keep in tasks:
        for h in (0,1):
            qh=jnp.where((lane//64)==h,q.astype(F32),0.0).astype(BF)
            s=dot(qh,k,NT)
            scores.append(s if keep is None else jnp.where(keep,s,-1e30))
    tops=[];outs=[]
    depth=PHASE
    n=len(scores)
    def soft(i):
        m=jnp.max(scores[i],axis=1,keepdims=True)
        tops.append(m)
        return jnp.exp2(scores[i]-m).astype(BF)
    ps=[]
    for i in range(n+depth):
        if i<n: ps.append(soft(i))
        if i>=depth: outs.append(dot(ps[i-depth],tasks[(i-depth)//2][2][(i-depth)%2],NN))
    done=[]
    for t,(q,_,_,_) in enumerate(tasks):
        os=[];augs=[]
        for h in (0,1):
            o=outs[2*t+h]
            os.append(o/pltpu.roll(o,64,1))
            augs.append(spread(q,h,-(tops[2*t+h]+jnp.log2(o)),lane))
        done.append((jnp.where(lane<64,os[0],os[1]),augs))
    return done
def fwd_store(refs,rows,o,augs):
    o_ref,ol_ref,qa_ref=refs
    o_ref[rows,:]=o.astype(BF)
    ol_ref[rows,:]=(o-o.astype(BF).astype(F32)).astype(BF)
    for h in (0,1): qa_ref[h,rows,:]=augs[h]
def fwd_kernel(bq,info,q_ref,k_ref,v_ref,*refs):
    *refs,vs_ref=refs
    single=info[0]==1
    @pl.when(single)
    def _():
        v=v_ref[0:FILLED,:]
        for h in (0,1): vs_ref[h,...]=ones3(v,h,lanes(FILLED),64)
        lq=lanes(bq)
        @pl.loop(0,FILLED//bq)
        def _(r):
            rows=pl.ds(pl.multiple_of(r*bq,bq),bq)
            (o,augs),=fwd_tiles([(q_ref[rows,:],k_ref[0:FILLED,:],(vs_ref[0],vs_ref[1]),None)],lq)
            fwd_store(refs,rows,o,augs)
    @pl.when(info[0]==2)
    def _():
        lq=lanes(128)
        each=[slice(i*128,i*128+128) for i in range(13)]
        tasks=[(q_ref[r,:],k_ref[r,:],[ones3(v_ref[r,:],h,lq,64) for h in (0,1)],None) for r in each]
        for r,(o,augs) in zip(each,fwd_tiles(tasks,lq)): fwd_store(refs,r,o,augs)
    @pl.when(info[0]==0)
    def _():
        col=lax.broadcasted_iota(jnp.int32,(128,512),1)
        lw=lanes(512); lq=lanes(128)
        @pl.loop(0,13)
        def _(i):
            lo=info[1+i]; hi=info[14+i]
            at=jnp.minimum(lo,9)
            window=pl.ds(pl.multiple_of(at*128,128),512)
            k=k_ref[window,:]; v=v_ref[window,:]
            vs=[ones3(v,h,lw,64) for h in (0,1)]
            keep=(col>=(lo-at)*128)&(col<(hi-at)*128)
            rows=pl.ds(pl.multiple_of(i*128,128),128)
            (o,augs),=fwd_tiles([(q_ref[rows,:],k,vs,keep)],lq)
            fwd_store(refs,rows,o,augs)
    rows=slice(FILLED,FILLED+PAD)
    lp=lanes(PAD)
    v=v_ref[rows,:]
    (o,augs),=fwd_tiles([(q_ref[rows,:],k_ref[rows,:],[ones3(v,h,lp,64) for h in (0,1)],None)],lp)
    fwd_store(refs,rows,o,augs)
def attn_fwd(info,qkv,first,count,bq=416):
    L,W3=qkv.shape; n=W3//384
    spec=lambda j: pl.BlockSpec((L,128),lambda p,s,j=j:(0,p+first+j*n))
    one=pl.BlockSpec((L,128),lambda p,s:(0,p))
    return pl.pallas_call(functools.partial(fwd_kernel,bq),
        out_shape=(jax.ShapeDtypeStruct((L,count*128),BF),)*2+(jax.ShapeDtypeStruct((2*count,L,128),BF),),
        grid_spec=pltpu.PrefetchScalarGridSpec(num_scalar_prefetch=1,grid=(count,),
            in_specs=[spec(0),spec(1),spec(2)],
            out_specs=(one,one,pl.BlockSpec((2,L,128),lambda p,s:(p,0,0))),
            scratch_shapes=[pltpu.VMEM((2,FILLED,128),BF)]),
        compiler_params=pltpu.CompilerParams(vmem_limit_bytes=50<<20),name="attn_forward",
        cost_estimate=pl.CostEstimate(flops=8*count*L*L*256,bytes_accessed=10*L*count*128,transcendentals=2*count*L*L))(info,qkv,qkv,qkv)
def deltas(g,o,ol,lane):
    prod=g.astype(F32)*(o.astype(F32)+ol.astype(F32))
    return [augment(g,h,-jnp.sum(jnp.where((lane//64)==h,prod,0.0),axis=1,keepdims=True),lane) for h in (0,1)]
def bwd_tiles(tasks,lane):
    khs=[ones3(t[1],t[4],lane) for t in tasks]
    ps=[dot(kh,t[0],NT) for kh,t in zip(khs,tasks)]
    ds=[dot(ones3(t[2],t[4],lane),t[3],NT) for t in tasks]
    done=[]
    for kh,p,d,(qa,_,_,ga,h,keep) in zip(khs,ps,ds,tasks):
        p=jnp.exp2(p)
        if keep is not None: p=jnp.where(keep,p,0.0)
        d=(p*d).astype(BF)
        done.append((kh,p.astype(BF),d,qa,ga))
    return [(dot(d,kh,TN),dot(d,qa,NN),dot(p,ga,NN)) for kh,p,d,qa,ga in done]
LN2=0.6931471805599453
def both(a,lane): return jnp.where(lane<64,a[0],a[1])
def bwd_alone(each,lane,qa_ref,k_ref,v_ref,o_ref,ol_ref,g_ref,dq_ref,dk_ref,dv_ref):
    tasks=[]
    for r in each:
        gas=deltas(g_ref[r,:],o_ref[r,:],ol_ref[r,:],lane)
        tasks+=[(qa_ref[h,r,:],k_ref[r,:],v_ref[r,:],gas[h],h,None) for h in (0,1)]
    got=bwd_tiles(tasks,lane)
    for i,r in enumerate(each):
        x,y=got[2*i],got[2*i+1]
        dq_ref[r,:]=(both((x[0],y[0]),lane)*0.125).astype(BF)
        dk_ref[r,:]=(both((x[1],y[1]),lane)*LN2).astype(BF)
        dv_ref[r,:]=both((x[2],y[2]),lane).astype(BF)
def bwd_kernel(bk,joined,info,qa_ref,k_ref,v_ref,o_ref,ol_ref,g_ref,*rest):
    d_ref,sum_ref,acc,acc_k,acc_v,ga_ref=rest[1:] if joined else rest
    dq_ref,dk_ref,dv_ref=d_ref.at[0],d_ref.at[1],d_ref.at[2]
    tile_refs=(qa_ref,k_ref,v_ref,o_ref,ol_ref,g_ref,dq_ref,dk_ref,dv_ref)
    single=info[0]==1
    @pl.when(single)
    def _():
        lf=lanes(FILLED)
        gas=deltas(g_ref[0:FILLED,:],o_ref[0:FILLED,:],ol_ref[0:FILLED,:],lf)
        acc[...]=jnp.zeros_like(acc)
        lb=lanes(bk)
        ga_ref[0,...]=gas[0]; ga_ref[1,...]=gas[1]
        @pl.loop(0,FILLED//bk)
        def _(r):
            rows=pl.ds(pl.multiple_of(r*bk,bk),bk)
            k=k_ref[rows,:]; v=v_ref[rows,:]
            dks=[];dvs=[]
            got=bwd_tiles([(qa_ref[h,0:FILLED,:],k,v,ga_ref[h],h,None) for h in (0,1)],lb)
            for h in (0,1):
                dq,dk,dv=got[h]
                acc[h,0:FILLED,:]+=dq
                dks.append(dk); dvs.append(dv)
            dk_ref[rows,:]=(both(dks,lb)*LN2).astype(BF)
            dv_ref[rows,:]=both(dvs,lb).astype(BF)
        dq_ref[0:FILLED,:]=(jnp.where(lf<64,acc[0,0:FILLED,:],acc[1,0:FILLED,:])*0.125).astype(BF)
    @pl.when(info[0]==2)
    def _():
        lq=lanes(128)
        bwd_alone([slice(i*128,i*128+128) for i in range(13)],lq,*tile_refs)
    @pl.when(info[0]==0)
    def _():
        row=lax.broadcasted_iota(jnp.int32,(512,128),0)
        lw=lanes(512); lq=lanes(128)
        acc_k[...]=jnp.zeros_like(acc_k); acc_v[...]=jnp.zeros_like(acc_v)
        @pl.loop(0,13)
        def _(i):
            lo=info[1+i]; hi=info[14+i]
            at=jnp.minimum(lo,9)
            window=pl.ds(pl.multiple_of(at*128,128),512)
            k=k_ref[window,:]; v=v_ref[window,:]
            keep=(row>=(lo-at)*128)&(row<(hi-at)*128)
            rows=pl.ds(pl.multiple_of(i*128,128),128)
            gas=deltas(g_ref[rows,:],o_ref[rows,:],ol_ref[rows,:],lq)
            dqs=[]
            got=bwd_tiles([(qa_ref[h,rows,:],k,v,gas[h],h,keep) for h in (0,1)],lw)
            for h in (0,1):
                dq,dk,dv=got[h]
                dqs.append(dq)
                acc_k[h,window,:]+=dk
                acc_v[h,window,:]+=dv
            dq_ref[rows,:]=(both(dqs,lq)*0.125).astype(BF)
        lf=lanes(FILLED)
        dk_ref[0:FILLED,:]=(jnp.where(lf<64,acc_k[0],acc_k[1])*LN2).astype(BF)
        dv_ref[0:FILLED,:]=jnp.where(lf<64,acc_v[0],acc_v[1]).astype(BF)
    bwd_alone([slice(FILLED,FILLED+PAD)],lanes(PAD),*tile_refs)
    sum_ref[0:1,:]=jnp.sum(dq_ref[...].astype(F32),axis=0,keepdims=True)
    sum_ref[1:2,:]=jnp.sum(dv_ref[...].astype(F32),axis=0,keepdims=True)
def attn_bwd(info,qa,qkv,o,ol,g,first,count,inner,wide,at,into=None,bk=416):
    L,W3=qkv.shape; n=W3//384
    spec=lambda j: pl.BlockSpec((L,128),lambda p,s,j=j:(0,p+first+j*n))
    one=pl.BlockSpec((L,128),lambda p,s:(0,p))
    part=pl.BlockSpec((L,128),lambda p,s:(0,p+inner))
    every=pl.BlockSpec((L,128),lambda p,s:(0,p+first))
    return pl.pallas_call(functools.partial(bwd_kernel,bk,into is not None),
        input_output_aliases={} if into is None else {7:0},
        out_shape=(jax.ShapeDtypeStruct((3,L,wide*128),BF),jax.ShapeDtypeStruct((2,count*128),F32)),
        grid_spec=pltpu.PrefetchScalarGridSpec(num_scalar_prefetch=1,grid=(count,),
            in_specs=[pl.BlockSpec((2,L,128),lambda p,s:(p+inner,0,0)),spec(1),spec(2),part,part,every]+([] if into is None else [pl.BlockSpec(memory_space=pl.ANY)]),
            out_specs=(pl.BlockSpec((3,L,128),lambda p,s:(0,0,p+at)),pl.BlockSpec((2,128),lambda p,s:(0,p))),
            scratch_shapes=[pltpu.VMEM((2,FILLED,128),F32)]*3+[pltpu.VMEM((2,FILLED,128),BF)]),
        compiler_params=pltpu.CompilerParams(vmem_limit_bytes=56<<20),name="attn_backward",
        cost_estimate=pl.CostEstimate(flops=20*count*L*L*256,bytes_accessed=16*L*count*128,transcendentals=2*count*L*L))(*((info,qa,qkv,qkv,o,ol,g) if into is None else (info,qa,qkv,qkv,o,ol,g,into)))


def gelu_exact(values):
    return jax.nn.gelu(values, approximate=False)


def norm_forward(values, gain, shift):
    centered = values - jnp.mean(values, axis=-1, keepdims=True)
    inverse = lax.rsqrt(jnp.mean(centered * centered, axis=-1, keepdims=True) + 1e-05)
    unit_part = centered * inverse
    return (unit_part * gain + shift, unit_part, inverse)


def norm_backward(grad_out, unit_part, inverse, gain):
    scaled = grad_out * gain
    centered = scaled - jnp.mean(scaled, axis=-1, keepdims=True)
    grad_in = inverse * (
        centered - unit_part * jnp.mean(scaled * unit_part, axis=-1, keepdims=True)
    )
    return (grad_in, jnp.sum(grad_out * unit_part, axis=0), jnp.sum(grad_out, axis=0))


def attention_forward(query_all, key_all, value_all, segments, head_dim):
    length, local_width = (query_all.shape[1], query_all.shape[2])
    head_count = local_width // head_dim
    block_len = length // 3
    score_scale = head_dim ** (-0.5)

    def per_sequence(pieces):
        queries, key_rows, value_rows, seq_ids = pieces
        key_heads = key_rows.reshape(length, head_count, head_dim)
        value_heads = value_rows.reshape(length, head_count, head_dim)

        def per_block(block_pieces):
            query_part, id_part = block_pieces
            query_heads = query_part.reshape(block_len, head_count, head_dim)
            scores = (
                jnp.einsum(
                    "qhd,khd->hqk", query_heads, key_heads, preferred_element_type=jnp.float32
                )
                * score_scale
            )
            masked = jnp.where(id_part[None, :, None] == seq_ids[None, None, :], scores, -1e30)
            maxima = jnp.max(masked, axis=-1, keepdims=True)
            exp_scores = jnp.exp(masked - maxima)
            totals = jnp.sum(exp_scores, axis=-1, keepdims=True)
            weights_low = (exp_scores / totals).astype(jnp.bfloat16)
            context = jnp.einsum(
                "hqk,khd->qhd", weights_low, value_heads, preferred_element_type=jnp.float32
            )
            return (
                context.astype(jnp.bfloat16).reshape(block_len, local_width),
                (maxima + jnp.log(totals))[..., 0],
            )

        contexts, logsums = lax.map(
            per_block, (queries.reshape(3, block_len, local_width), seq_ids.reshape(3, block_len))
        )
        return (contexts.reshape(length, local_width), logsums)

    return lax.map(per_sequence, (query_all, key_all, value_all, segments))


def attention_backward(query_all, key_all, value_all, segments, logsums, grad_all, head_dim):
    length, local_width = (query_all.shape[1], query_all.shape[2])
    head_count = local_width // head_dim
    block_len = length // 3
    score_scale = head_dim ** (-0.5)

    def per_sequence(pieces):
        queries, key_rows, value_rows, seq_ids, sum_rows, grad_rows = pieces
        key_heads = key_rows.reshape(length, head_count, head_dim)
        value_heads = value_rows.reshape(length, head_count, head_dim)

        def per_block(carry, block_pieces):
            key_total, value_total = carry
            query_part, id_part, sum_part, grad_part = block_pieces
            query_heads = query_part.reshape(block_len, head_count, head_dim)
            grad_heads = grad_part.reshape(block_len, head_count, head_dim)
            scores = (
                jnp.einsum(
                    "qhd,khd->hqk", query_heads, key_heads, preferred_element_type=jnp.float32
                )
                * score_scale
            )
            allowed = id_part[None, :, None] == seq_ids[None, None, :]
            prob_weights = jnp.where(allowed, jnp.exp(scores - sum_part[:, :, None]), 0.0)
            grad_probs = jnp.einsum(
                "qhd,khd->hqk", grad_heads, value_heads, preferred_element_type=jnp.float32
            )
            delta = jnp.sum(prob_weights * grad_probs, axis=-1, keepdims=True)
            grad_scores = (prob_weights * (grad_probs - delta)).astype(jnp.bfloat16)
            query_grad = (
                jnp.einsum(
                    "hqk,khd->qhd", grad_scores, key_heads, preferred_element_type=jnp.float32
                )
                * score_scale
            )
            key_total = (
                key_total
                + jnp.einsum(
                    "hqk,qhd->khd", grad_scores, query_heads, preferred_element_type=jnp.float32
                )
                * score_scale
            )
            value_total = value_total + jnp.einsum(
                "hqk,qhd->khd",
                prob_weights.astype(jnp.bfloat16),
                grad_heads,
                preferred_element_type=jnp.float32,
            )
            return (
                (key_total, value_total),
                query_grad.astype(jnp.bfloat16).reshape(block_len, local_width),
            )

        zero_heads = jnp.zeros((length, head_count, head_dim), jnp.float32)
        (key_total, value_total), query_grads = lax.scan(
            per_block,
            (zero_heads, zero_heads),
            (
                queries.reshape(3, block_len, local_width),
                seq_ids.reshape(3, block_len),
                sum_rows,
                grad_rows.reshape(3, block_len, local_width),
            ),
        )
        return (
            query_grads.reshape(length, local_width),
            key_total.astype(jnp.bfloat16).reshape(length, local_width),
            value_total.astype(jnp.bfloat16).reshape(length, local_width),
        )

    return lax.map(per_sequence, (query_all, key_all, value_all, segments, logsums, grad_all))


def per_device(
    inputs,
    timesteps,
    segments,
    cotangent,
    w_qkv,
    b_query,
    b_value,
    w_out,
    b_out,
    ln1_gain,
    ln1_bias,
    w_up,
    b_up,
    w_down,
    b_down,
    ln2_gain,
    ln2_bias,
    w_time,
    b_time,
):
    groups, local_len, model_width = inputs.shape
    row_count = groups * local_len
    head_dim = D // HEADS
    fraction = timesteps.astype(jnp.float32) / TSTEPS
    start_sum = (
        inputs.astype(jnp.float32)
        + fraction[:, None, None] * w_time.astype(jnp.float32)
        + b_time.astype(jnp.float32)
    )
    start_low = start_sum.astype(jnp.bfloat16)
    projected = jnp.einsum("bld,de->ble", start_low, w_qkv, preferred_element_type=jnp.float32)
    query_low = (projected[..., :model_width] + b_query.astype(jnp.float32)).astype(jnp.bfloat16)
    key_low = projected[..., model_width : 2 * model_width].astype(jnp.bfloat16)
    value_low = (projected[..., 2 * model_width :] + b_value.astype(jnp.float32)).astype(
        jnp.bfloat16
    )
    query_all, key_all, value_all = (
        lax.all_to_all(query_low, "seq", split_axis=2, concat_axis=1, tiled=True),
        lax.all_to_all(key_low, "seq", split_axis=2, concat_axis=1, tiled=True),
        lax.all_to_all(value_low, "seq", split_axis=2, concat_axis=1, tiled=True),
    )
    context_heads, logsums = attention_forward(query_all, key_all, value_all, segments, head_dim)
    context = lax.all_to_all(context_heads, "seq", split_axis=1, concat_axis=2, tiled=True)
    context_rows = context.reshape(row_count, model_width)
    start_rows = start_sum.reshape(row_count, model_width)
    residual_one = (
        start_rows
        + jnp.dot(context_rows, w_out, preferred_element_type=jnp.float32)
        + b_out.astype(jnp.float32)
    )
    normed, unit_one, inverse_one = norm_forward(
        residual_one, ln1_gain.astype(jnp.float32), ln1_bias.astype(jnp.float32)
    )
    normed_low = normed.astype(jnp.bfloat16)
    hidden_pre = jnp.dot(normed_low, w_up, preferred_element_type=jnp.float32) + b_up.astype(
        jnp.float32
    )
    activated, gelu_pull = jax.vjp(gelu_exact, hidden_pre)
    activated_low = activated.astype(jnp.bfloat16)
    residual_two = (
        normed
        + jnp.dot(activated_low, w_down, preferred_element_type=jnp.float32)
        + b_down.astype(jnp.float32)
    )
    result, unit_two, inverse_two = norm_forward(
        residual_two, ln2_gain.astype(jnp.float32), ln2_bias.astype(jnp.float32)
    )
    output = result.astype(jnp.bfloat16).reshape(groups, local_len, model_width)
    grad_result = cotangent.reshape(row_count, model_width).astype(jnp.float32)
    grad_two, grad_ln2_gain, grad_ln2_bias = norm_backward(
        grad_result, unit_two, inverse_two, ln2_gain.astype(jnp.float32)
    )
    grad_b_down = jnp.sum(grad_two, axis=0)
    grad_two_low = grad_two.astype(jnp.bfloat16)
    grad_w_down = jnp.einsum(
        "rf,rd->fd", activated_low, grad_two_low, preferred_element_type=jnp.float32
    )
    grad_activated = jnp.einsum(
        "rd,fd->rf", grad_two_low, w_down, preferred_element_type=jnp.float32
    )
    grad_hidden = gelu_pull(grad_activated)[0]
    grad_b_up = jnp.sum(grad_hidden, axis=0)
    grad_hidden_low = grad_hidden.astype(jnp.bfloat16)
    grad_w_up = jnp.einsum(
        "rd,rf->df", normed_low, grad_hidden_low, preferred_element_type=jnp.float32
    )
    grad_normed = grad_two + jnp.einsum(
        "rf,df->rd", grad_hidden_low, w_up, preferred_element_type=jnp.float32
    )
    grad_one, grad_ln1_gain, grad_ln1_bias = norm_backward(
        grad_normed, unit_one, inverse_one, ln1_gain.astype(jnp.float32)
    )
    grad_b_out = jnp.sum(grad_one, axis=0)
    grad_one_low = grad_one.astype(jnp.bfloat16)
    grad_w_out = jnp.einsum(
        "rd,re->de", context_rows, grad_one_low, preferred_element_type=jnp.float32
    )
    grad_context = (
        jnp.einsum("re,de->rd", grad_one_low, w_out, preferred_element_type=jnp.float32)
        .astype(jnp.bfloat16)
        .reshape(groups, local_len, model_width)
    )
    grad_context_heads = lax.all_to_all(
        grad_context, "seq", split_axis=2, concat_axis=1, tiled=True
    )
    query_grads, key_grads, value_grads = attention_backward(
        query_all, key_all, value_all, segments, logsums, grad_context_heads, head_dim
    )
    grad_query, grad_key, grad_value = (
        lax.all_to_all(query_grads, "seq", split_axis=1, concat_axis=2, tiled=True),
        lax.all_to_all(key_grads, "seq", split_axis=1, concat_axis=2, tiled=True),
        lax.all_to_all(value_grads, "seq", split_axis=1, concat_axis=2, tiled=True),
    )
    grad_projected = jnp.concatenate((grad_query, grad_key, grad_value), axis=2).reshape(
        row_count, 3 * model_width
    )
    grad_w_qkv = jnp.einsum(
        "rd,re->de",
        start_low.reshape(row_count, model_width),
        grad_projected,
        preferred_element_type=jnp.float32,
    )
    grad_b_query = jnp.sum(grad_query.astype(jnp.float32), axis=(0, 1))
    grad_b_value = jnp.sum(grad_value.astype(jnp.float32), axis=(0, 1))
    grad_start = grad_one + jnp.einsum(
        "re,de->rd", grad_projected, w_qkv, preferred_element_type=jnp.float32
    )
    grad_inputs = grad_start.astype(jnp.bfloat16).reshape(groups, local_len, model_width)
    per_sequence_grad = jnp.sum(grad_start.reshape(groups, local_len, model_width), axis=1)
    grad_w_time = jnp.einsum("g,gd->d", fraction, per_sequence_grad)
    grad_b_time = jnp.sum(per_sequence_grad, axis=0)
    (
        sum_w_qkv,
        sum_b_query,
        sum_b_value,
        sum_w_out,
        sum_b_out,
        sum_ln1_gain,
        sum_ln1_bias,
        sum_w_up,
        sum_b_up,
        sum_w_down,
        sum_b_down,
        sum_ln2_gain,
        sum_ln2_bias,
        sum_w_time,
        sum_b_time,
    ) = (
        lax.psum_scatter(grad_w_qkv, ("batch", "seq"), scatter_dimension=0, tiled=True),
        lax.psum_scatter(grad_b_query, ("batch", "seq"), scatter_dimension=0, tiled=True),
        lax.psum_scatter(grad_b_value, ("batch", "seq"), scatter_dimension=0, tiled=True),
        lax.psum_scatter(grad_w_out, ("batch", "seq"), scatter_dimension=0, tiled=True),
        lax.psum_scatter(grad_b_out, ("batch", "seq"), scatter_dimension=0, tiled=True),
        lax.psum_scatter(grad_ln1_gain, ("batch", "seq"), scatter_dimension=0, tiled=True),
        lax.psum_scatter(grad_ln1_bias, ("batch", "seq"), scatter_dimension=0, tiled=True),
        lax.psum_scatter(grad_w_up, ("batch", "seq"), scatter_dimension=0, tiled=True),
        lax.psum_scatter(grad_b_up, ("batch", "seq"), scatter_dimension=0, tiled=True),
        lax.psum_scatter(grad_w_down, ("batch", "seq"), scatter_dimension=0, tiled=True),
        lax.psum_scatter(grad_b_down, ("batch", "seq"), scatter_dimension=0, tiled=True),
        lax.psum_scatter(grad_ln2_gain, ("batch", "seq"), scatter_dimension=0, tiled=True),
        lax.psum_scatter(grad_ln2_bias, ("batch", "seq"), scatter_dimension=0, tiled=True),
        lax.psum_scatter(grad_w_time, ("batch", "seq"), scatter_dimension=0, tiled=True),
        lax.psum_scatter(grad_b_time, ("batch", "seq"), scatter_dimension=0, tiled=True),
    )
    return (
        output,
        grad_inputs,
        sum_w_qkv,
        sum_b_query,
        sum_b_value,
        sum_w_out,
        sum_b_out,
        sum_ln1_gain,
        sum_ln1_bias,
        sum_w_up,
        sum_b_up,
        sum_w_down,
        sum_b_down,
        sum_ln2_gain,
        sum_ln2_bias,
        sum_w_time,
        sum_b_time,
    )


SLOPE = F32
LOG2E = 1.4426950408889634


def layer_norm(values):
    centered = values - jnp.mean(values, axis=1, keepdims=True)
    inverse = lax.rsqrt(jnp.mean(centered * centered, axis=1, keepdims=True) + 1e-05)
    return centered * inverse, inverse


def layer_norm_back(scaled, unit_part, inverse):
    return inverse * (
        scaled
        - jnp.mean(scaled, axis=1, keepdims=True)
        - unit_part * jnp.mean(scaled * unit_part, axis=1, keepdims=True)
    )


def gelu_pair(v):
    bell = jnp.exp2(v * v * (-0.5 * LOG2E))
    base = 1.0 + 0.2316418882663604 * jnp.abs(v)
    t = pltpu.reciprocal(base, approx=True)
    t = t * (2.0 - base * t)
    tail = t * (
        0.127414796
        + t * (-0.142248368 + t * (0.7107068705 + t * (-0.7265760135 + t * 0.5307027145)))
    )
    tail = tail * bell
    cover = jnp.where(v >= 0, 1.0 - tail, tail)
    return v * cover, cover + v * bell * 0.3989422804014327


def middle_kernel(
    fc,
    sel_ref,
    frac_ref,
    inp_ref,
    ctx_a_ref,
    ctx_b_ref,
    cot_ref,
    vec_ref,
    b_up_ref,
    wo_a_ref,
    wo_b_ref,
    w_up_hbm,
    w_down_hbm,
    out_ref,
    norm_ref,
    act_ref,
    two_ref,
    hid_ref,
    one_ref,
    onel_ref,
    small_ref,
    smallup_ref,
    w_up,
    w_down,
    slope,
    sems,
):
    step = pl.program_id(0)
    up_copy = pltpu.make_async_copy(w_up_hbm, w_up, sems.at[0])
    down_copy = pltpu.make_async_copy(w_down_hbm, w_down, sems.at[1])

    @pl.when(step == 0)
    def _():
        up_copy.start()
        down_copy.start()
        small_ref[...] = jnp.zeros_like(small_ref)
        smallup_ref[...] = jnp.zeros_like(smallup_ref)

    vec = lambda i: vec_ref[i : i + 1, :]
    start = inp_ref[...].astype(F32) + (frac_ref[0] * vec(0) + vec(1))
    residual = (
        start
        + dot(ctx_a_ref[...], wo_a_ref[...].reshape(-1, wo_a_ref.shape[-1]), NN)
        + dot(ctx_b_ref[...], wo_b_ref[...].reshape(-1, wo_b_ref.shape[-1]), NN)
        + vec(2)
    )
    unit_one, inverse_one = layer_norm(residual)
    normed = unit_one * vec(3) + vec(4)
    low = normed.astype(BF)
    norm_ref[...] = low

    @pl.when(step == 0)
    def _():
        up_copy.wait()
        down_copy.wait()

    width = w_up.shape[1]
    total = normed + vec(5)
    for f in range(0, width, fc):
        cols = slice(f, f + fc)
        v = dot(low, w_up[:, cols], NN) + b_up_ref[:, cols]
        a, g = gelu_pair(v)
        a = a.astype(BF)
        act_ref[:, cols] = a
        slope[:, cols] = g.astype(slope.dtype)
        total = total + dot(a, w_down[cols, :], NN)
    unit_two, inverse_two = layer_norm(total)
    out_ref[...] = (unit_two * vec(6) + vec(7)).astype(BF)
    cot = cot_ref[...].astype(F32)
    two = layer_norm_back(cot * vec(6), unit_two, inverse_two)
    add = lambda v: jnp.sum(v, axis=0, keepdims=True)
    small_ref[3:4, :] += add(two)
    small_ref[4:5, :] += add(cot * unit_two)
    small_ref[5:6, :] += add(cot)
    two_low = two.astype(BF)
    two_ref[...] = two_low
    total = two
    for f in range(0, width, fc):
        cols = slice(f, f + fc)
        d = dot(two_low, w_down[cols, :], NT) * slope[:, cols].astype(F32)
        smallup_ref[:, cols] += add(d)
        d = d.astype(BF)
        hid_ref[:, cols] = d
        total = total + dot(d, w_up[:, cols], NT)
    small_ref[1:2, :] += add(total * unit_one)
    small_ref[2:3, :] += add(total)
    one = layer_norm_back(total * vec(3), unit_one, inverse_one)
    small_ref[0:1, :] += add(one)
    one_ref[...] = one
    onel_ref[...] = one.astype(BF)


def middle(core, fraction, inp, ctx_a, ctx_b, cot, vecs, b_up, w_out, w_up, w_down, br=288, fc=2048):
    rows, model = inp.shape
    width = w_up.shape[1]
    half = model // 2
    quads = w_out.shape[0]
    row = lambda w: pl.BlockSpec((br, w), lambda i, s: (i, 0))
    fixed = lambda shape: pl.BlockSpec(shape, lambda i, s: (0,) * len(shape))
    wo = lambda flip: pl.BlockSpec(
        (quads, 1, model // quads // 2, model),
        (lambda i, s: (0, s[0], 0, 0)) if not flip else (lambda i, s: (0, 1 - s[0], 0, 0)),
    )
    out = lambda w, t: jax.ShapeDtypeStruct((rows, w), t)
    return pl.pallas_call(
        functools.partial(middle_kernel, fc),
        out_shape=(
            out(model, BF),
            out(model, BF),
            out(width, BF),
            out(model, BF),
            out(width, BF),
            out(model, F32),
            out(model, BF),
            jax.ShapeDtypeStruct((8, model), F32),
            jax.ShapeDtypeStruct((1, width), F32),
        ),
        grid_spec=pltpu.PrefetchScalarGridSpec(
            num_scalar_prefetch=1,
            grid=(rows // br,),
            in_specs=[
                pl.BlockSpec(memory_space=pltpu.SMEM),
                row(model),
                row(half),
                row(half),
                row(model),
                fixed((8, model)),
                fixed((1, width)),
                wo(False),
                wo(True),
                pl.BlockSpec(memory_space=pl.ANY),
                pl.BlockSpec(memory_space=pl.ANY),
            ],
            out_specs=(
                row(model),
                row(model),
                row(width),
                row(model),
                row(width),
                row(model),
                row(model),
                fixed((8, model)),
                fixed((1, width)),
            ),
            scratch_shapes=[
                pltpu.VMEM(w_up.shape, BF),
                pltpu.VMEM(w_down.shape, BF),
                pltpu.VMEM((br, width), SLOPE),
                pltpu.SemaphoreType.DMA((2,)),
            ],
        ),
        compiler_params=pltpu.CompilerParams(vmem_limit_bytes=60 << 20),
        cost_estimate=pl.CostEstimate(
            flops=4 * rows * model * (model // 2 + 2 * width),
            bytes_accessed=4 * model * width + rows * (16 * model + 4 * width),
            transcendentals=rows * width * 2,
        ),
        name="middle",
    )(core, fraction, inp, ctx_a, ctx_b, cot, vecs, b_up, w_out, w_out, w_up, w_down)


def grad_kernel(count, extra, *refs):
    lhs = [r[...] for r in refs[1 : 1 + count]]
    rhs_ref = refs[1 + count]
    out_ref = refs[-1]
    left = lhs[0] if count == 1 else jnp.concatenate(lhs, axis=1)
    right = rhs_ref[0] if len(rhs_ref.shape) == 3 else rhs_ref[...]
    total = dot(left, right, TN)
    if extra:
        total = total + refs[2 + count][...].astype(F32)
    out_ref[...] = total.astype(BF)


def weight_grad(sel, lhs, rhs, add=None, cols=1024, quads=4, pairs=2):
    depth, width = lhs.shape
    three = rhs.ndim == 3
    n = rhs.shape[0] * rhs.shape[2] if three else rhs.shape[1]
    cols = rhs.shape[2] if three else cols
    w = width // (quads * pairs)
    extra = add is not None
    if w >= 512:
        grid, count = (quads,), 1
        ins = [
            pl.BlockSpec((depth, w), lambda i, s: (0, pairs * i + s[0])),
            pl.BlockSpec((depth, n), lambda i, s: (0, 0)),
        ]
        out = pl.BlockSpec((w, n), lambda i, s: (i, 0))
        args = [lhs, rhs]
    else:
        grid, count = (n // cols,), quads
        ins = [
            pl.BlockSpec((depth, w), lambda i, s, q=q: (0, pairs * q + s[0])) for q in range(quads)
        ] + [
            pl.BlockSpec((1, depth, cols), lambda i, s: (i, 0, 0))
            if three
            else pl.BlockSpec((depth, cols), lambda i, s: (0, i))
        ]
        out = pl.BlockSpec((quads * w, cols), lambda i, s: (0, i))
        args = [lhs] * quads + [rhs]
    if extra:
        ins.append(out)
        args.append(add)
    total = quads * w
    return pl.pallas_call(
        functools.partial(grad_kernel, count, extra),
        out_shape=jax.ShapeDtypeStruct((total, n), BF),
        grid_spec=pltpu.PrefetchScalarGridSpec(
            num_scalar_prefetch=1, grid=grid, in_specs=ins, out_specs=out
        ),
        compiler_params=pltpu.CompilerParams(vmem_limit_bytes=48 << 20),
        cost_estimate=pl.CostEstimate(
            flops=2 * depth * total * n,
            bytes_accessed=2 * depth * (total + n) + (4 if extra else 2) * total * n,
            transcendentals=0,
        ),
        name="weight_grad",
    )(sel, *args)


def finish_kernel(sel_ref, base_ref, mine_ref, got_ref, w_mine_ref, w_got_ref, out_ref, *rest):
    n = mine_ref.shape[2]
    total = base_ref[...]
    for t in range(3):
        total = total + dot(mine_ref[t], w_mine_ref[:, t * n : (t + 1) * n], NT)
        total = total + dot(got_ref[t], w_got_ref[:, t * n : (t + 1) * n], NT)
    out_ref[...] = total.astype(out_ref.dtype)
    if rest:
        step = pl.program_id(0)

        @pl.when(step == 0)
        def _():
            rest[0][...] = jnp.zeros_like(rest[0])

        rest[0][...] += jnp.sum(total, axis=0, keepdims=True)


def add_start(core, base, grads, got, w_mine, w_got, last, br=288):
    rows, model = base.shape
    n = got.shape[2]
    steps = rows // br
    fixed = lambda w: pl.BlockSpec(w.shape, lambda i, s: (0, 0))
    row = pl.BlockSpec((br, model), lambda i, s: (i, 0))
    outs = [jax.ShapeDtypeStruct((rows, model), BF if last else F32)]
    specs = [row]
    if last:
        outs.append(jax.ShapeDtypeStruct((1, model), F32))
        specs.append(pl.BlockSpec((1, model), lambda i, s: (0, 0)))
    return pl.pallas_call(
        finish_kernel,
        out_shape=tuple(outs),
        grid_spec=pltpu.PrefetchScalarGridSpec(
            num_scalar_prefetch=1,
            grid=(steps,),
            in_specs=[
                row,
                pl.BlockSpec((3, br, n), lambda i, s: (0, s[0] * steps + i, 0)),
                pl.BlockSpec((3, br, n), lambda i, s: (0, i, 0)),
                fixed(w_mine),
                fixed(w_got),
            ],
            out_specs=tuple(specs),
        ),
        compiler_params=pltpu.CompilerParams(vmem_limit_bytes=40 << 20),
        cost_estimate=pl.CostEstimate(
            flops=12 * rows * n * model,
            bytes_accessed=8 * rows * model + 12 * n * (rows + model),
            transcendentals=0,
        ),
        name="add_start",
    )(core, base, grads, got, w_mine, w_got)


class Plan:
    def __init__(self, mesh):
        sizes = dict(mesh.shape)
        self.batch, self.depth = sizes["batch"], sizes["seq"]
        chips = self.batch // 2
        side = 1
        while side * side < chips:
            side *= 2
        self.nx, self.ny = side, chips // side

    def perm(self, target):
        pairs = []
        for y in range(self.ny):
            for x in range(self.nx):
                for c in range(2):
                    for z in range(self.depth):
                        to = target(y, x, c, z)
                        if to != (y, x, c, z):
                            pairs.append((self.index(y, x, c, z), self.index(*to)))
        return pairs

    def index(self, y, x, c, z):
        return ((y * self.nx + x) * 2 + c) * self.depth + z

    def send(self, value, target):
        return lax.ppermute(value, AXES, self.perm(target))

    def sibling(self, value):
        return self.send(value, lambda y, x, c, z: (y, x, 1 - c, z))


def pick(array, index, axis):
    return lax.dynamic_index_in_dim(array, index, axis, keepdims=False)


def tie(*values):
    return lax.optimization_barrier(values)


class Sum:
    def __init__(self, plan, terms, where):
        self.plan, self.terms = plan, terms
        self.where = dict(zip("yxz", where))

    def send(self, axis):
        plan, terms = self.plan, self.terms
        self.axis = axis
        self.at = terms.ndim - 4 if axis == "x" else 0
        if axis == "z":
            self.got = [lax.all_to_all(terms, "seq", 0, 0, tiled=True)]
            return self
        size = {"x": plan.nx, "y": plan.ny}[axis]
        here = self.where[axis]
        self.got = []
        for r in range(1, size):

            def target(y, x, c, z, r=r):
                at = {"y": y, "x": x}
                at[axis] = (at[axis] + r) % size
                return at["y"], at["x"], c, z

            self.got.append(plan.send(pick(terms, (here + r) % size, self.at), target))
        return self

    def add(self):
        if self.axis == "z":
            self.terms = jnp.sum(self.got[0].astype(F32), axis=0)
            return self.terms
        total = pick(self.terms, self.where[self.axis], self.at).astype(F32)
        for got in self.got:
            total = total + got.astype(F32)
        self.terms = total.astype(self.terms.dtype)
        return self.terms

    def hold(self, *others):
        self.terms, *rest = tie(self.terms, *others)
        return rest


def per_chip(
    plan,
    inputs,
    timesteps,
    segments,
    cotangent,
    w_qkv,
    b_query,
    b_value,
    w_out,
    b_out,
    ln1_gain,
    ln1_bias,
    w_up,
    b_up,
    w_down,
    b_down,
    ln2_gain,
    ln2_bias,
    w_time,
    b_time,
):
    local_len = inputs.shape[1]
    rows = 2 * local_len
    length = segments.shape[1]
    b = lax.axis_index("batch")
    z = lax.axis_index("seq")
    c, x, y = b % 2, (b // 2) % plan.nx, b // 2 // plan.nx
    part = z % 2
    where = (y, x, z)
    first = (segments[1, 0] == segments[1, 128 * 12]).astype(jnp.int32)
    which = lambda s: (first + s) % 2
    facts = jnp.concatenate(
        [segments[:, : 128 * 13 : 128], timesteps[:, None], jnp.zeros((2, 2), jnp.int32)], axis=1
    )
    facts = jnp.stack([pick(facts, which(0), 0), pick(facts, which(1), 0)])
    other_facts = plan.sibling(facts)
    facts = jnp.where(z // 2 == c, facts, other_facts)
    mine = pick(facts, z % 2, 0)
    marks = mine[:13]
    info = jnp.concatenate(
        [
            jnp.where(marks[:1] == marks[12:], 1, jnp.where(marks[12:] == marks[:1] + 12, 2, 0)),
            jnp.sum((marks[None, :] < marks[:, None]).astype(jnp.int32), axis=1),
            jnp.sum((marks[None, :] <= marks[:, None]).astype(jnp.int32), axis=1),
        ]
    )
    fraction = mine[13].astype(F32) / TSTEPS

    stays = z // 2 == c

    def exchange(parts):
        got = [
            plan.send(v, lambda y, x, c, z, j=j: (y, x, z // 2, 2 * c + (z + j) % 2))
            for j, v in enumerate(parts)
        ]
        return [(got[0], parts[0]), (got[1], None)]

    def arrived(got):
        return [jnp.where(stays, got[0][1], got[0][0]), got[1][0]]

    def gather_parts(array):
        return [pick(array, which((part + j) % 2), 0) for j in (0, 1)]

    def gather_end(got):
        got = arrived(got)
        return jnp.concatenate(
            [jnp.where(part == 0, got[0], got[1]), jnp.where(part == 0, got[1], got[0])], axis=0
        )

    def spread_parts(array):
        array = array.reshape(2, local_len, array.shape[-1])
        return [pick(array, (part + j) % 2, 0) for j in (0, 1)]

    def spread_end(got):
        got = arrived(got)
        swap = (part + first) % 2
        return jnp.stack(
            [jnp.where(swap == 0, got[0], got[1]), jnp.where(swap == 0, got[1], got[0])], axis=0
        )

    def whole(own, other):
        return jnp.where(c == 0, jnp.concatenate([own, other]), jnp.concatenate([other, own]))

    def halves(array, axis):
        shape = array.shape
        cut = shape[:axis] + (plan.ny * plan.nx, 2, -1) + shape[axis + 1 :]
        flat = shape[:axis] + (-1,) + shape[axis + 1 :]
        split = array.reshape(cut)
        return (
            pick(split, c, axis + 1).reshape(flat),
            pick(split, 1 - c, axis + 1).reshape(flat),
        )

    def blocks(array):
        return array.reshape(plan.ny, plan.nx, plan.depth, -1, array.shape[-1])

    model = inputs.shape[-1]
    half = model // 2
    quads = plan.ny * plan.nx
    core = jnp.stack([c]).astype(jnp.int32)
    away = 1 - core
    w_four = w_qkv.reshape(model, 3, quads, 2, half // quads)
    w_own, w_oth = pick(w_four, c, 3), pick(w_four, 1 - c, 3)
    bias = jnp.concatenate(
        [
            halves(b_query.astype(F32), 0)[0],
            jnp.zeros((half,), F32),
            halves(b_value.astype(F32), 0)[0],
        ]
    )
    w_out_own = halves(w_out, 0)[0]
    w_all = w_own.reshape(model, 3 * half)
    ahead = [range(0, quads // 2), range(quads // 2, quads)]
    groups = ahead
    cut = lambda w: [w[:, :, g.start : g.stop].reshape(model, -1) for g in groups]
    w_cut, w_cut_oth = cut(w_own), cut(w_oth)
    own_inputs = gather_end(exchange(gather_parts(inputs)))
    vecs = jnp.stack(
        [v.astype(F32) for v in (w_time, b_time, b_out, ln1_gain, ln1_bias, b_down, ln2_gain, ln2_bias)]
    )
    cot_parts = gather_parts(cotangent)
    own_inputs, w_all, w_cut, w_cut_oth, w_out_own, vecs, info, bias, cot_parts = tie(
        own_inputs, w_all, w_cut, w_cut_oth, w_out_own, vecs, info, bias, cot_parts
    )
    start = (
        own_inputs.astype(F32) + fraction * w_time.astype(F32)[None] + b_time.astype(F32)[None]
    )
    start_low = start.astype(BF)
    cot_parts, start_low = tie(cot_parts, start_low)
    own_cotangent = gather_end(exchange(cot_parts))
    start_full = whole(start_low, plan.sibling(start_low))
    scale = jnp.where(jnp.arange(3 * half) < half, 0.125 * LOG2E, 1.0)
    qkv = ((jnp.dot(start_full, w_all, preferred_element_type=F32) + bias) * scale).astype(BF)
    fwd = [attn_fwd(info, qkv, g.start, len(g)) for g in ahead]
    mine_of, away_of = [], []
    for g in range(2):
        split = fwd[g][0].reshape(2, rows, -1)
        mine_of.append(pick(split, c, 0))
        away_of.append(plan.sibling(pick(split, 1 - c, 0)))
    result, normed_low, act, two_low, hid, grad_one, one_low, small_sums, up_sums = middle(
        core,
        fraction[None],
        own_inputs,
        jnp.concatenate(mine_of, axis=1),
        jnp.concatenate(away_of, axis=1),
        own_cotangent,
        vecs,
        b_up.astype(F32)[None],
        w_out.reshape(quads, 2, -1, model),
        w_up,
        w_down,
    )
    one_sib = plan.sibling(one_low)
    output_got = exchange(spread_parts(result))
    down_part = weight_grad(away, act, two_low, quads=quads)
    normed_low, down_part = tie(normed_low, down_part)
    down_got = plan.sibling(down_part)
    up_part = weight_grad(away, normed_low, hid, quads=quads)
    act, up_part = tie(act, up_part)
    up_got = plan.sibling(up_part)
    down_sum = weight_grad(core, act, two_low, down_got, quads=quads)
    normed_low, down_sum = tie(normed_low, down_sum)
    down = Sum(plan, blocks(down_sum), where).send("x")
    up_sum = weight_grad(core, normed_low, hid, up_got, quads=quads)
    one_low, one_sib, up_sum = tie(one_low, one_sib, up_sum)
    up = Sum(plan, blocks(up_sum), where).send("y")
    grad_one_full = whole(one_low, one_sib)
    context = jnp.concatenate([f[0] for f in fwd], axis=1)
    out_sum = weight_grad(0 * core, context, grad_one_full, quads=quads, pairs=1, cols=512)
    grad_one_full, out_sum = tie(grad_one_full, out_sum)
    out = Sum(plan, blocks(out_sum), where).send("x")
    grad_context = lax.dot_general(
        grad_one_full, w_out_own, NT, preferred_element_type=F32
    ).astype(BF)

    def back(first, count, into=None):
        f = first // (quads // 2)
        start = ahead[f].start
        return attn_bwd(
            info,
            fwd[f][2],
            qkv,
            fwd[f][0],
            fwd[f][1],
            grad_context,
            first,
            count,
            first - start,
            quads // 2,
            first - start,
            into,
        )

    def away_rows(grads):
        return plan.sibling(pick(grads.reshape(3, 2, rows, -1), 1 - c, 1))

    def products(grads):
        cross_part = weight_grad(away, start_full, grads, quads=quads)
        grads, cross_part = tie(grads, cross_part)
        cross = plan.sibling(cross_part)
        keep = weight_grad(core, start_full, grads, quads=quads)
        return Sum(plan, blocks(cross), where), Sum(plan, blocks(keep), where)

    def settle(items, other):
        for item in items:
            item.got, other = tie(item.got, other)
            item.add()
            item.terms, other = tie(item.terms, other)
        return other

    grads, b_sum0 = back(0, quads // 2)
    got = away_rows(grads)
    output_got, grads = tie(output_got, grads)
    grads = settle([down, up, out], grads)
    down.send("y")
    up.send("x")
    out.send("y")
    cross0, keep0 = products(grads)
    got, cross0.terms, keep0.terms = tie(got, cross0.terms, keep0.terms)
    (grad_start,) = add_start(core, grad_one, grads, got, w_cut[0], w_cut_oth[0], False)
    keep0.send("x")
    cross0.send("y")
    grad_context, grad_start = tie(grad_context, grad_start)
    grads, b_sum1 = back(quads // 2, quads // 4)
    grads = settle([down, up], grads)
    down.send("z")
    up.send("z")
    grads, b_sum2 = back(quads // 2 + quads // 4, quads // 4, grads)
    got = away_rows(grads)
    cross1, keep1 = products(grads)
    got, keep1.terms = tie(got, keep1.terms)
    grad_low, b_time_sum = add_start(core, grad_start, grads, got, w_cut[1], w_cut_oth[1], True)
    in_parts, b_time_sum = tie(spread_parts(grad_low), b_time_sum)
    grad_inputs_got = exchange(in_parts)
    keep1.send("x")
    cross1.send("y")
    for item in (out, keep0, cross0, keep1, cross1, down, up):
        item.got, b_time_sum = tie(item.got, b_time_sum)
    out.add()
    keep0.add()
    cross0.add()
    keep0.send("y")
    cross0.send("x")
    keep1.add()
    cross1.add()
    keep1.send("y")
    cross1.send("x")
    for item in (keep0, cross0, keep1, cross1):
        item.add()
    late = Sum(
        plan,
        jnp.concatenate([i.terms for i in (keep0, cross0, keep1, cross1, out)], axis=2),
        where,
    ).send("z")
    small_sums, up_sums, b_time_sum = tie(small_sums, up_sums, b_time_sum)
    b_sum = jnp.concatenate([b_sum0, b_sum1, b_sum2], axis=1)
    zero = jnp.zeros((quads, 2, half // quads), F32)

    def placed(v):
        return lax.dynamic_update_index_in_dim(zero, v.reshape(quads, half // quads), c, 1).reshape(-1)

    vectors = [small_sums[i] for i in range(6)]
    vectors += [placed(b_sum[0]), placed(b_sum[1]), fraction * b_time_sum[0], b_time_sum[0]]
    small = jnp.concatenate([v[:, None] for v in vectors] + [up_sums.reshape(model, -1)], axis=1)
    small_own, small_oth = halves(small, 0)
    small = Sum(plan, blocks(small_own + plan.sibling(small_oth)), where)
    for axis in "xyz":
        small.send(axis).add()
    small = small.terms
    late = late.add()
    wide = 3 * half // 2
    keeps = [late[:, :wide], late[:, 2 * wide : 3 * wide]]
    crosses = [late[:, wide : 2 * wide], late[:, 3 * wide : 4 * wide]]
    sum_w_down, sum_w_up, sum_w_out = down.add(), up.add(), late[:, 4 * wide :]
    output = spread_end(output_got)
    grad_inputs = spread_end(grad_inputs_got)
    split3 = lambda parts: jnp.concatenate(
        [p.reshape(p.shape[0], 3, len(g), -1) for p, g in zip(parts, groups)], axis=2
    )
    sum_own, sum_oth = split3(keeps), split3(crosses)
    pair = jnp.where(c == 0, jnp.stack([sum_own, sum_oth]), jnp.stack([sum_oth, sum_own]))
    sum_w_qkv = (
        pair.transpose(1, 2, 3, 0, 4).reshape(-1, 3 * model)
    )
    v = [small[:, i] for i in (6, 7, 0, 1, 2, 3, 4, 5, 8, 9)]
    return (
        output,
        grad_inputs,
        sum_w_qkv,
        v[0],
        v[1],
        sum_w_out,
        v[2],
        v[3],
        v[4],
        sum_w_up,
        small[:, 10:].reshape(-1),
        sum_w_down,
        v[5],
        v[6],
        v[7],
        v[8],
        v[9],
    )


def solution(mesh):
    placed = (
        P("batch", "seq", None),
        P("batch"),
        P("batch", None),
        P("batch", "seq", None),
        P(),
        P(),
        P(),
        P(),
        P(),
        P(),
        P(),
        P(),
        P(),
        P(),
        P(),
        P(),
        P(),
        P(),
        P(),
    )
    sizes = dict(mesh.shape)
    body = per_device
    if sizes["seq"] == 4 and sizes["batch"] % 2 == 0:
        body = functools.partial(per_chip, Plan(mesh))
    return jax.shard_map(
        body,
        mesh=mesh,
        in_specs=placed,
        out_specs=(
            P("batch", "seq", None),
            P("batch", "seq", None),
            P(("batch", "seq"), None),
            P(("batch", "seq")),
            P(("batch", "seq")),
            P(("batch", "seq"), None),
            P(("batch", "seq")),
            P(("batch", "seq")),
            P(("batch", "seq")),
            P(("batch", "seq"), None),
            P(("batch", "seq")),
            P(("batch", "seq"), None),
            P(("batch", "seq")),
            P(("batch", "seq")),
            P(("batch", "seq")),
            P(("batch", "seq")),
            P(("batch", "seq")),
        ),
        check_vma=False,
    )
```

```python
import functools

import jax
import jax.numpy as jnp
from jax import lax
from jax.experimental import pallas as pl
from jax.experimental.pallas import tpu as pltpu
from jax.sharding import PartitionSpec as P

D = 1024
HEADS = 16
TSTEPS = 5000
AXES = ("batch", "seq")


BF=jnp.bfloat16; F32=jnp.float32
NT=(((1,),(1,)),((),())); NN=(((1,),(0,)),((),())); TN=(((0,),(0,)),((),()))
def dot(a,b,d): return lax.dot_general(a,b,d,preferred_element_type=F32)
PHASE=1
FILLED=1664; PAD=64
def lanes(rows):
    return lax.broadcasted_iota(jnp.int32,(rows,128),1)
def parts3(x):
    a=x.astype(BF).astype(F32); r=x-a; b=r.astype(BF).astype(F32); c=r-b
    return a,b,c
def augment(base,h,x,lane):
    a,b,c=parts3(x)
    o=(1-h)*64
    f=base.astype(F32)
    f=jnp.where((lane>=o)&(lane<o+64),jnp.where(lane==o,a,jnp.where(lane==o+1,b,jnp.where(lane==o+2,c,0.0))),f)
    return f.astype(BF)
def ones3(base,h,lane,n=3):
    o=(1-h)*64
    f=base.astype(F32)
    f=jnp.where((lane>=o)&(lane<o+64),jnp.where(lane<o+n,1.0,0.0),f)
    return f.astype(BF)
def spread(base,h,x,lane):
    a=x.astype(BF).astype(F32); r=x-a; b=r.astype(BF).astype(F32); c=r-b
    o=(1-h)*64
    f=jnp.where(lane==o,a,jnp.where(lane==o+1,b,jnp.where(lane==o+2,c,0.0)))
    return jnp.where((lane//64)==h,base.astype(F32),f).astype(BF)
def fwd_tiles(tasks,lane):
    scores=[]
    for q,k,vs,keep in tasks:
        for h in (0,1):
            qh=jnp.where((lane//64)==h,q.astype(F32),0.0).astype(BF)
            s=dot(qh,k,NT)
            scores.append(s if keep is None else jnp.where(keep,s,-1e30))
    tops=[];outs=[]
    depth=PHASE
    n=len(scores)
    def soft(i):
        m=jnp.max(scores[i],axis=1,keepdims=True)
        tops.append(m)
        return jnp.exp2(scores[i]-m).astype(BF)
    ps=[]
    for i in range(n+depth):
        if i<n: ps.append(soft(i))
        if i>=depth: outs.append(dot(ps[i-depth],tasks[(i-depth)//2][2][(i-depth)%2],NN))
    done=[]
    for t,(q,_,_,_) in enumerate(tasks):
        os=[];augs=[]
        for h in (0,1):
            o=outs[2*t+h]
            os.append(o/pltpu.roll(o,64,1))
            augs.append(spread(q,h,-(tops[2*t+h]+jnp.log2(o)),lane))
        done.append((jnp.where(lane<64,os[0],os[1]),augs))
    return done
def fwd_store(refs,rows,o,augs):
    o_ref,ol_ref,qa_ref=refs
    o_ref[rows,:]=o.astype(BF)
    ol_ref[rows,:]=(o-o.astype(BF).astype(F32)).astype(BF)
    for h in (0,1): qa_ref[h,rows,:]=augs[h]
def fwd_kernel(bq,info,q_ref,k_ref,v_ref,*refs):
    *refs,vs_ref=refs
    single=info[0]==1
    @pl.when(single)
    def _():
        v=v_ref[0:FILLED,:]
        for h in (0,1): vs_ref[h,...]=ones3(v,h,lanes(FILLED),64)
        lq=lanes(bq)
        @pl.loop(0,FILLED//bq)
        def _(r):
            rows=pl.ds(pl.multiple_of(r*bq,bq),bq)
            (o,augs),=fwd_tiles([(q_ref[rows,:],k_ref[0:FILLED,:],(vs_ref[0],vs_ref[1]),None)],lq)
            fwd_store(refs,rows,o,augs)
    @pl.when(info[0]==2)
    def _():
        lq=lanes(128)
        each=[slice(i*128,i*128+128) for i in range(13)]
        tasks=[(q_ref[r,:],k_ref[r,:],[ones3(v_ref[r,:],h,lq,64) for h in (0,1)],None) for r in each]
        for r,(o,augs) in zip(each,fwd_tiles(tasks,lq)): fwd_store(refs,r,o,augs)
    @pl.when(info[0]==0)
    def _():
        col=lax.broadcasted_iota(jnp.int32,(128,512),1)
        lw=lanes(512); lq=lanes(128)
        @pl.loop(0,13)
        def _(i):
            lo=info[1+i]; hi=info[14+i]
            at=jnp.minimum(lo,9)
            window=pl.ds(pl.multiple_of(at*128,128),512)
            k=k_ref[window,:]; v=v_ref[window,:]
            vs=[ones3(v,h,lw,64) for h in (0,1)]
            keep=(col>=(lo-at)*128)&(col<(hi-at)*128)
            rows=pl.ds(pl.multiple_of(i*128,128),128)
            (o,augs),=fwd_tiles([(q_ref[rows,:],k,vs,keep)],lq)
            fwd_store(refs,rows,o,augs)
    rows=slice(FILLED,FILLED+PAD)
    lp=lanes(PAD)
    v=v_ref[rows,:]
    (o,augs),=fwd_tiles([(q_ref[rows,:],k_ref[rows,:],[ones3(v,h,lp,64) for h in (0,1)],None)],lp)
    fwd_store(refs,rows,o,augs)
def attn_fwd(info,qkv,first,count,bq=416):
    L,W3=qkv.shape; n=W3//384
    spec=lambda j: pl.BlockSpec((L,128),lambda p,s,j=j:(0,p+first+j*n))
    one=pl.BlockSpec((L,128),lambda p,s:(0,p))
    return pl.pallas_call(functools.partial(fwd_kernel,bq),
        out_shape=(jax.ShapeDtypeStruct((L,count*128),BF),)*2+(jax.ShapeDtypeStruct((2*count,L,128),BF),),
        grid_spec=pltpu.PrefetchScalarGridSpec(num_scalar_prefetch=1,grid=(count,),
            in_specs=[spec(0),spec(1),spec(2)],
            out_specs=(one,one,pl.BlockSpec((2,L,128),lambda p,s:(p,0,0))),
            scratch_shapes=[pltpu.VMEM((2,FILLED,128),BF)]),
        compiler_params=pltpu.CompilerParams(vmem_limit_bytes=50<<20),name="attn_forward",
        cost_estimate=pl.CostEstimate(flops=8*count*L*L*256,bytes_accessed=10*L*count*128,transcendentals=2*count*L*L))(info,qkv,qkv,qkv)
def deltas(g,o,ol,lane):
    prod=g.astype(F32)*(o.astype(F32)+ol.astype(F32))
    return [augment(g,h,-jnp.sum(jnp.where((lane//64)==h,prod,0.0),axis=1,keepdims=True),lane) for h in (0,1)]
def bwd_tiles(tasks,lane):
    khs=[ones3(t[1],t[4],lane) for t in tasks]
    ps=[dot(kh,t[0],NT) for kh,t in zip(khs,tasks)]
    ds=[dot(ones3(t[2],t[4],lane),t[3],NT) for t in tasks]
    done=[]
    for kh,p,d,(qa,_,_,ga,h,keep) in zip(khs,ps,ds,tasks):
        p=jnp.exp2(p)
        if keep is not None: p=jnp.where(keep,p,0.0)
        d=(p*d).astype(BF)
        done.append((kh,p.astype(BF),d,qa,ga))
    return [(dot(d,kh,TN),dot(d,qa,NN),dot(p,ga,NN)) for kh,p,d,qa,ga in done]
LN2=0.6931471805599453
def both(a,lane): return jnp.where(lane<64,a[0],a[1])
def bwd_alone(each,lane,qa_ref,k_ref,v_ref,o_ref,ol_ref,g_ref,dq_ref,dk_ref,dv_ref):
    tasks=[]
    for r in each:
        gas=deltas(g_ref[r,:],o_ref[r,:],ol_ref[r,:],lane)
        tasks+=[(qa_ref[h,r,:],k_ref[r,:],v_ref[r,:],gas[h],h,None) for h in (0,1)]
    got=bwd_tiles(tasks,lane)
    for i,r in enumerate(each):
        x,y=got[2*i],got[2*i+1]
        dq_ref[r,:]=(both((x[0],y[0]),lane)*0.125).astype(BF)
        dk_ref[r,:]=(both((x[1],y[1]),lane)*LN2).astype(BF)
        dv_ref[r,:]=both((x[2],y[2]),lane).astype(BF)
def bwd_kernel(bk,joined,info,qa_ref,k_ref,v_ref,o_ref,ol_ref,g_ref,*rest):
    d_ref,sum_ref,acc,acc_k,acc_v,ga_ref=rest[1:] if joined else rest
    dq_ref,dk_ref,dv_ref=d_ref.at[0],d_ref.at[1],d_ref.at[2]
    tile_refs=(qa_ref,k_ref,v_ref,o_ref,ol_ref,g_ref,dq_ref,dk_ref,dv_ref)
    single=info[0]==1
    @pl.when(single)
    def _():
        lf=lanes(FILLED)
        gas=deltas(g_ref[0:FILLED,:],o_ref[0:FILLED,:],ol_ref[0:FILLED,:],lf)
        acc[...]=jnp.zeros_like(acc)
        lb=lanes(bk)
        ga_ref[0,...]=gas[0]; ga_ref[1,...]=gas[1]
        @pl.loop(0,FILLED//bk)
        def _(r):
            rows=pl.ds(pl.multiple_of(r*bk,bk),bk)
            k=k_ref[rows,:]; v=v_ref[rows,:]
            dks=[];dvs=[]
            got=bwd_tiles([(qa_ref[h,0:FILLED,:],k,v,ga_ref[h],h,None) for h in (0,1)],lb)
            for h in (0,1):
                dq,dk,dv=got[h]
                acc[h,0:FILLED,:]+=dq
                dks.append(dk); dvs.append(dv)
            dk_ref[rows,:]=(both(dks,lb)*LN2).astype(BF)
            dv_ref[rows,:]=both(dvs,lb).astype(BF)
        dq_ref[0:FILLED,:]=(jnp.where(lf<64,acc[0,0:FILLED,:],acc[1,0:FILLED,:])*0.125).astype(BF)
    @pl.when(info[0]==2)
    def _():
        lq=lanes(128)
        bwd_alone([slice(i*128,i*128+128) for i in range(13)],lq,*tile_refs)
    @pl.when(info[0]==0)
    def _():
        row=lax.broadcasted_iota(jnp.int32,(512,128),0)
        lw=lanes(512); lq=lanes(128)
        acc_k[...]=jnp.zeros_like(acc_k); acc_v[...]=jnp.zeros_like(acc_v)
        @pl.loop(0,13)
        def _(i):
            lo=info[1+i]; hi=info[14+i]
            at=jnp.minimum(lo,9)
            window=pl.ds(pl.multiple_of(at*128,128),512)
            k=k_ref[window,:]; v=v_ref[window,:]
            keep=(row>=(lo-at)*128)&(row<(hi-at)*128)
            rows=pl.ds(pl.multiple_of(i*128,128),128)
            gas=deltas(g_ref[rows,:],o_ref[rows,:],ol_ref[rows,:],lq)
            dqs=[]
            got=bwd_tiles([(qa_ref[h,rows,:],k,v,gas[h],h,keep) for h in (0,1)],lw)
            for h in (0,1):
                dq,dk,dv=got[h]
                dqs.append(dq)
                acc_k[h,window,:]+=dk
                acc_v[h,window,:]+=dv
            dq_ref[rows,:]=(both(dqs,lq)*0.125).astype(BF)
        lf=lanes(FILLED)
        dk_ref[0:FILLED,:]=(jnp.where(lf<64,acc_k[0],acc_k[1])*LN2).astype(BF)
        dv_ref[0:FILLED,:]=jnp.where(lf<64,acc_v[0],acc_v[1]).astype(BF)
    bwd_alone([slice(FILLED,FILLED+PAD)],lanes(PAD),*tile_refs)
    sum_ref[0:1,:]=jnp.sum(dq_ref[...].astype(F32),axis=0,keepdims=True)
    sum_ref[1:2,:]=jnp.sum(dv_ref[...].astype(F32),axis=0,keepdims=True)
def attn_bwd(info,qa,qkv,o,ol,g,first,count,inner,wide,at,into=None,bk=416):
    L,W3=qkv.shape; n=W3//384
    spec=lambda j: pl.BlockSpec((L,128),lambda p,s,j=j:(0,p+first+j*n))
    one=pl.BlockSpec((L,128),lambda p,s:(0,p))
    part=pl.BlockSpec((L,128),lambda p,s:(0,p+inner))
    every=pl.BlockSpec((L,128),lambda p,s:(0,p+first))
    return pl.pallas_call(functools.partial(bwd_kernel,bk,into is not None),
        input_output_aliases={} if into is None else {7:0},
        out_shape=(jax.ShapeDtypeStruct((3,L,wide*128),BF),jax.ShapeDtypeStruct((2,count*128),F32)),
        grid_spec=pltpu.PrefetchScalarGridSpec(num_scalar_prefetch=1,grid=(count,),
            in_specs=[pl.BlockSpec((2,L,128),lambda p,s:(p+inner,0,0)),spec(1),spec(2),part,part,every]+([] if into is None else [pl.BlockSpec(memory_space=pl.ANY)]),
            out_specs=(pl.BlockSpec((3,L,128),lambda p,s:(0,0,p+at)),pl.BlockSpec((2,128),lambda p,s:(0,p))),
            scratch_shapes=[pltpu.VMEM((2,FILLED,128),F32)]*3+[pltpu.VMEM((2,FILLED,128),BF)]),
        compiler_params=pltpu.CompilerParams(vmem_limit_bytes=56<<20),name="attn_backward",
        cost_estimate=pl.CostEstimate(flops=20*count*L*L*256,bytes_accessed=16*L*count*128,transcendentals=2*count*L*L))(*((info,qa,qkv,qkv,o,ol,g) if into is None else (info,qa,qkv,qkv,o,ol,g,into)))


def gelu_exact(values):
    return jax.nn.gelu(values, approximate=False)


def norm_forward(values, gain, shift):
    centered = values - jnp.mean(values, axis=-1, keepdims=True)
    inverse = lax.rsqrt(jnp.mean(centered * centered, axis=-1, keepdims=True) + 1e-05)
    unit_part = centered * inverse
    return (unit_part * gain + shift, unit_part, inverse)


def norm_backward(grad_out, unit_part, inverse, gain):
    scaled = grad_out * gain
    centered = scaled - jnp.mean(scaled, axis=-1, keepdims=True)
    grad_in = inverse * (
        centered - unit_part * jnp.mean(scaled * unit_part, axis=-1, keepdims=True)
    )
    return (grad_in, jnp.sum(grad_out * unit_part, axis=0), jnp.sum(grad_out, axis=0))


def attention_forward(query_all, key_all, value_all, segments, head_dim):
    length, local_width = (query_all.shape[1], query_all.shape[2])
    head_count = local_width // head_dim
    block_len = length // 3
    score_scale = head_dim ** (-0.5)

    def per_sequence(pieces):
        queries, key_rows, value_rows, seq_ids = pieces
        key_heads = key_rows.reshape(length, head_count, head_dim)
        value_heads = value_rows.reshape(length, head_count, head_dim)

        def per_block(block_pieces):
            query_part, id_part = block_pieces
            query_heads = query_part.reshape(block_len, head_count, head_dim)
            scores = (
                jnp.einsum(
                    "qhd,khd->hqk", query_heads, key_heads, preferred_element_type=jnp.float32
                )
                * score_scale
            )
            masked = jnp.where(id_part[None, :, None] == seq_ids[None, None, :], scores, -1e30)
            maxima = jnp.max(masked, axis=-1, keepdims=True)
            exp_scores = jnp.exp(masked - maxima)
            totals = jnp.sum(exp_scores, axis=-1, keepdims=True)
            weights_low = (exp_scores / totals).astype(jnp.bfloat16)
            context = jnp.einsum(
                "hqk,khd->qhd", weights_low, value_heads, preferred_element_type=jnp.float32
            )
            return (
                context.astype(jnp.bfloat16).reshape(block_len, local_width),
                (maxima + jnp.log(totals))[..., 0],
            )

        contexts, logsums = lax.map(
            per_block, (queries.reshape(3, block_len, local_width), seq_ids.reshape(3, block_len))
        )
        return (contexts.reshape(length, local_width), logsums)

    return lax.map(per_sequence, (query_all, key_all, value_all, segments))


def attention_backward(query_all, key_all, value_all, segments, logsums, grad_all, head_dim):
    length, local_width = (query_all.shape[1], query_all.shape[2])
    head_count = local_width // head_dim
    block_len = length // 3
    score_scale = head_dim ** (-0.5)

    def per_sequence(pieces):
        queries, key_rows, value_rows, seq_ids, sum_rows, grad_rows = pieces
        key_heads = key_rows.reshape(length, head_count, head_dim)
        value_heads = value_rows.reshape(length, head_count, head_dim)

        def per_block(carry, block_pieces):
            key_total, value_total = carry
            query_part, id_part, sum_part, grad_part = block_pieces
            query_heads = query_part.reshape(block_len, head_count, head_dim)
            grad_heads = grad_part.reshape(block_len, head_count, head_dim)
            scores = (
                jnp.einsum(
                    "qhd,khd->hqk", query_heads, key_heads, preferred_element_type=jnp.float32
                )
                * score_scale
            )
            allowed = id_part[None, :, None] == seq_ids[None, None, :]
            prob_weights = jnp.where(allowed, jnp.exp(scores - sum_part[:, :, None]), 0.0)
            grad_probs = jnp.einsum(
                "qhd,khd->hqk", grad_heads, value_heads, preferred_element_type=jnp.float32
            )
            delta = jnp.sum(prob_weights * grad_probs, axis=-1, keepdims=True)
            grad_scores = (prob_weights * (grad_probs - delta)).astype(jnp.bfloat16)
            query_grad = (
                jnp.einsum(
                    "hqk,khd->qhd", grad_scores, key_heads, preferred_element_type=jnp.float32
                )
                * score_scale
            )
            key_total = (
                key_total
                + jnp.einsum(
                    "hqk,qhd->khd", grad_scores, query_heads, preferred_element_type=jnp.float32
                )
                * score_scale
            )
            value_total = value_total + jnp.einsum(
                "hqk,qhd->khd",
                prob_weights.astype(jnp.bfloat16),
                grad_heads,
                preferred_element_type=jnp.float32,
            )
            return (
                (key_total, value_total),
                query_grad.astype(jnp.bfloat16).reshape(block_len, local_width),
            )

        zero_heads = jnp.zeros((length, head_count, head_dim), jnp.float32)
        (key_total, value_total), query_grads = lax.scan(
            per_block,
            (zero_heads, zero_heads),
            (
                queries.reshape(3, block_len, local_width),
                seq_ids.reshape(3, block_len),
                sum_rows,
                grad_rows.reshape(3, block_len, local_width),
            ),
        )
        return (
            query_grads.reshape(length, local_width),
            key_total.astype(jnp.bfloat16).reshape(length, local_width),
            value_total.astype(jnp.bfloat16).reshape(length, local_width),
        )

    return lax.map(per_sequence, (query_all, key_all, value_all, segments, logsums, grad_all))


def per_device(
    inputs,
    timesteps,
    segments,
    cotangent,
    w_qkv,
    b_query,
    b_value,
    w_out,
    b_out,
    ln1_gain,
    ln1_bias,
    w_up,
    b_up,
    w_down,
    b_down,
    ln2_gain,
    ln2_bias,
    w_time,
    b_time,
):
    groups, local_len, model_width = inputs.shape
    row_count = groups * local_len
    head_dim = D // HEADS
    fraction = timesteps.astype(jnp.float32) / TSTEPS
    start_sum = (
        inputs.astype(jnp.float32)
        + fraction[:, None, None] * w_time.astype(jnp.float32)
        + b_time.astype(jnp.float32)
    )
    start_low = start_sum.astype(jnp.bfloat16)
    projected = jnp.einsum("bld,de->ble", start_low, w_qkv, preferred_element_type=jnp.float32)
    query_low = (projected[..., :model_width] + b_query.astype(jnp.float32)).astype(jnp.bfloat16)
    key_low = projected[..., model_width : 2 * model_width].astype(jnp.bfloat16)
    value_low = (projected[..., 2 * model_width :] + b_value.astype(jnp.float32)).astype(
        jnp.bfloat16
    )
    query_all, key_all, value_all = (
        lax.all_to_all(query_low, "seq", split_axis=2, concat_axis=1, tiled=True),
        lax.all_to_all(key_low, "seq", split_axis=2, concat_axis=1, tiled=True),
        lax.all_to_all(value_low, "seq", split_axis=2, concat_axis=1, tiled=True),
    )
    context_heads, logsums = attention_forward(query_all, key_all, value_all, segments, head_dim)
    context = lax.all_to_all(context_heads, "seq", split_axis=1, concat_axis=2, tiled=True)
    context_rows = context.reshape(row_count, model_width)
    start_rows = start_sum.reshape(row_count, model_width)
    residual_one = (
        start_rows
        + jnp.dot(context_rows, w_out, preferred_element_type=jnp.float32)
        + b_out.astype(jnp.float32)
    )
    normed, unit_one, inverse_one = norm_forward(
        residual_one, ln1_gain.astype(jnp.float32), ln1_bias.astype(jnp.float32)
    )
    normed_low = normed.astype(jnp.bfloat16)
    hidden_pre = jnp.dot(normed_low, w_up, preferred_element_type=jnp.float32) + b_up.astype(
        jnp.float32
    )
    activated, gelu_pull = jax.vjp(gelu_exact, hidden_pre)
    activated_low = activated.astype(jnp.bfloat16)
    residual_two = (
        normed
        + jnp.dot(activated_low, w_down, preferred_element_type=jnp.float32)
        + b_down.astype(jnp.float32)
    )
    result, unit_two, inverse_two = norm_forward(
        residual_two, ln2_gain.astype(jnp.float32), ln2_bias.astype(jnp.float32)
    )
    output = result.astype(jnp.bfloat16).reshape(groups, local_len, model_width)
    grad_result = cotangent.reshape(row_count, model_width).astype(jnp.float32)
    grad_two, grad_ln2_gain, grad_ln2_bias = norm_backward(
        grad_result, unit_two, inverse_two, ln2_gain.astype(jnp.float32)
    )
    grad_b_down = jnp.sum(grad_two, axis=0)
    grad_two_low = grad_two.astype(jnp.bfloat16)
    grad_w_down = jnp.einsum(
        "rf,rd->fd", activated_low, grad_two_low, preferred_element_type=jnp.float32
    )
    grad_activated = jnp.einsum(
        "rd,fd->rf", grad_two_low, w_down, preferred_element_type=jnp.float32
    )
    grad_hidden = gelu_pull(grad_activated)[0]
    grad_b_up = jnp.sum(grad_hidden, axis=0)
    grad_hidden_low = grad_hidden.astype(jnp.bfloat16)
    grad_w_up = jnp.einsum(
        "rd,rf->df", normed_low, grad_hidden_low, preferred_element_type=jnp.float32
    )
    grad_normed = grad_two + jnp.einsum(
        "rf,df->rd", grad_hidden_low, w_up, preferred_element_type=jnp.float32
    )
    grad_one, grad_ln1_gain, grad_ln1_bias = norm_backward(
        grad_normed, unit_one, inverse_one, ln1_gain.astype(jnp.float32)
    )
    grad_b_out = jnp.sum(grad_one, axis=0)
    grad_one_low = grad_one.astype(jnp.bfloat16)
    grad_w_out = jnp.einsum(
        "rd,re->de", context_rows, grad_one_low, preferred_element_type=jnp.float32
    )
    grad_context = (
        jnp.einsum("re,de->rd", grad_one_low, w_out, preferred_element_type=jnp.float32)
        .astype(jnp.bfloat16)
        .reshape(groups, local_len, model_width)
    )
    grad_context_heads = lax.all_to_all(
        grad_context, "seq", split_axis=2, concat_axis=1, tiled=True
    )
    query_grads, key_grads, value_grads = attention_backward(
        query_all, key_all, value_all, segments, logsums, grad_context_heads, head_dim
    )
    grad_query, grad_key, grad_value = (
        lax.all_to_all(query_grads, "seq", split_axis=1, concat_axis=2, tiled=True),
        lax.all_to_all(key_grads, "seq", split_axis=1, concat_axis=2, tiled=True),
        lax.all_to_all(value_grads, "seq", split_axis=1, concat_axis=2, tiled=True),
    )
    grad_projected = jnp.concatenate((grad_query, grad_key, grad_value), axis=2).reshape(
        row_count, 3 * model_width
    )
    grad_w_qkv = jnp.einsum(
        "rd,re->de",
        start_low.reshape(row_count, model_width),
        grad_projected,
        preferred_element_type=jnp.float32,
    )
    grad_b_query = jnp.sum(grad_query.astype(jnp.float32), axis=(0, 1))
    grad_b_value = jnp.sum(grad_value.astype(jnp.float32), axis=(0, 1))
    grad_start = grad_one + jnp.einsum(
        "re,de->rd", grad_projected, w_qkv, preferred_element_type=jnp.float32
    )
    grad_inputs = grad_start.astype(jnp.bfloat16).reshape(groups, local_len, model_width)
    per_sequence_grad = jnp.sum(grad_start.reshape(groups, local_len, model_width), axis=1)
    grad_w_time = jnp.einsum("g,gd->d", fraction, per_sequence_grad)
    grad_b_time = jnp.sum(per_sequence_grad, axis=0)
    (
        sum_w_qkv,
        sum_b_query,
        sum_b_value,
        sum_w_out,
        sum_b_out,
        sum_ln1_gain,
        sum_ln1_bias,
        sum_w_up,
        sum_b_up,
        sum_w_down,
        sum_b_down,
        sum_ln2_gain,
        sum_ln2_bias,
        sum_w_time,
        sum_b_time,
    ) = (
        lax.psum_scatter(grad_w_qkv, ("batch", "seq"), scatter_dimension=0, tiled=True),
        lax.psum_scatter(grad_b_query, ("batch", "seq"), scatter_dimension=0, tiled=True),
        lax.psum_scatter(grad_b_value, ("batch", "seq"), scatter_dimension=0, tiled=True),
        lax.psum_scatter(grad_w_out, ("batch", "seq"), scatter_dimension=0, tiled=True),
        lax.psum_scatter(grad_b_out, ("batch", "seq"), scatter_dimension=0, tiled=True),
        lax.psum_scatter(grad_ln1_gain, ("batch", "seq"), scatter_dimension=0, tiled=True),
        lax.psum_scatter(grad_ln1_bias, ("batch", "seq"), scatter_dimension=0, tiled=True),
        lax.psum_scatter(grad_w_up, ("batch", "seq"), scatter_dimension=0, tiled=True),
        lax.psum_scatter(grad_b_up, ("batch", "seq"), scatter_dimension=0, tiled=True),
        lax.psum_scatter(grad_w_down, ("batch", "seq"), scatter_dimension=0, tiled=True),
        lax.psum_scatter(grad_b_down, ("batch", "seq"), scatter_dimension=0, tiled=True),
        lax.psum_scatter(grad_ln2_gain, ("batch", "seq"), scatter_dimension=0, tiled=True),
        lax.psum_scatter(grad_ln2_bias, ("batch", "seq"), scatter_dimension=0, tiled=True),
        lax.psum_scatter(grad_w_time, ("batch", "seq"), scatter_dimension=0, tiled=True),
        lax.psum_scatter(grad_b_time, ("batch", "seq"), scatter_dimension=0, tiled=True),
    )
    return (
        output,
        grad_inputs,
        sum_w_qkv,
        sum_b_query,
        sum_b_value,
        sum_w_out,
        sum_b_out,
        sum_ln1_gain,
        sum_ln1_bias,
        sum_w_up,
        sum_b_up,
        sum_w_down,
        sum_b_down,
        sum_ln2_gain,
        sum_ln2_bias,
        sum_w_time,
        sum_b_time,
    )


SLOPE = F32
LOG2E = 1.4426950408889634


def layer_norm(values):
    centered = values - jnp.mean(values, axis=1, keepdims=True)
    inverse = lax.rsqrt(jnp.mean(centered * centered, axis=1, keepdims=True) + 1e-05)
    return centered * inverse, inverse


def layer_norm_back(scaled, unit_part, inverse):
    return inverse * (
        scaled
        - jnp.mean(scaled, axis=1, keepdims=True)
        - unit_part * jnp.mean(scaled * unit_part, axis=1, keepdims=True)
    )


def gelu_pair(v):
    bell = jnp.exp2(v * v * (-0.5 * LOG2E))
    base = 1.0 + 0.2316418882663604 * jnp.abs(v)
    t = pltpu.reciprocal(base, approx=True)
    t = t * (2.0 - base * t)
    tail = t * (
        0.127414796
        + t * (-0.142248368 + t * (0.7107068705 + t * (-0.7265760135 + t * 0.5307027145)))
    )
    tail = tail * bell
    cover = jnp.where(v >= 0, 1.0 - tail, tail)
    return v * cover, cover + v * bell * 0.3989422804014327


def middle_kernel(
    fc,
    sel_ref,
    frac_ref,
    inp_ref,
    ctx_a0_ref,
    ctx_a1_ref,
    ctx_b0_ref,
    ctx_b1_ref,
    cot_ref,
    vec_ref,
    b_up_ref,
    wo_a_ref,
    wo_b_ref,
    w_up_hbm,
    w_down_hbm,
    out_ref,
    norm_ref,
    act_ref,
    two_ref,
    hid_ref,
    one_ref,
    onel_ref,
    small_ref,
    smallup_ref,
    w_up,
    w_down,
    slope,
    sems,
):
    step = pl.program_id(0)
    up_copy = pltpu.make_async_copy(w_up_hbm, w_up, sems.at[0])
    down_copy = pltpu.make_async_copy(w_down_hbm, w_down, sems.at[1])

    @pl.when(step == 0)
    def _():
        up_copy.start()
        down_copy.start()
        small_ref[...] = jnp.zeros_like(small_ref)
        smallup_ref[...] = jnp.zeros_like(smallup_ref)

    vec = lambda i: vec_ref[i : i + 1, :]
    start = inp_ref[...].astype(F32) + (frac_ref[0] * vec(0) + vec(1))
    residual = (
        start
        + dot(jnp.concatenate([ctx_a0_ref[...], ctx_a1_ref[...]], axis=1), wo_a_ref[...].reshape(-1, wo_a_ref.shape[-1]), NN)
        + dot(jnp.concatenate([ctx_b0_ref[...], ctx_b1_ref[...]], axis=1), wo_b_ref[...].reshape(-1, wo_b_ref.shape[-1]), NN)
        + vec(2)
    )
    unit_one, inverse_one = layer_norm(residual)
    normed = unit_one * vec(3) + vec(4)
    low = normed.astype(BF)
    norm_ref[...] = low

    @pl.when(step == 0)
    def _():
        up_copy.wait()
        down_copy.wait()

    width = w_up.shape[1]
    total = normed + vec(5)
    for f in range(0, width, fc):
        cols = slice(f, f + fc)
        v = dot(low, w_up[:, cols], NN) + b_up_ref[:, cols]
        a, g = gelu_pair(v)
        a = a.astype(BF)
        act_ref[:, cols] = a
        slope[:, cols] = g.astype(slope.dtype)
        total = total + dot(a, w_down[cols, :], NN)
    unit_two, inverse_two = layer_norm(total)
    out_ref[...] = (unit_two * vec(6) + vec(7)).astype(BF)
    cot = cot_ref[...].astype(F32)
    two = layer_norm_back(cot * vec(6), unit_two, inverse_two)
    add = lambda v: jnp.sum(v, axis=0, keepdims=True)
    small_ref[3:4, :] += add(two)
    small_ref[4:5, :] += add(cot * unit_two)
    small_ref[5:6, :] += add(cot)
    two_low = two.astype(BF)
    two_ref[...] = two_low
    total = two
    for f in range(0, width, fc):
        cols = slice(f, f + fc)
        d = dot(two_low, w_down[cols, :], NT) * slope[:, cols].astype(F32)
        smallup_ref[:, cols] += add(d)
        d = d.astype(BF)
        hid_ref[:, cols] = d
        total = total + dot(d, w_up[:, cols], NT)
    small_ref[1:2, :] += add(total * unit_one)
    small_ref[2:3, :] += add(total)
    one = layer_norm_back(total * vec(3), unit_one, inverse_one)
    small_ref[0:1, :] += add(one)
    one_ref[...] = one
    onel_ref[...] = one.astype(BF)


def middle(core, fraction, inp, ctx_a, ctx_b, cot, vecs, b_up, w_out, w_up, w_down, br=288, fc=2048):
    rows, model = inp.shape
    width = w_up.shape[1]
    half = model // 2
    quads = w_out.shape[0]
    row = lambda w: pl.BlockSpec((br, w), lambda i, s: (i, 0))
    fixed = lambda shape: pl.BlockSpec(shape, lambda i, s: (0,) * len(shape))
    here = pl.BlockSpec((br, half // 2), lambda i, s: (s[0] * (rows // br) + i, 0))
    wo = lambda flip: pl.BlockSpec(
        (quads, 1, model // quads // 2, model),
        (lambda i, s: (0, s[0], 0, 0)) if not flip else (lambda i, s: (0, 1 - s[0], 0, 0)),
    )
    out = lambda w, t: jax.ShapeDtypeStruct((rows, w), t)
    return pl.pallas_call(
        functools.partial(middle_kernel, fc),
        out_shape=(
            out(model, BF),
            out(model, BF),
            out(width, BF),
            out(model, BF),
            out(width, BF),
            out(model, F32),
            out(model, BF),
            jax.ShapeDtypeStruct((8, model), F32),
            jax.ShapeDtypeStruct((1, width), F32),
        ),
        grid_spec=pltpu.PrefetchScalarGridSpec(
            num_scalar_prefetch=1,
            grid=(rows // br,),
            in_specs=[
                pl.BlockSpec(memory_space=pltpu.SMEM),
                row(model),
                here,
                here,
                row(half // 2),
                row(half // 2),
                row(model),
                fixed((8, model)),
                fixed((1, width)),
                wo(False),
                wo(True),
                pl.BlockSpec(memory_space=pl.ANY),
                pl.BlockSpec(memory_space=pl.ANY),
            ],
            out_specs=(
                row(model),
                row(model),
                row(width),
                row(model),
                row(width),
                row(model),
                row(model),
                fixed((8, model)),
                fixed((1, width)),
            ),
            scratch_shapes=[
                pltpu.VMEM(w_up.shape, BF),
                pltpu.VMEM(w_down.shape, BF),
                pltpu.VMEM((br, width), SLOPE),
                pltpu.SemaphoreType.DMA((2,)),
            ],
        ),
        compiler_params=pltpu.CompilerParams(vmem_limit_bytes=60 << 20),
        cost_estimate=pl.CostEstimate(
            flops=4 * rows * model * (model // 2 + 2 * width),
            bytes_accessed=4 * model * width + rows * (16 * model + 4 * width),
            transcendentals=rows * width * 2,
        ),
        name="middle",
    )(core, fraction, inp, *ctx_a, *ctx_b, cot, vecs, b_up, w_out, w_out, w_up, w_down)


def grad_kernel(count, extra, *refs):
    lhs = [r[...] for r in refs[1 : 1 + count]]
    rhs_ref = refs[1 + count]
    out_ref = refs[-1]
    left = lhs[0] if count == 1 else jnp.concatenate(lhs, axis=1)
    right = rhs_ref[0] if len(rhs_ref.shape) == 3 else rhs_ref[...]
    total = dot(left, right, TN)
    if extra:
        total = total + refs[2 + count][...].astype(F32)
    out_ref[...] = total.astype(BF)


def weight_grad(sel, lhs, rhs, add=None, cols=1024, quads=4, pairs=2):
    depth, width = lhs.shape
    three = rhs.ndim == 3
    n = rhs.shape[0] * rhs.shape[2] if three else rhs.shape[1]
    cols = rhs.shape[2] if three else cols
    w = width // (quads * pairs)
    extra = add is not None
    if w >= 512:
        grid, count = (quads,), 1
        ins = [
            pl.BlockSpec((depth, w), lambda i, s: (0, pairs * i + s[0])),
            pl.BlockSpec((depth, n), lambda i, s: (0, 0)),
        ]
        out = pl.BlockSpec((w, n), lambda i, s: (i, 0))
        args = [lhs, rhs]
    else:
        grid, count = (n // cols,), quads
        ins = [
            pl.BlockSpec((depth, w), lambda i, s, q=q: (0, pairs * q + s[0])) for q in range(quads)
        ] + [
            pl.BlockSpec((1, depth, cols), lambda i, s: (i, 0, 0))
            if three
            else pl.BlockSpec((depth, cols), lambda i, s: (0, i))
        ]
        out = pl.BlockSpec((quads * w, cols), lambda i, s: (0, i))
        args = [lhs] * quads + [rhs]
    if extra:
        ins.append(out)
        args.append(add)
    total = quads * w
    return pl.pallas_call(
        functools.partial(grad_kernel, count, extra),
        out_shape=jax.ShapeDtypeStruct((total, n), BF),
        grid_spec=pltpu.PrefetchScalarGridSpec(
            num_scalar_prefetch=1, grid=grid, in_specs=ins, out_specs=out
        ),
        compiler_params=pltpu.CompilerParams(vmem_limit_bytes=48 << 20),
        cost_estimate=pl.CostEstimate(
            flops=2 * depth * total * n,
            bytes_accessed=2 * depth * (total + n) + (4 if extra else 2) * total * n,
            transcendentals=0,
        ),
        name="weight_grad",
    )(sel, *args)


def columns_kernel(sel_ref, a_ref, b_ref, own_ref, oth_ref):
    own_ref[...] = a_ref[...]
    oth_ref[...] = b_ref[...]


def split_columns(core, w, quads):
    model, wide = w.shape
    width = wide // 6 // quads
    at = lambda flip: lambda i, s: (
        0,
        (i // quads) * 2 * quads + 2 * (i % quads) + (1 - s[0] if flip else s[0]),
    )
    out = pl.BlockSpec((model, width), lambda i, s: (0, i))
    return pl.pallas_call(
        columns_kernel,
        out_shape=(jax.ShapeDtypeStruct((model, wide // 2), BF),) * 2,
        grid_spec=pltpu.PrefetchScalarGridSpec(
            num_scalar_prefetch=1,
            grid=(3 * quads,),
            in_specs=[pl.BlockSpec((model, width), at(False)), pl.BlockSpec((model, width), at(True))],
            out_specs=(out, out),
        ),
        compiler_params=pltpu.CompilerParams(vmem_limit_bytes=8 << 20),
        cost_estimate=pl.CostEstimate(flops=0, bytes_accessed=4 * model * wide, transcendentals=0),
        name="split_columns",
    )(core, w, w)


def chosen(sel_ref, own_ref, oth_ref):
    mine = pl.program_id(0) // 2 == sel_ref[0]
    return jnp.where(mine, own_ref[...].astype(F32), oth_ref[...].astype(F32))


def project_kernel(sel_ref, frac_ref, own_ref, oth_ref, vec_ref, w_ref, bias_ref, qkv_ref, start_ref):
    start = chosen(sel_ref, own_ref, oth_ref) + (frac_ref[0] * vec_ref[0:1, :] + vec_ref[1:2, :])
    start = start.astype(BF)
    start_ref[...] = start
    half = w_ref.shape[1] // 3
    out = dot(start, w_ref[...], NN) + bias_ref[...]
    qkv_ref[:, :half] = (out[:, :half] * (0.125 * LOG2E)).astype(BF)
    qkv_ref[:, half:] = out[:, half:].astype(BF)


def project(core, fraction, own, oth, vecs, w, bias):
    rows, model = own.shape
    br = rows // 2
    fixed = lambda shape: pl.BlockSpec(shape, lambda i, s: (0, 0))
    part = pl.BlockSpec((br, model), lambda i, s: (i % 2, 0))
    out = lambda w: pl.BlockSpec((br, w), lambda i, s: (i, 0))
    return pl.pallas_call(
        project_kernel,
        out_shape=(
            jax.ShapeDtypeStruct((2 * rows, w.shape[1]), BF),
            jax.ShapeDtypeStruct((2 * rows, model), BF),
        ),
        grid_spec=pltpu.PrefetchScalarGridSpec(
            num_scalar_prefetch=1,
            grid=(4,),
            in_specs=[
                pl.BlockSpec(memory_space=pltpu.SMEM),
                part,
                part,
                fixed(vecs.shape),
                fixed(w.shape),
                fixed(bias.shape),
            ],
            out_specs=(out(w.shape[1]), out(model)),
        ),
        compiler_params=pltpu.CompilerParams(vmem_limit_bytes=40 << 20),
        cost_estimate=pl.CostEstimate(
            flops=4 * rows * model * w.shape[1],
            bytes_accessed=4 * rows * (2 * model + w.shape[1]) + 2 * model * w.shape[1],
            transcendentals=0,
        ),
        name="project",
    )(core, fraction, own, oth, vecs, w, bias)


def context_grad_kernel(sel_ref, own_ref, oth_ref, w_ref, out_ref):
    rows = chosen(sel_ref, own_ref, oth_ref).astype(BF)
    out_ref[...] = dot(rows, w_ref[...].reshape(-1, w_ref.shape[-1]), NT).astype(BF)


def context_grad(core, own, oth, w_out):
    rows, model = own.shape
    br = rows // 2
    quads, _, w, _ = w_out.shape
    part = pl.BlockSpec((br, model), lambda i, s: (i % 2, 0))
    return pl.pallas_call(
        context_grad_kernel,
        out_shape=jax.ShapeDtypeStruct((2 * rows, quads * w), BF),
        grid_spec=pltpu.PrefetchScalarGridSpec(
            num_scalar_prefetch=1,
            grid=(4,),
            in_specs=[
                part,
                part,
                pl.BlockSpec((quads, 1, w, model), lambda i, s: (0, s[0], 0, 0)),
            ],
            out_specs=pl.BlockSpec((br, quads * w), lambda i, s: (i, 0)),
        ),
        compiler_params=pltpu.CompilerParams(vmem_limit_bytes=32 << 20),
        cost_estimate=pl.CostEstimate(
            flops=4 * rows * model * quads * w,
            bytes_accessed=4 * rows * (model + quads * w) + 2 * quads * w * model,
            transcendentals=0,
        ),
        name="context_grad",
    )(core, own, oth, w_out)


def out_grad_kernel(sel_ref, a0, b0, a1, b1, own_ref, oth_ref, out_ref):
    w = a0.shape[1]
    out_ref[:w, :] = (dot(a0[...], own_ref[...], TN) + dot(b0[...], oth_ref[...], TN)).astype(BF)
    out_ref[w:, :] = (dot(a1[...], own_ref[...], TN) + dot(b1[...], oth_ref[...], TN)).astype(BF)


def out_grad(core, contexts, own, oth):
    rows, model = own.shape
    w = contexts[0].shape[1]
    here = pl.BlockSpec((rows, w), lambda i, s: (s[0], 0))
    there = pl.BlockSpec((rows, w), lambda i, s: (1 - s[0], 0))
    full = pl.BlockSpec((rows, model), lambda i, s: (0, 0))
    return pl.pallas_call(
        out_grad_kernel,
        out_shape=jax.ShapeDtypeStruct((2 * w, model), BF),
        grid_spec=pltpu.PrefetchScalarGridSpec(
            num_scalar_prefetch=1,
            grid=(1,),
            in_specs=[here, there, here, there, full, full],
            out_specs=pl.BlockSpec((2 * w, model), lambda i, s: (0, 0)),
        ),
        compiler_params=pltpu.CompilerParams(vmem_limit_bytes=40 << 20),
        cost_estimate=pl.CostEstimate(
            flops=8 * rows * model * w, bytes_accessed=8 * rows * (model + w), transcendentals=0
        ),
        name="out_grad",
    )(core, contexts[0], contexts[0], contexts[1], contexts[1], own, oth)


def finish_kernel(sel_ref, base_ref, mine_ref, got_ref, wm0, wm1, wm2, wg0, wg1, wg2, out_ref, *rest):
    total = base_ref[...]
    for t, (wm, wg) in enumerate(((wm0, wg0), (wm1, wg1), (wm2, wg2))):
        total = total + dot(mine_ref[t], wm[...], NT)
        total = total + dot(got_ref[t], wg[...], NT)
    out_ref[...] = total.astype(out_ref.dtype)
    if rest:
        step = pl.program_id(0)

        @pl.when(step == 0)
        def _():
            rest[0][...] = jnp.zeros_like(rest[0])

        rest[0][...] += jnp.sum(total, axis=0, keepdims=True)


def add_start(core, base, grads, got, w_mine, w_got, group, last, br=288):
    rows, model = base.shape
    n = got.shape[2]
    steps = rows // br
    every = w_mine.shape[1] // (3 * n)
    cols = [pl.BlockSpec((model, n), lambda i, s, t=t: (0, t * every + group)) for t in range(3)]
    row = pl.BlockSpec((br, model), lambda i, s: (i, 0))
    outs = [jax.ShapeDtypeStruct((rows, model), BF if last else F32)]
    specs = [row]
    if last:
        outs.append(jax.ShapeDtypeStruct((1, model), F32))
        specs.append(pl.BlockSpec((1, model), lambda i, s: (0, 0)))
    return pl.pallas_call(
        finish_kernel,
        out_shape=tuple(outs),
        grid_spec=pltpu.PrefetchScalarGridSpec(
            num_scalar_prefetch=1,
            grid=(steps,),
            in_specs=[
                row,
                pl.BlockSpec((3, br, n), lambda i, s: (0, s[0] * steps + i, 0)),
                pl.BlockSpec((3, br, n), lambda i, s: (0, i, 0)),
                *cols,
                *cols,
            ],
            out_specs=tuple(specs),
        ),
        compiler_params=pltpu.CompilerParams(vmem_limit_bytes=40 << 20),
        cost_estimate=pl.CostEstimate(
            flops=12 * rows * n * model,
            bytes_accessed=8 * rows * model + 12 * n * (rows + model),
            transcendentals=0,
        ),
        name="add_start",
    )(core, base, grads, got, *(w_mine,) * 3, *(w_got,) * 3)


class Plan:
    def __init__(self, mesh):
        sizes = dict(mesh.shape)
        self.batch, self.depth = sizes["batch"], sizes["seq"]
        chips = self.batch // 2
        side = 1
        while side * side < chips:
            side *= 2
        self.nx, self.ny = side, chips // side

    def perm(self, target):
        pairs = []
        for y in range(self.ny):
            for x in range(self.nx):
                for c in range(2):
                    for z in range(self.depth):
                        to = target(y, x, c, z)
                        if to != (y, x, c, z):
                            pairs.append((self.index(y, x, c, z), self.index(*to)))
        return pairs

    def index(self, y, x, c, z):
        return ((y * self.nx + x) * 2 + c) * self.depth + z

    def send(self, value, target):
        return lax.ppermute(value, AXES, self.perm(target))

    def sibling(self, value):
        return self.send(value, lambda y, x, c, z: (y, x, 1 - c, z))


def pick(array, index, axis):
    return lax.dynamic_index_in_dim(array, index, axis, keepdims=False)


def tie(*values):
    return lax.optimization_barrier(values)


class Sum:
    def __init__(self, plan, terms, where, axes="yxhl"):
        self.plan, self.terms, self.axes = plan, terms, axes
        y, x, z = where
        self.where = {"y": y, "x": x, "h": z // 2, "l": z % 2}

    def send(self, axis):
        plan, terms = self.plan, self.terms
        self.axis, self.at = axis, self.axes.index(axis)
        self.axes = self.axes.replace(axis, "")
        size = {"x": plan.nx, "y": plan.ny}.get(axis, 2)
        here = self.where[axis]
        self.got = []
        for r in range(1, size):

            def target(y, x, c, z, r=r):
                at = {"y": y, "x": x, "h": z // 2, "l": z % 2}
                at[axis] = (at[axis] + r) % size
                return at["y"], at["x"], c, 2 * at["h"] + at["l"]

            self.got.append(plan.send(pick(terms, (here + r) % size, self.at), target))
        return self

    def add(self):
        total = pick(self.terms, self.where[self.axis], self.at).astype(F32)
        for got in self.got:
            total = total + got.astype(F32)
        self.terms = total.astype(self.terms.dtype) if self.axes else total
        return self.terms

    def hold(self, *others):
        self.terms, *rest = tie(self.terms, *others)
        return rest


def per_chip(
    plan,
    inputs,
    timesteps,
    segments,
    cotangent,
    w_qkv,
    b_query,
    b_value,
    w_out,
    b_out,
    ln1_gain,
    ln1_bias,
    w_up,
    b_up,
    w_down,
    b_down,
    ln2_gain,
    ln2_bias,
    w_time,
    b_time,
):
    local_len = inputs.shape[1]
    rows = 2 * local_len
    length = segments.shape[1]
    b = lax.axis_index("batch")
    z = lax.axis_index("seq")
    c, x, y = b % 2, (b // 2) % plan.nx, b // 2 // plan.nx
    part = z % 2
    where = (y, x, z)
    first = (segments[1, 0] == segments[1, 128 * 12]).astype(jnp.int32)
    which = lambda s: (first + s) % 2
    facts = jnp.concatenate(
        [segments[:, : 128 * 13 : 128], timesteps[:, None], jnp.zeros((2, 2), jnp.int32)], axis=1
    )
    facts = jnp.stack([pick(facts, which(0), 0), pick(facts, which(1), 0)])
    other_facts = plan.sibling(facts)
    facts = jnp.where(z // 2 == c, facts, other_facts)
    mine = pick(facts, z % 2, 0)
    marks = mine[:13]
    info = jnp.concatenate(
        [
            jnp.where(marks[:1] == marks[12:], 1, jnp.where(marks[12:] == marks[:1] + 12, 2, 0)),
            jnp.sum((marks[None, :] < marks[:, None]).astype(jnp.int32), axis=1),
            jnp.sum((marks[None, :] <= marks[:, None]).astype(jnp.int32), axis=1),
        ]
    )
    fraction = mine[13].astype(F32) / TSTEPS

    stays = z // 2 == c

    def exchange(parts):
        got = [
            plan.send(v, lambda y, x, c, z, j=j: (y, x, z // 2, 2 * c + (z + j) % 2))
            for j, v in enumerate(parts)
        ]
        return [(got[0], parts[0]), (got[1], None)]

    def arrived(got):
        return [jnp.where(stays, got[0][1], got[0][0]), got[1][0]]

    def gather_parts(array):
        return [pick(array, which((part + j) % 2), 0) for j in (0, 1)]

    def gather_end(got):
        got = arrived(got)
        return jnp.concatenate(
            [jnp.where(part == 0, got[0], got[1]), jnp.where(part == 0, got[1], got[0])], axis=0
        )

    def spread_parts(array):
        array = array.reshape(2, local_len, array.shape[-1])
        return [pick(array, (part + j) % 2, 0) for j in (0, 1)]

    def spread_end(got):
        got = arrived(got)
        swap = (part + first) % 2
        return jnp.stack(
            [jnp.where(swap == 0, got[0], got[1]), jnp.where(swap == 0, got[1], got[0])], axis=0
        )

    def whole(own, other):
        return jnp.where(c == 0, jnp.concatenate([own, other]), jnp.concatenate([other, own]))

    def halves(array, axis):
        shape = array.shape
        cut = shape[:axis] + (plan.ny * plan.nx, 2, -1) + shape[axis + 1 :]
        flat = shape[:axis] + (-1,) + shape[axis + 1 :]
        split = array.reshape(cut)
        return (
            pick(split, c, axis + 1).reshape(flat),
            pick(split, 1 - c, axis + 1).reshape(flat),
        )

    def blocks(array):
        return array.reshape(plan.ny, plan.nx, 2, 2, -1, array.shape[-1])

    model = inputs.shape[-1]
    half = model // 2
    quads = plan.ny * plan.nx
    core = jnp.stack([c]).astype(jnp.int32)
    away = 1 - core
    w_own, w_oth = split_columns(core, w_qkv, quads)
    bias = jnp.concatenate(
        [
            halves(b_query.astype(F32), 0)[0],
            jnp.zeros((half,), F32),
            halves(b_value.astype(F32), 0)[0],
        ]
    )
    w_out_four = w_out.reshape(quads, 2, -1, model)
    ahead = [range(0, quads // 2), range(quads // 2, quads)]
    groups = ahead
    own_inputs = gather_end(exchange(gather_parts(inputs)))
    vecs = jnp.stack(
        [v.astype(F32) for v in (w_time, b_time, b_out, ln1_gain, ln1_bias, b_down, ln2_gain, ln2_bias)]
    )
    cot_parts = gather_parts(cotangent)
    bias = bias[None]
    own_inputs, w_own, w_oth, vecs, info, bias, cot_parts = tie(
        own_inputs, w_own, w_oth, vecs, info, bias, cot_parts
    )
    sib_inputs = plan.sibling(own_inputs)
    cot_parts, sib_inputs = tie(cot_parts, sib_inputs)
    own_cotangent = gather_end(exchange(cot_parts))
    qkv, start_full = project(core, fraction[None], own_inputs, sib_inputs, vecs, w_own, bias)
    fwd = [attn_fwd(info, qkv, g.start, len(g)) for g in ahead]
    away_of = [
        plan.sibling(pick(f[0].reshape(2, rows, -1), 1 - c, 0)) for f in fwd
    ]
    result, normed_low, act, two_low, hid, grad_one, one_low, small_sums, up_sums = middle(
        core,
        fraction[None],
        own_inputs,
        [f[0] for f in fwd],
        away_of,
        own_cotangent,
        vecs,
        b_up.astype(F32)[None],
        w_out_four,
        w_up,
        w_down,
    )
    one_sib = plan.sibling(one_low)
    output_got = exchange(spread_parts(result))
    down_part = weight_grad(away, act, two_low, quads=quads)
    normed_low, down_part = tie(normed_low, down_part)
    down_got = plan.sibling(down_part)
    up_part = weight_grad(away, normed_low, hid, quads=quads)
    act, up_part = tie(act, up_part)
    up_got = plan.sibling(up_part)
    down_sum = weight_grad(core, act, two_low, down_got, quads=quads)
    normed_low, down_sum = tie(normed_low, down_sum)
    down = Sum(plan, blocks(down_sum), where).send("x")
    up_sum = weight_grad(core, normed_low, hid, up_got, quads=quads)
    one_low, one_sib, up_sum = tie(one_low, one_sib, up_sum)
    up = Sum(plan, blocks(up_sum), where).send("y")
    out_sum = out_grad(core, [f[0] for f in fwd], one_low, one_sib)
    one_low, one_sib, out_sum = tie(one_low, one_sib, out_sum)
    out = Sum(plan, blocks(out_sum), where).send("x")
    grad_context = context_grad(core, one_low, one_sib, w_out_four)

    def back(first, count, into=None):
        f = first // (quads // 2)
        start = ahead[f].start
        return attn_bwd(
            info,
            fwd[f][2],
            qkv,
            fwd[f][0],
            fwd[f][1],
            grad_context,
            first,
            count,
            first - start,
            quads // 2,
            first - start,
            into,
        )

    def away_rows(grads):
        return plan.sibling(pick(grads.reshape(3, 2, rows, -1), 1 - c, 1))

    def products(grads):
        cross_part = weight_grad(away, start_full, grads, quads=quads)
        grads, cross_part = tie(grads, cross_part)
        cross = plan.sibling(cross_part)
        keep = weight_grad(core, start_full, grads, quads=quads)
        return Sum(plan, blocks(cross), where), Sum(plan, blocks(keep), where)

    def settle(items, other):
        for item in items:
            item.got, other = tie(item.got, other)
            item.add()
            item.terms, other = tie(item.terms, other)
        return other

    grads, b_sum0 = back(0, quads // 2)
    got = away_rows(grads)
    output_got, grads = tie(output_got, grads)
    grads = settle([down, up, out], grads)
    down.send("y")
    up.send("x")
    out.send("y")
    cross0, keep0 = products(grads)
    got, cross0.terms, keep0.terms = tie(got, cross0.terms, keep0.terms)
    (grad_start,) = add_start(core, grad_one, grads, got, w_own, w_oth, 0, False)
    keep0.send("x")
    cross0.send("y")
    grad_context, grad_start = tie(grad_context, grad_start)
    grads, b_sum1 = back(quads // 2, quads // 4)
    grads = settle([down, up, out, keep0, cross0], grads)
    wide_rows = up.terms.shape[-2]
    slabs = [up.terms[..., i * model : (i + 1) * model] for i in range(up.terms.shape[-1] // model)]
    ffn = jnp.concatenate([down.terms, *slabs, out.terms], axis=2)
    ffn, grads = tie(ffn, grads)
    ffn = Sum(plan, ffn, where, "hl").send("l")
    keep0.send("y")
    cross0.send("x")
    grads, b_sum2 = back(quads // 2 + quads // 4, quads // 4, grads)
    got = away_rows(grads)
    grads = settle([ffn], grads)
    ffn.send("h")
    cross1, keep1 = products(grads)
    got, keep1.terms = tie(got, keep1.terms)
    keep1.send("x")
    cross1.send("y")
    grad_low, b_time_sum = add_start(core, grad_start, grads, got, w_own, w_oth, 1, True)
    in_parts, b_time_sum = tie(spread_parts(grad_low), b_time_sum)
    grad_inputs_got = exchange(in_parts)
    b_time_sum = settle([keep0, cross0, keep1, cross1], b_time_sum)
    ffn.got, b_time_sum = tie(ffn.got, b_time_sum)
    keep1.send("y")
    cross1.send("x")
    small_sums, up_sums, b_time_sum = tie(small_sums, up_sums, b_time_sum)
    b_sum = jnp.concatenate([b_sum0, b_sum1, b_sum2], axis=1)
    zero = jnp.zeros((quads, 2, half // quads), F32)

    def placed(v):
        return lax.dynamic_update_index_in_dim(zero, v.reshape(quads, half // quads), c, 1).reshape(-1)

    vectors = [small_sums[i] for i in range(6)]
    vectors += [placed(b_sum[0]), placed(b_sum[1]), fraction * b_time_sum[0], b_time_sum[0]]
    small = jnp.concatenate([v[:, None] for v in vectors] + [up_sums.reshape(model, -1)], axis=1)
    small_own, small_oth = halves(small, 0)
    small = Sum(plan, blocks(small_own + plan.sibling(small_oth)), where)
    small.send("x").add()
    small.send("y")
    keep1.got, cross1.got, small.got, grad_inputs_got = tie(
        keep1.got, cross1.got, small.got, grad_inputs_got
    )
    keep1.add()
    cross1.add()
    small.add()
    late = jnp.concatenate([i.terms for i in (keep0, cross0, keep1, cross1)], axis=3)
    late = Sum(plan, late, where, "hl").send("l")
    small.send("l")
    late.got, small.got = tie(late.got, small.got)
    late.add()
    small.add()
    late.send("h")
    small.send("h")
    small.add()
    small = small.terms
    late = late.add()
    wide = 3 * half // 2
    keeps = [late[:, :wide], late[:, 2 * wide : 3 * wide]]
    crosses = [late[:, wide : 2 * wide], late[:, 3 * wide : 4 * wide]]
    ffn = ffn.add()
    count = ffn.shape[0] - wide_rows * (len(slabs) + 1)
    sum_w_down, sum_w_out = ffn[:count], ffn[count + wide_rows * len(slabs) :]
    sum_w_up = jnp.concatenate(
        [ffn[count + i * wide_rows : count + (i + 1) * wide_rows] for i in range(len(slabs))], axis=1
    )
    output = spread_end(output_got)
    grad_inputs = spread_end(grad_inputs_got)
    split3 = lambda parts: jnp.concatenate(
        [p.reshape(p.shape[0], 3, len(g), -1) for p, g in zip(parts, groups)], axis=2
    )
    sum_own, sum_oth = split3(keeps), split3(crosses)
    pair = jnp.where(c == 0, jnp.stack([sum_own, sum_oth]), jnp.stack([sum_oth, sum_own]))
    sum_w_qkv = (
        pair.transpose(1, 2, 3, 0, 4).reshape(-1, 3 * model)
    )
    v = [small[:, i] for i in (6, 7, 0, 1, 2, 3, 4, 5, 8, 9)]
    return (
        output,
        grad_inputs,
        sum_w_qkv,
        v[0],
        v[1],
        sum_w_out,
        v[2],
        v[3],
        v[4],
        sum_w_up,
        small[:, 10:].reshape(-1),
        sum_w_down,
        v[5],
        v[6],
        v[7],
        v[8],
        v[9],
    )


def solution(mesh):
    placed = (
        P("batch", "seq", None),
        P("batch"),
        P("batch", None),
        P("batch", "seq", None),
        P(),
        P(),
        P(),
        P(),
        P(),
        P(),
        P(),
        P(),
        P(),
        P(),
        P(),
        P(),
        P(),
        P(),
        P(),
    )
    sizes = dict(mesh.shape)
    body = per_device
    if sizes["seq"] == 4 and sizes["batch"] % 2 == 0:
        body = functools.partial(per_chip, Plan(mesh))
    return jax.shard_map(
        body,
        mesh=mesh,
        in_specs=placed,
        out_specs=(
            P("batch", "seq", None),
            P("batch", "seq", None),
            P(("batch", "seq"), None),
            P(("batch", "seq")),
            P(("batch", "seq")),
            P(("batch", "seq"), None),
            P(("batch", "seq")),
            P(("batch", "seq")),
            P(("batch", "seq")),
            P(("batch", "seq"), None),
            P(("batch", "seq")),
            P(("batch", "seq"), None),
            P(("batch", "seq")),
            P(("batch", "seq")),
            P(("batch", "seq")),
            P(("batch", "seq")),
            P(("batch", "seq")),
        ),
        check_vma=False,
    )
```

```python
import functools

import jax
import jax.numpy as jnp
from jax import lax
from jax.experimental import pallas as pl
from jax.experimental.pallas import tpu as pltpu
from jax.sharding import PartitionSpec as P

D = 1024
HEADS = 16
TSTEPS = 5000
AXES = ("batch", "seq")


BF=jnp.bfloat16; F32=jnp.float32
NT=(((1,),(1,)),((),())); NN=(((1,),(0,)),((),())); TN=(((0,),(0,)),((),()))
def dot(a,b,d): return lax.dot_general(a,b,d,preferred_element_type=F32)
PHASE=1
FILLED=1664; PAD=64
def lanes(rows):
    return lax.broadcasted_iota(jnp.int32,(rows,128),1)
def parts3(x):
    a=x.astype(BF).astype(F32); r=x-a; b=r.astype(BF).astype(F32); c=r-b
    return a,b,c
def augment(base,h,x,lane):
    a,b,c=parts3(x)
    o=(1-h)*64
    f=base.astype(F32)
    f=jnp.where((lane>=o)&(lane<o+64),jnp.where(lane==o,a,jnp.where(lane==o+1,b,jnp.where(lane==o+2,c,0.0))),f)
    return f.astype(BF)
def ones3(base,h,lane,n=3):
    o=(1-h)*64
    f=base.astype(F32)
    f=jnp.where((lane>=o)&(lane<o+64),jnp.where(lane<o+n,1.0,0.0),f)
    return f.astype(BF)
def spread(base,h,x,lane):
    a=x.astype(BF).astype(F32); r=x-a; b=r.astype(BF).astype(F32); c=r-b
    o=(1-h)*64
    f=jnp.where(lane==o,a,jnp.where(lane==o+1,b,jnp.where(lane==o+2,c,0.0)))
    return jnp.where((lane//64)==h,base.astype(F32),f).astype(BF)
def fwd_tiles(tasks,lane):
    scores=[]
    for q,k,vs,keep in tasks:
        for h in (0,1):
            qh=jnp.where((lane//64)==h,q.astype(F32),0.0).astype(BF)
            s=dot(qh,k,NT)
            scores.append(s if keep is None else jnp.where(keep,s,-1e30))
    tops=[];outs=[]
    depth=PHASE
    n=len(scores)
    def soft(i):
        m=jnp.max(scores[i],axis=1,keepdims=True)
        tops.append(m)
        return jnp.exp2(scores[i]-m).astype(BF)
    ps=[]
    for i in range(n+depth):
        if i<n: ps.append(soft(i))
        if i>=depth: outs.append(dot(ps[i-depth],tasks[(i-depth)//2][2][(i-depth)%2],NN))
    done=[]
    for t,(q,_,_,_) in enumerate(tasks):
        os=[];augs=[]
        for h in (0,1):
            o=outs[2*t+h]
            os.append(o/pltpu.roll(o,64,1))
            augs.append(spread(q,h,-(tops[2*t+h]+jnp.log2(o)),lane))
        done.append((jnp.where(lane<64,os[0],os[1]),augs))
    return done
def fwd_store(refs,rows,o,augs):
    o_ref,ol_ref,qa_ref=refs
    o_ref[rows,:]=o.astype(BF)
    ol_ref[rows,:]=(o-o.astype(BF).astype(F32)).astype(BF)
    for h in (0,1): qa_ref[h,rows,:]=augs[h]
def fwd_kernel(bq,info,q_ref,k_ref,v_ref,*refs):
    *refs,vs_ref=refs
    single=info[0]==1
    @pl.when(single)
    def _():
        v=v_ref[0:FILLED,:]
        for h in (0,1): vs_ref[h,...]=ones3(v,h,lanes(FILLED),64)
        lq=lanes(bq)
        @pl.loop(0,FILLED//bq)
        def _(r):
            rows=pl.ds(pl.multiple_of(r*bq,bq),bq)
            (o,augs),=fwd_tiles([(q_ref[rows,:],k_ref[0:FILLED,:],(vs_ref[0],vs_ref[1]),None)],lq)
            fwd_store(refs,rows,o,augs)
    @pl.when(info[0]==2)
    def _():
        lq=lanes(128)
        each=[slice(i*128,i*128+128) for i in range(13)]
        tasks=[(q_ref[r,:],k_ref[r,:],[ones3(v_ref[r,:],h,lq,64) for h in (0,1)],None) for r in each]
        for r,(o,augs) in zip(each,fwd_tiles(tasks,lq)): fwd_store(refs,r,o,augs)
    @pl.when(info[0]==0)
    def _():
        col=lax.broadcasted_iota(jnp.int32,(128,512),1)
        lw=lanes(512); lq=lanes(128)
        @pl.loop(0,13)
        def _(i):
            lo=info[1+i]; hi=info[14+i]
            at=jnp.minimum(lo,9)
            window=pl.ds(pl.multiple_of(at*128,128),512)
            k=k_ref[window,:]; v=v_ref[window,:]
            vs=[ones3(v,h,lw,64) for h in (0,1)]
            keep=(col>=(lo-at)*128)&(col<(hi-at)*128)
            rows=pl.ds(pl.multiple_of(i*128,128),128)
            (o,augs),=fwd_tiles([(q_ref[rows,:],k,vs,keep)],lq)
            fwd_store(refs,rows,o,augs)
    rows=slice(FILLED,FILLED+PAD)
    lp=lanes(PAD)
    v=v_ref[rows,:]
    (o,augs),=fwd_tiles([(q_ref[rows,:],k_ref[rows,:],[ones3(v,h,lp,64) for h in (0,1)],None)],lp)
    fwd_store(refs,rows,o,augs)
def attn_fwd(info,qkv,first,count,bq=832):
    L,W3=qkv.shape; n=W3//384
    spec=lambda j: pl.BlockSpec((L,128),lambda p,s,j=j:(0,p+first+j*n))
    one=pl.BlockSpec((L,128),lambda p,s:(0,p))
    return pl.pallas_call(functools.partial(fwd_kernel,bq),
        out_shape=(jax.ShapeDtypeStruct((L,count*128),BF),)*2+(jax.ShapeDtypeStruct((2*count,L,128),BF),),
        grid_spec=pltpu.PrefetchScalarGridSpec(num_scalar_prefetch=1,grid=(count,),
            in_specs=[spec(0),spec(1),spec(2)],
            out_specs=(one,one,pl.BlockSpec((2,L,128),lambda p,s:(p,0,0))),
            scratch_shapes=[pltpu.VMEM((2,FILLED,128),BF)]),
        compiler_params=pltpu.CompilerParams(vmem_limit_bytes=50<<20),name="attn_forward",
        cost_estimate=pl.CostEstimate(flops=8*count*L*L*256,bytes_accessed=10*L*count*128,transcendentals=2*count*L*L))(info,qkv,qkv,qkv)
def deltas(g,o,ol,lane):
    prod=g.astype(F32)*(o.astype(F32)+ol.astype(F32))
    return [augment(g,h,-jnp.sum(jnp.where((lane//64)==h,prod,0.0),axis=1,keepdims=True),lane) for h in (0,1)]
def bwd_tiles(tasks,lane,turned=None):
    khs=[ones3(t[1],t[4],lane) for t in tasks]
    ps=[dot(kh,t[0],NT) for kh,t in zip(khs,tasks)]
    ds=[dot(ones3(t[2],t[4],lane),t[3],NT) for t in tasks]
    done=[]
    for kh,p,d,(qa,_,_,ga,h,keep) in zip(khs,ps,ds,tasks):
        p=jnp.exp2(p)
        if keep is not None: p=jnp.where(keep,p,0.0)
        d=(p*d).astype(BF)
        done.append((kh,p.astype(BF),d,qa,ga))
    back=lambda i,kh,d: dot(d,kh,TN) if turned is None else dot(turned[i*64:i*64+64,:],d,NN)
    return [(back(i,kh,d),dot(d,qa,NN),dot(p,ga,NN)) for i,(kh,p,d,qa,ga) in enumerate(done)]
LN2=0.6931471805599453
def both(a,lane): return jnp.where(lane<64,a[0],a[1])
def bwd_alone(each,lane,qa_ref,k_ref,v_ref,o_ref,ol_ref,g_ref,dq_ref,dk_ref,dv_ref):
    tasks=[]
    for r in each:
        gas=deltas(g_ref[r,:],o_ref[r,:],ol_ref[r,:],lane)
        tasks+=[(qa_ref[h,r,:],k_ref[r,:],v_ref[r,:],gas[h],h,None) for h in (0,1)]
    got=bwd_tiles(tasks,lane)
    for i,r in enumerate(each):
        x,y=got[2*i],got[2*i+1]
        dq_ref[r,:]=(both((x[0],y[0]),lane)*0.125).astype(BF)
        dk_ref[r,:]=(both((x[1],y[1]),lane)*LN2).astype(BF)
        dv_ref[r,:]=both((x[2],y[2]),lane).astype(BF)
def bwd_kernel(bk,joined,info,qa_ref,k_ref,v_ref,o_ref,ol_ref,g_ref,*rest):
    d_ref,sum_ref,acc,acc_k,acc_v,ga_ref=rest[1:] if joined else rest
    dq_ref,dk_ref,dv_ref=d_ref.at[0],d_ref.at[1],d_ref.at[2]
    tile_refs=(qa_ref,k_ref,v_ref,o_ref,ol_ref,g_ref,dq_ref,dk_ref,dv_ref)
    single=info[0]==1
    @pl.when(single)
    def _():
        lf=lanes(FILLED)
        gas=deltas(g_ref[0:FILLED,:],o_ref[0:FILLED,:],ol_ref[0:FILLED,:],lf)
        acc[...]=jnp.zeros_like(acc)
        lb=lanes(bk)
        ga_ref[0,...]=gas[0]; ga_ref[1,...]=gas[1]
        @pl.loop(0,FILLED//bk)
        def _(r):
            rows=pl.ds(pl.multiple_of(r*bk,bk),bk)
            k=k_ref[rows,:]; v=v_ref[rows,:]
            dks=[];dvs=[]
            got=bwd_tiles([(qa_ref[h,0:FILLED,:],k,v,ga_ref[h],h,None) for h in (0,1)],lb,k.astype(F32).T.astype(BF))
            for h in (0,1):
                dq,dk,dv=got[h]
                acc[h*64:h*64+64,:]+=dq
                dks.append(dk); dvs.append(dv)
            dk_ref[rows,:]=(both(dks,lb)*LN2).astype(BF)
            dv_ref[rows,:]=both(dvs,lb).astype(BF)
        dq_ref[0:FILLED,:]=(acc[...].T*0.125).astype(BF)
    @pl.when(info[0]==2)
    def _():
        lq=lanes(128)
        bwd_alone([slice(i*128,i*128+128) for i in range(13)],lq,*tile_refs)
    @pl.when(info[0]==0)
    def _():
        row=lax.broadcasted_iota(jnp.int32,(512,128),0)
        lw=lanes(512); lq=lanes(128)
        acc_k[...]=jnp.zeros_like(acc_k); acc_v[...]=jnp.zeros_like(acc_v)
        @pl.loop(0,13)
        def _(i):
            lo=info[1+i]; hi=info[14+i]
            at=jnp.minimum(lo,9)
            window=pl.ds(pl.multiple_of(at*128,128),512)
            k=k_ref[window,:]; v=v_ref[window,:]
            keep=(row>=(lo-at)*128)&(row<(hi-at)*128)
            rows=pl.ds(pl.multiple_of(i*128,128),128)
            gas=deltas(g_ref[rows,:],o_ref[rows,:],ol_ref[rows,:],lq)
            dqs=[]
            got=bwd_tiles([(qa_ref[h,rows,:],k,v,gas[h],h,keep) for h in (0,1)],lw)
            for h in (0,1):
                dq,dk,dv=got[h]
                dqs.append(dq)
                acc_k[h,window,:]+=dk
                acc_v[h,window,:]+=dv
            dq_ref[rows,:]=(both(dqs,lq)*0.125).astype(BF)
        lf=lanes(FILLED)
        dk_ref[0:FILLED,:]=(jnp.where(lf<64,acc_k[0],acc_k[1])*LN2).astype(BF)
        dv_ref[0:FILLED,:]=jnp.where(lf<64,acc_v[0],acc_v[1]).astype(BF)
    bwd_alone([slice(FILLED,FILLED+PAD)],lanes(PAD),*tile_refs)
    sum_ref[0:1,:]=jnp.sum(dq_ref[...].astype(F32),axis=0,keepdims=True)
    sum_ref[1:2,:]=jnp.sum(dv_ref[...].astype(F32),axis=0,keepdims=True)
def attn_bwd(info,qa,qkv,o,ol,g,first,count,inner,wide,at,into=None,bk=416):
    L,W3=qkv.shape; n=W3//384
    spec=lambda j: pl.BlockSpec((L,128),lambda p,s,j=j:(0,p+first+j*n))
    one=pl.BlockSpec((L,128),lambda p,s:(0,p))
    part=pl.BlockSpec((L,128),lambda p,s:(0,p+inner))
    every=pl.BlockSpec((L,128),lambda p,s:(0,p+first))
    return pl.pallas_call(functools.partial(bwd_kernel,bk,into is not None),
        input_output_aliases={} if into is None else {7:0},
        out_shape=(jax.ShapeDtypeStruct((3,L,wide*128),BF),jax.ShapeDtypeStruct((2,count*128),F32)),
        grid_spec=pltpu.PrefetchScalarGridSpec(num_scalar_prefetch=1,grid=(count,),
            in_specs=[pl.BlockSpec((2,L,128),lambda p,s:(p+inner,0,0)),spec(1),spec(2),part,part,every]+([] if into is None else [pl.BlockSpec(memory_space=pl.ANY)]),
            out_specs=(pl.BlockSpec((3,L,128),lambda p,s:(0,0,p+at)),pl.BlockSpec((2,128),lambda p,s:(0,p))),
            scratch_shapes=[pltpu.VMEM((128,FILLED),F32)]+[pltpu.VMEM((2,FILLED,128),F32)]*2+[pltpu.VMEM((2,FILLED,128),BF)]),
        compiler_params=pltpu.CompilerParams(vmem_limit_bytes=56<<20),name="attn_backward",
        cost_estimate=pl.CostEstimate(flops=20*count*L*L*256,bytes_accessed=16*L*count*128,transcendentals=2*count*L*L))(*((info,qa,qkv,qkv,o,ol,g) if into is None else (info,qa,qkv,qkv,o,ol,g,into)))


def gelu_exact(values):
    return jax.nn.gelu(values, approximate=False)


def norm_forward(values, gain, shift):
    centered = values - jnp.mean(values, axis=-1, keepdims=True)
    inverse = lax.rsqrt(jnp.mean(centered * centered, axis=-1, keepdims=True) + 1e-05)
    unit_part = centered * inverse
    return (unit_part * gain + shift, unit_part, inverse)


def norm_backward(grad_out, unit_part, inverse, gain):
    scaled = grad_out * gain
    centered = scaled - jnp.mean(scaled, axis=-1, keepdims=True)
    grad_in = inverse * (
        centered - unit_part * jnp.mean(scaled * unit_part, axis=-1, keepdims=True)
    )
    return (grad_in, jnp.sum(grad_out * unit_part, axis=0), jnp.sum(grad_out, axis=0))


def attention_forward(query_all, key_all, value_all, segments, head_dim):
    length, local_width = (query_all.shape[1], query_all.shape[2])
    head_count = local_width // head_dim
    block_len = length // 3
    score_scale = head_dim ** (-0.5)

    def per_sequence(pieces):
        queries, key_rows, value_rows, seq_ids = pieces
        key_heads = key_rows.reshape(length, head_count, head_dim)
        value_heads = value_rows.reshape(length, head_count, head_dim)

        def per_block(block_pieces):
            query_part, id_part = block_pieces
            query_heads = query_part.reshape(block_len, head_count, head_dim)
            scores = (
                jnp.einsum(
                    "qhd,khd->hqk", query_heads, key_heads, preferred_element_type=jnp.float32
                )
                * score_scale
            )
            masked = jnp.where(id_part[None, :, None] == seq_ids[None, None, :], scores, -1e30)
            maxima = jnp.max(masked, axis=-1, keepdims=True)
            exp_scores = jnp.exp(masked - maxima)
            totals = jnp.sum(exp_scores, axis=-1, keepdims=True)
            weights_low = (exp_scores / totals).astype(jnp.bfloat16)
            context = jnp.einsum(
                "hqk,khd->qhd", weights_low, value_heads, preferred_element_type=jnp.float32
            )
            return (
                context.astype(jnp.bfloat16).reshape(block_len, local_width),
                (maxima + jnp.log(totals))[..., 0],
            )

        contexts, logsums = lax.map(
            per_block, (queries.reshape(3, block_len, local_width), seq_ids.reshape(3, block_len))
        )
        return (contexts.reshape(length, local_width), logsums)

    return lax.map(per_sequence, (query_all, key_all, value_all, segments))


def attention_backward(query_all, key_all, value_all, segments, logsums, grad_all, head_dim):
    length, local_width = (query_all.shape[1], query_all.shape[2])
    head_count = local_width // head_dim
    block_len = length // 3
    score_scale = head_dim ** (-0.5)

    def per_sequence(pieces):
        queries, key_rows, value_rows, seq_ids, sum_rows, grad_rows = pieces
        key_heads = key_rows.reshape(length, head_count, head_dim)
        value_heads = value_rows.reshape(length, head_count, head_dim)

        def per_block(carry, block_pieces):
            key_total, value_total = carry
            query_part, id_part, sum_part, grad_part = block_pieces
            query_heads = query_part.reshape(block_len, head_count, head_dim)
            grad_heads = grad_part.reshape(block_len, head_count, head_dim)
            scores = (
                jnp.einsum(
                    "qhd,khd->hqk", query_heads, key_heads, preferred_element_type=jnp.float32
                )
                * score_scale
            )
            allowed = id_part[None, :, None] == seq_ids[None, None, :]
            prob_weights = jnp.where(allowed, jnp.exp(scores - sum_part[:, :, None]), 0.0)
            grad_probs = jnp.einsum(
                "qhd,khd->hqk", grad_heads, value_heads, preferred_element_type=jnp.float32
            )
            delta = jnp.sum(prob_weights * grad_probs, axis=-1, keepdims=True)
            grad_scores = (prob_weights * (grad_probs - delta)).astype(jnp.bfloat16)
            query_grad = (
                jnp.einsum(
                    "hqk,khd->qhd", grad_scores, key_heads, preferred_element_type=jnp.float32
                )
                * score_scale
            )
            key_total = (
                key_total
                + jnp.einsum(
                    "hqk,qhd->khd", grad_scores, query_heads, preferred_element_type=jnp.float32
                )
                * score_scale
            )
            value_total = value_total + jnp.einsum(
                "hqk,qhd->khd",
                prob_weights.astype(jnp.bfloat16),
                grad_heads,
                preferred_element_type=jnp.float32,
            )
            return (
                (key_total, value_total),
                query_grad.astype(jnp.bfloat16).reshape(block_len, local_width),
            )

        zero_heads = jnp.zeros((length, head_count, head_dim), jnp.float32)
        (key_total, value_total), query_grads = lax.scan(
            per_block,
            (zero_heads, zero_heads),
            (
                queries.reshape(3, block_len, local_width),
                seq_ids.reshape(3, block_len),
                sum_rows,
                grad_rows.reshape(3, block_len, local_width),
            ),
        )
        return (
            query_grads.reshape(length, local_width),
            key_total.astype(jnp.bfloat16).reshape(length, local_width),
            value_total.astype(jnp.bfloat16).reshape(length, local_width),
        )

    return lax.map(per_sequence, (query_all, key_all, value_all, segments, logsums, grad_all))


def per_device(
    inputs,
    timesteps,
    segments,
    cotangent,
    w_qkv,
    b_query,
    b_value,
    w_out,
    b_out,
    ln1_gain,
    ln1_bias,
    w_up,
    b_up,
    w_down,
    b_down,
    ln2_gain,
    ln2_bias,
    w_time,
    b_time,
):
    groups, local_len, model_width = inputs.shape
    row_count = groups * local_len
    head_dim = D // HEADS
    fraction = timesteps.astype(jnp.float32) / TSTEPS
    start_sum = (
        inputs.astype(jnp.float32)
        + fraction[:, None, None] * w_time.astype(jnp.float32)
        + b_time.astype(jnp.float32)
    )
    start_low = start_sum.astype(jnp.bfloat16)
    projected = jnp.einsum("bld,de->ble", start_low, w_qkv, preferred_element_type=jnp.float32)
    query_low = (projected[..., :model_width] + b_query.astype(jnp.float32)).astype(jnp.bfloat16)
    key_low = projected[..., model_width : 2 * model_width].astype(jnp.bfloat16)
    value_low = (projected[..., 2 * model_width :] + b_value.astype(jnp.float32)).astype(
        jnp.bfloat16
    )
    query_all, key_all, value_all = (
        lax.all_to_all(query_low, "seq", split_axis=2, concat_axis=1, tiled=True),
        lax.all_to_all(key_low, "seq", split_axis=2, concat_axis=1, tiled=True),
        lax.all_to_all(value_low, "seq", split_axis=2, concat_axis=1, tiled=True),
    )
    context_heads, logsums = attention_forward(query_all, key_all, value_all, segments, head_dim)
    context = lax.all_to_all(context_heads, "seq", split_axis=1, concat_axis=2, tiled=True)
    context_rows = context.reshape(row_count, model_width)
    start_rows = start_sum.reshape(row_count, model_width)
    residual_one = (
        start_rows
        + jnp.dot(context_rows, w_out, preferred_element_type=jnp.float32)
        + b_out.astype(jnp.float32)
    )
    normed, unit_one, inverse_one = norm_forward(
        residual_one, ln1_gain.astype(jnp.float32), ln1_bias.astype(jnp.float32)
    )
    normed_low = normed.astype(jnp.bfloat16)
    hidden_pre = jnp.dot(normed_low, w_up, preferred_element_type=jnp.float32) + b_up.astype(
        jnp.float32
    )
    activated, gelu_pull = jax.vjp(gelu_exact, hidden_pre)
    activated_low = activated.astype(jnp.bfloat16)
    residual_two = (
        normed
        + jnp.dot(activated_low, w_down, preferred_element_type=jnp.float32)
        + b_down.astype(jnp.float32)
    )
    result, unit_two, inverse_two = norm_forward(
        residual_two, ln2_gain.astype(jnp.float32), ln2_bias.astype(jnp.float32)
    )
    output = result.astype(jnp.bfloat16).reshape(groups, local_len, model_width)
    grad_result = cotangent.reshape(row_count, model_width).astype(jnp.float32)
    grad_two, grad_ln2_gain, grad_ln2_bias = norm_backward(
        grad_result, unit_two, inverse_two, ln2_gain.astype(jnp.float32)
    )
    grad_b_down = jnp.sum(grad_two, axis=0)
    grad_two_low = grad_two.astype(jnp.bfloat16)
    grad_w_down = jnp.einsum(
        "rf,rd->fd", activated_low, grad_two_low, preferred_element_type=jnp.float32
    )
    grad_activated = jnp.einsum(
        "rd,fd->rf", grad_two_low, w_down, preferred_element_type=jnp.float32
    )
    grad_hidden = gelu_pull(grad_activated)[0]
    grad_b_up = jnp.sum(grad_hidden, axis=0)
    grad_hidden_low = grad_hidden.astype(jnp.bfloat16)
    grad_w_up = jnp.einsum(
        "rd,rf->df", normed_low, grad_hidden_low, preferred_element_type=jnp.float32
    )
    grad_normed = grad_two + jnp.einsum(
        "rf,df->rd", grad_hidden_low, w_up, preferred_element_type=jnp.float32
    )
    grad_one, grad_ln1_gain, grad_ln1_bias = norm_backward(
        grad_normed, unit_one, inverse_one, ln1_gain.astype(jnp.float32)
    )
    grad_b_out = jnp.sum(grad_one, axis=0)
    grad_one_low = grad_one.astype(jnp.bfloat16)
    grad_w_out = jnp.einsum(
        "rd,re->de", context_rows, grad_one_low, preferred_element_type=jnp.float32
    )
    grad_context = (
        jnp.einsum("re,de->rd", grad_one_low, w_out, preferred_element_type=jnp.float32)
        .astype(jnp.bfloat16)
        .reshape(groups, local_len, model_width)
    )
    grad_context_heads = lax.all_to_all(
        grad_context, "seq", split_axis=2, concat_axis=1, tiled=True
    )
    query_grads, key_grads, value_grads = attention_backward(
        query_all, key_all, value_all, segments, logsums, grad_context_heads, head_dim
    )
    grad_query, grad_key, grad_value = (
        lax.all_to_all(query_grads, "seq", split_axis=1, concat_axis=2, tiled=True),
        lax.all_to_all(key_grads, "seq", split_axis=1, concat_axis=2, tiled=True),
        lax.all_to_all(value_grads, "seq", split_axis=1, concat_axis=2, tiled=True),
    )
    grad_projected = jnp.concatenate((grad_query, grad_key, grad_value), axis=2).reshape(
        row_count, 3 * model_width
    )
    grad_w_qkv = jnp.einsum(
        "rd,re->de",
        start_low.reshape(row_count, model_width),
        grad_projected,
        preferred_element_type=jnp.float32,
    )
    grad_b_query = jnp.sum(grad_query.astype(jnp.float32), axis=(0, 1))
    grad_b_value = jnp.sum(grad_value.astype(jnp.float32), axis=(0, 1))
    grad_start = grad_one + jnp.einsum(
        "re,de->rd", grad_projected, w_qkv, preferred_element_type=jnp.float32
    )
    grad_inputs = grad_start.astype(jnp.bfloat16).reshape(groups, local_len, model_width)
    per_sequence_grad = jnp.sum(grad_start.reshape(groups, local_len, model_width), axis=1)
    grad_w_time = jnp.einsum("g,gd->d", fraction, per_sequence_grad)
    grad_b_time = jnp.sum(per_sequence_grad, axis=0)
    (
        sum_w_qkv,
        sum_b_query,
        sum_b_value,
        sum_w_out,
        sum_b_out,
        sum_ln1_gain,
        sum_ln1_bias,
        sum_w_up,
        sum_b_up,
        sum_w_down,
        sum_b_down,
        sum_ln2_gain,
        sum_ln2_bias,
        sum_w_time,
        sum_b_time,
    ) = (
        lax.psum_scatter(grad_w_qkv, ("batch", "seq"), scatter_dimension=0, tiled=True),
        lax.psum_scatter(grad_b_query, ("batch", "seq"), scatter_dimension=0, tiled=True),
        lax.psum_scatter(grad_b_value, ("batch", "seq"), scatter_dimension=0, tiled=True),
        lax.psum_scatter(grad_w_out, ("batch", "seq"), scatter_dimension=0, tiled=True),
        lax.psum_scatter(grad_b_out, ("batch", "seq"), scatter_dimension=0, tiled=True),
        lax.psum_scatter(grad_ln1_gain, ("batch", "seq"), scatter_dimension=0, tiled=True),
        lax.psum_scatter(grad_ln1_bias, ("batch", "seq"), scatter_dimension=0, tiled=True),
        lax.psum_scatter(grad_w_up, ("batch", "seq"), scatter_dimension=0, tiled=True),
        lax.psum_scatter(grad_b_up, ("batch", "seq"), scatter_dimension=0, tiled=True),
        lax.psum_scatter(grad_w_down, ("batch", "seq"), scatter_dimension=0, tiled=True),
        lax.psum_scatter(grad_b_down, ("batch", "seq"), scatter_dimension=0, tiled=True),
        lax.psum_scatter(grad_ln2_gain, ("batch", "seq"), scatter_dimension=0, tiled=True),
        lax.psum_scatter(grad_ln2_bias, ("batch", "seq"), scatter_dimension=0, tiled=True),
        lax.psum_scatter(grad_w_time, ("batch", "seq"), scatter_dimension=0, tiled=True),
        lax.psum_scatter(grad_b_time, ("batch", "seq"), scatter_dimension=0, tiled=True),
    )
    return (
        output,
        grad_inputs,
        sum_w_qkv,
        sum_b_query,
        sum_b_value,
        sum_w_out,
        sum_b_out,
        sum_ln1_gain,
        sum_ln1_bias,
        sum_w_up,
        sum_b_up,
        sum_w_down,
        sum_b_down,
        sum_ln2_gain,
        sum_ln2_bias,
        sum_w_time,
        sum_b_time,
    )


SLOPE = F32
PIECES = 8
LOG2E = 1.4426950408889634


def layer_norm(values):
    centered = values - jnp.mean(values, axis=1, keepdims=True)
    inverse = lax.rsqrt(jnp.mean(centered * centered, axis=1, keepdims=True) + 1e-05)
    return centered * inverse, inverse


def layer_norm_back(scaled, unit_part, inverse):
    return inverse * (
        scaled
        - jnp.mean(scaled, axis=1, keepdims=True)
        - unit_part * jnp.mean(scaled * unit_part, axis=1, keepdims=True)
    )


def gelu_pair(v):
    bell = jnp.exp2(v * v * (-0.5 * LOG2E))
    base = 1.0 + 0.2316418882663604 * jnp.abs(v)
    t = pltpu.reciprocal(base, approx=True)
    t = t * (2.0 - base * t)
    tail = t * (
        0.127414796
        + t * (-0.142248368 + t * (0.7107068705 + t * (-0.7265760135 + t * 0.5307027145)))
    )
    tail = tail * bell
    cover = jnp.where(v >= 0, 1.0 - tail, tail)
    return v * cover, cover + v * bell * 0.3989422804014327


def middle_kernel(
    fc,
    sel_ref,
    frac_ref,
    inp_ref,
    ctx_a0_ref,
    ctx_a1_ref,
    ctx_b0_ref,
    ctx_b1_ref,
    cot_ref,
    vec_ref,
    b_up_ref,
    wo_a_ref,
    wo_b_ref,
    w_up_hbm,
    w_down_hbm,
    out_ref,
    norm_ref,
    act_ref,
    two_ref,
    hid_ref,
    one_ref,
    onel_ref,
    small_ref,
    smallup_ref,
    w_up,
    w_down,
    slope,
    sems,
):
    step = pl.program_id(0)
    def pieces(i, source, target):
        size = source.shape[0] // PIECES
        return [
            pltpu.make_async_copy(
                source.at[pl.ds(j * size, size)],
                target.at[pl.ds(j * size, size)],
                sems.at[i * PIECES + j],
            )
            for j in range(PIECES)
        ]

    copies = pieces(0, w_up_hbm, w_up) + pieces(1, w_down_hbm, w_down)

    @pl.when(step == 0)
    def _():
        for copy in copies:
            copy.start()
        small_ref[...] = jnp.zeros_like(small_ref)
        smallup_ref[...] = jnp.zeros_like(smallup_ref)

    vec = lambda i: vec_ref[i : i + 1, :]
    start = inp_ref[...].astype(F32) + (frac_ref[0] * vec(0) + vec(1))
    residual = (
        start
        + dot(jnp.concatenate([ctx_a0_ref[...], ctx_a1_ref[...]], axis=1), wo_a_ref[...].reshape(-1, wo_a_ref.shape[-1]), NN)
        + dot(jnp.concatenate([ctx_b0_ref[...], ctx_b1_ref[...]], axis=1), wo_b_ref[...].reshape(-1, wo_b_ref.shape[-1]), NN)
        + vec(2)
    )
    unit_one, inverse_one = layer_norm(residual)
    normed = unit_one * vec(3) + vec(4)
    low = normed.astype(BF)
    norm_ref[...] = low

    @pl.when(step == 0)
    def _():
        for copy in copies:
            copy.wait()

    width = w_up.shape[1]
    total = normed + vec(5)
    for f in range(0, width, fc):
        cols = slice(f, f + fc)
        v = dot(low, w_up[:, cols], NN) + b_up_ref[:, cols]
        a, g = gelu_pair(v)
        a = a.astype(BF)
        act_ref[:, cols] = a
        slope[:, cols] = g.astype(slope.dtype)
        total = total + dot(a, w_down[cols, :], NN)
    unit_two, inverse_two = layer_norm(total)
    out_ref[...] = (unit_two * vec(6) + vec(7)).astype(BF)
    cot = cot_ref[...].astype(F32)
    two = layer_norm_back(cot * vec(6), unit_two, inverse_two)
    add = lambda v: jnp.sum(v, axis=0, keepdims=True)
    small_ref[3:4, :] += add(two)
    small_ref[4:5, :] += add(cot * unit_two)
    small_ref[5:6, :] += add(cot)
    two_low = two.astype(BF)
    two_ref[...] = two_low
    total = two
    for f in range(0, width, fc):
        cols = slice(f, f + fc)
        d = dot(two_low, w_down[cols, :], NT) * slope[:, cols].astype(F32)
        smallup_ref[:, cols] += add(d)
        d = d.astype(BF)
        hid_ref[:, cols] = d
        total = total + dot(d, w_up[:, cols], NT)
    small_ref[1:2, :] += add(total * unit_one)
    small_ref[2:3, :] += add(total)
    one = layer_norm_back(total * vec(3), unit_one, inverse_one)
    small_ref[0:1, :] += add(one)
    one_ref[...] = one
    onel_ref[...] = one.astype(BF)


def middle(core, fraction, inp, ctx_a, ctx_b, cot, vecs, b_up, w_out, w_up, w_down, br=288, fc=2048):
    rows, model = inp.shape
    width = w_up.shape[1]
    half = model // 2
    quads = w_out.shape[0]
    row = lambda w: pl.BlockSpec((br, w), lambda i, s: (i, 0))
    fixed = lambda shape: pl.BlockSpec(shape, lambda i, s: (0,) * len(shape))
    here = pl.BlockSpec((br, half // 2), lambda i, s: (s[0] * (rows // br) + i, 0))
    wo = lambda flip: pl.BlockSpec(
        (quads, 1, model // quads // 2, model),
        (lambda i, s: (0, s[0], 0, 0)) if not flip else (lambda i, s: (0, 1 - s[0], 0, 0)),
    )
    out = lambda w, t: jax.ShapeDtypeStruct((rows, w), t)
    return pl.pallas_call(
        functools.partial(middle_kernel, fc),
        out_shape=(
            out(model, BF),
            out(model, BF),
            out(width, BF),
            out(model, BF),
            out(width, BF),
            out(model, F32),
            out(model, BF),
            jax.ShapeDtypeStruct((8, model), F32),
            jax.ShapeDtypeStruct((1, width), F32),
        ),
        grid_spec=pltpu.PrefetchScalarGridSpec(
            num_scalar_prefetch=1,
            grid=(rows // br,),
            in_specs=[
                pl.BlockSpec(memory_space=pltpu.SMEM),
                row(model),
                here,
                here,
                row(half // 2),
                row(half // 2),
                row(model),
                fixed((8, model)),
                fixed((1, width)),
                wo(False),
                wo(True),
                pl.BlockSpec(memory_space=pl.ANY),
                pl.BlockSpec(memory_space=pl.ANY),
            ],
            out_specs=(
                row(model),
                row(model),
                row(width),
                row(model),
                row(width),
                row(model),
                row(model),
                fixed((8, model)),
                fixed((1, width)),
            ),
            scratch_shapes=[
                pltpu.VMEM(w_up.shape, BF),
                pltpu.VMEM(w_down.shape, BF),
                pltpu.VMEM((br, width), SLOPE),
                pltpu.SemaphoreType.DMA((2 * PIECES,)),
            ],
        ),
        compiler_params=pltpu.CompilerParams(vmem_limit_bytes=60 << 20),
        cost_estimate=pl.CostEstimate(
            flops=4 * rows * model * (model // 2 + 2 * width),
            bytes_accessed=4 * model * width + rows * (16 * model + 4 * width),
            transcendentals=rows * width * 2,
        ),
        name="middle",
    )(core, fraction, inp, *ctx_a, *ctx_b, cot, vecs, b_up, w_out, w_out, w_up, w_down)


def grad_kernel(count, extra, *refs):
    lhs = [r[...] for r in refs[1 : 1 + count]]
    rhs_ref = refs[1 + count]
    out_ref = refs[-1]
    left = lhs[0] if count == 1 else jnp.concatenate(lhs, axis=1)
    right = rhs_ref[0] if len(rhs_ref.shape) == 3 else rhs_ref[...]
    total = dot(left, right, TN)
    if extra:
        total = total + refs[2 + count][...].astype(F32)
    out_ref[...] = total.astype(BF)


def weight_grad(sel, lhs, rhs, add=None, cols=1024, quads=4, pairs=2):
    depth, width = lhs.shape
    three = rhs.ndim == 3
    n = rhs.shape[0] * rhs.shape[2] if three else rhs.shape[1]
    cols = rhs.shape[2] if three else cols
    w = width // (quads * pairs)
    extra = add is not None
    if w >= 512:
        grid, count = (quads,), 1
        ins = [
            pl.BlockSpec((depth, w), lambda i, s: (0, pairs * i + s[0])),
            pl.BlockSpec((depth, n), lambda i, s: (0, 0)),
        ]
        out = pl.BlockSpec((w, n), lambda i, s: (i, 0))
        args = [lhs, rhs]
    else:
        grid, count = (n // cols,), quads
        ins = [
            pl.BlockSpec((depth, w), lambda i, s, q=q: (0, pairs * q + s[0])) for q in range(quads)
        ] + [
            pl.BlockSpec((1, depth, cols), lambda i, s: (i, 0, 0))
            if three
            else pl.BlockSpec((depth, cols), lambda i, s: (0, i))
        ]
        out = pl.BlockSpec((quads * w, cols), lambda i, s: (0, i))
        args = [lhs] * quads + [rhs]
    if extra:
        ins.append(out)
        args.append(add)
    total = quads * w
    return pl.pallas_call(
        functools.partial(grad_kernel, count, extra),
        out_shape=jax.ShapeDtypeStruct((total, n), BF),
        grid_spec=pltpu.PrefetchScalarGridSpec(
            num_scalar_prefetch=1, grid=grid, in_specs=ins, out_specs=out
        ),
        compiler_params=pltpu.CompilerParams(vmem_limit_bytes=48 << 20),
        cost_estimate=pl.CostEstimate(
            flops=2 * depth * total * n,
            bytes_accessed=2 * depth * (total + n) + (4 if extra else 2) * total * n,
            transcendentals=0,
        ),
        name="weight_grad",
    )(sel, *args)


def columns_kernel(sel_ref, a_ref, b_ref, own_ref, oth_ref):
    own_ref[...] = a_ref[...]
    oth_ref[...] = b_ref[...]


def split_columns(core, w, quads):
    model, wide = w.shape
    width = wide // 6 // quads
    at = lambda flip: lambda i, s: (
        0,
        (i // quads) * 2 * quads + 2 * (i % quads) + (1 - s[0] if flip else s[0]),
    )
    out = pl.BlockSpec((model, width), lambda i, s: (0, i))
    return pl.pallas_call(
        columns_kernel,
        out_shape=(jax.ShapeDtypeStruct((model, wide // 2), BF),) * 2,
        grid_spec=pltpu.PrefetchScalarGridSpec(
            num_scalar_prefetch=1,
            grid=(3 * quads,),
            in_specs=[pl.BlockSpec((model, width), at(False)), pl.BlockSpec((model, width), at(True))],
            out_specs=(out, out),
        ),
        compiler_params=pltpu.CompilerParams(vmem_limit_bytes=8 << 20),
        cost_estimate=pl.CostEstimate(flops=0, bytes_accessed=4 * model * wide, transcendentals=0),
        name="split_columns",
    )(core, w, w)


def chosen(sel_ref, own_ref, oth_ref):
    mine = pl.program_id(0) // 2 == sel_ref[0]
    return jnp.where(mine, own_ref[...].astype(F32), oth_ref[...].astype(F32))


def project_kernel(sel_ref, frac_ref, own_ref, oth_ref, vec_ref, w_ref, bias_ref, qkv_ref, start_ref):
    start = chosen(sel_ref, own_ref, oth_ref) + (frac_ref[0] * vec_ref[0:1, :] + vec_ref[1:2, :])
    start = start.astype(BF)
    start_ref[...] = start
    half = w_ref.shape[1] // 3
    out = dot(start, w_ref[...], NN) + bias_ref[...]
    qkv_ref[:, :half] = (out[:, :half] * (0.125 * LOG2E)).astype(BF)
    qkv_ref[:, half:] = out[:, half:].astype(BF)


def project(core, fraction, own, oth, vecs, w, bias):
    rows, model = own.shape
    br = rows // 2
    fixed = lambda shape: pl.BlockSpec(shape, lambda i, s: (0, 0))
    part = pl.BlockSpec((br, model), lambda i, s: (i % 2, 0))
    out = lambda w: pl.BlockSpec((br, w), lambda i, s: (i, 0))
    return pl.pallas_call(
        project_kernel,
        out_shape=(
            jax.ShapeDtypeStruct((2 * rows, w.shape[1]), BF),
            jax.ShapeDtypeStruct((2 * rows, model), BF),
        ),
        grid_spec=pltpu.PrefetchScalarGridSpec(
            num_scalar_prefetch=1,
            grid=(4,),
            in_specs=[
                pl.BlockSpec(memory_space=pltpu.SMEM),
                part,
                part,
                fixed(vecs.shape),
                fixed(w.shape),
                fixed(bias.shape),
            ],
            out_specs=(out(w.shape[1]), out(model)),
        ),
        compiler_params=pltpu.CompilerParams(vmem_limit_bytes=40 << 20),
        cost_estimate=pl.CostEstimate(
            flops=4 * rows * model * w.shape[1],
            bytes_accessed=4 * rows * (2 * model + w.shape[1]) + 2 * model * w.shape[1],
            transcendentals=0,
        ),
        name="project",
    )(core, fraction, own, oth, vecs, w, bias)


def context_grad_kernel(sel_ref, own_ref, oth_ref, w_ref, out_ref):
    rows = chosen(sel_ref, own_ref, oth_ref).astype(BF)
    out_ref[...] = dot(rows, w_ref[...].reshape(-1, w_ref.shape[-1]), NT).astype(BF)


def context_grad(core, own, oth, w_out):
    rows, model = own.shape
    br = rows // 2
    quads, _, w, _ = w_out.shape
    part = pl.BlockSpec((br, model), lambda i, s: (i % 2, 0))
    return pl.pallas_call(
        context_grad_kernel,
        out_shape=jax.ShapeDtypeStruct((2 * rows, quads * w), BF),
        grid_spec=pltpu.PrefetchScalarGridSpec(
            num_scalar_prefetch=1,
            grid=(4,),
            in_specs=[
                part,
                part,
                pl.BlockSpec((quads, 1, w, model), lambda i, s: (0, s[0], 0, 0)),
            ],
            out_specs=pl.BlockSpec((br, quads * w), lambda i, s: (i, 0)),
        ),
        compiler_params=pltpu.CompilerParams(vmem_limit_bytes=32 << 20),
        cost_estimate=pl.CostEstimate(
            flops=4 * rows * model * quads * w,
            bytes_accessed=4 * rows * (model + quads * w) + 2 * quads * w * model,
            transcendentals=0,
        ),
        name="context_grad",
    )(core, own, oth, w_out)


def out_grad_kernel(sel_ref, a0, b0, a1, b1, own_ref, oth_ref, out_ref):
    w = a0.shape[1]
    out_ref[:w, :] = (dot(a0[...], own_ref[...], TN) + dot(b0[...], oth_ref[...], TN)).astype(BF)
    out_ref[w:, :] = (dot(a1[...], own_ref[...], TN) + dot(b1[...], oth_ref[...], TN)).astype(BF)


def out_grad(core, contexts, own, oth):
    rows, model = own.shape
    w = contexts[0].shape[1]
    here = pl.BlockSpec((rows, w), lambda i, s: (s[0], 0))
    there = pl.BlockSpec((rows, w), lambda i, s: (1 - s[0], 0))
    full = pl.BlockSpec((rows, model), lambda i, s: (0, 0))
    return pl.pallas_call(
        out_grad_kernel,
        out_shape=jax.ShapeDtypeStruct((2 * w, model), BF),
        grid_spec=pltpu.PrefetchScalarGridSpec(
            num_scalar_prefetch=1,
            grid=(1,),
            in_specs=[here, there, here, there, full, full],
            out_specs=pl.BlockSpec((2 * w, model), lambda i, s: (0, 0)),
        ),
        compiler_params=pltpu.CompilerParams(vmem_limit_bytes=40 << 20),
        cost_estimate=pl.CostEstimate(
            flops=8 * rows * model * w, bytes_accessed=8 * rows * (model + w), transcendentals=0
        ),
        name="out_grad",
    )(core, contexts[0], contexts[0], contexts[1], contexts[1], own, oth)


def finish_kernel(sel_ref, base_ref, mine_ref, got_ref, wm0, wm1, wm2, wg0, wg1, wg2, out_ref, *rest):
    total = base_ref[...]
    for t, (wm, wg) in enumerate(((wm0, wg0), (wm1, wg1), (wm2, wg2))):
        total = total + dot(mine_ref[t], wm[...], NT)
        total = total + dot(got_ref[t], wg[...], NT)
    out_ref[...] = total.astype(out_ref.dtype)
    if rest:
        step = pl.program_id(0)

        @pl.when(step == 0)
        def _():
            rest[0][...] = jnp.zeros_like(rest[0])

        rest[0][...] += jnp.sum(total, axis=0, keepdims=True)


def add_start(core, base, grads, got, w_mine, w_got, group, last, br=288):
    rows, model = base.shape
    n = got.shape[2]
    steps = rows // br
    every = w_mine.shape[1] // (3 * n)
    cols = [pl.BlockSpec((model, n), lambda i, s, t=t: (0, t * every + group)) for t in range(3)]
    row = pl.BlockSpec((br, model), lambda i, s: (i, 0))
    outs = [jax.ShapeDtypeStruct((rows, model), BF if last else F32)]
    specs = [row]
    if last:
        outs.append(jax.ShapeDtypeStruct((1, model), F32))
        specs.append(pl.BlockSpec((1, model), lambda i, s: (0, 0)))
    return pl.pallas_call(
        finish_kernel,
        out_shape=tuple(outs),
        grid_spec=pltpu.PrefetchScalarGridSpec(
            num_scalar_prefetch=1,
            grid=(steps,),
            in_specs=[
                row,
                pl.BlockSpec((3, br, n), lambda i, s: (0, s[0] * steps + i, 0)),
                pl.BlockSpec((3, br, n), lambda i, s: (0, i, 0)),
                *cols,
                *cols,
            ],
            out_specs=tuple(specs),
        ),
        compiler_params=pltpu.CompilerParams(vmem_limit_bytes=40 << 20),
        cost_estimate=pl.CostEstimate(
            flops=12 * rows * n * model,
            bytes_accessed=8 * rows * model + 12 * n * (rows + model),
            transcendentals=0,
        ),
        name="add_start",
    )(core, base, grads, got, *(w_mine,) * 3, *(w_got,) * 3)


class Plan:
    def __init__(self, mesh):
        sizes = dict(mesh.shape)
        self.batch, self.depth = sizes["batch"], sizes["seq"]
        chips = self.batch // 2
        side = 1
        while side * side < chips:
            side *= 2
        self.nx, self.ny = side, chips // side

    def perm(self, target):
        pairs = []
        for y in range(self.ny):
            for x in range(self.nx):
                for c in range(2):
                    for z in range(self.depth):
                        to = target(y, x, c, z)
                        if to != (y, x, c, z):
                            pairs.append((self.index(y, x, c, z), self.index(*to)))
        return pairs

    def index(self, y, x, c, z):
        return ((y * self.nx + x) * 2 + c) * self.depth + z

    def send(self, value, target):
        return lax.ppermute(value, AXES, self.perm(target))

    def sibling(self, value):
        return self.send(value, lambda y, x, c, z: (y, x, 1 - c, z))


def pick(array, index, axis):
    return lax.dynamic_index_in_dim(array, index, axis, keepdims=False)


def tie(*values):
    return lax.optimization_barrier(values)


class Sum:
    def __init__(self, plan, terms, where, axes="yxhl"):
        self.plan, self.terms, self.axes = plan, terms, axes
        y, x, z = where
        self.where = {"y": y, "x": x, "h": z // 2, "l": z % 2}

    def send(self, axis):
        plan, terms = self.plan, self.terms
        self.axis, self.at = axis, self.axes.index(axis)
        self.axes = self.axes.replace(axis, "")
        size = {"x": plan.nx, "y": plan.ny}.get(axis, 2)
        here = self.where[axis]
        self.got = []
        for r in range(1, size):

            def target(y, x, c, z, r=r):
                at = {"y": y, "x": x, "h": z // 2, "l": z % 2}
                at[axis] = (at[axis] + r) % size
                return at["y"], at["x"], c, 2 * at["h"] + at["l"]

            self.got.append(plan.send(pick(terms, (here + r) % size, self.at), target))
        return self

    def add(self):
        total = pick(self.terms, self.where[self.axis], self.at).astype(F32)
        for got in self.got:
            total = total + got.astype(F32)
        self.terms = total.astype(self.terms.dtype) if self.axes else total
        return self.terms

    def hold(self, *others):
        self.terms, *rest = tie(self.terms, *others)
        return rest


def per_chip(
    plan,
    inputs,
    timesteps,
    segments,
    cotangent,
    w_qkv,
    b_query,
    b_value,
    w_out,
    b_out,
    ln1_gain,
    ln1_bias,
    w_up,
    b_up,
    w_down,
    b_down,
    ln2_gain,
    ln2_bias,
    w_time,
    b_time,
):
    local_len = inputs.shape[1]
    rows = 2 * local_len
    length = segments.shape[1]
    b = lax.axis_index("batch")
    z = lax.axis_index("seq")
    c, x, y = b % 2, (b // 2) % plan.nx, b // 2 // plan.nx
    part = z % 2
    where = (y, x, z)
    first = (segments[1, 0] == segments[1, 128 * 12]).astype(jnp.int32)
    which = lambda s: (first + s) % 2
    facts = jnp.concatenate(
        [segments[:, : 128 * 13 : 128], timesteps[:, None], jnp.zeros((2, 2), jnp.int32)], axis=1
    )
    facts = jnp.stack([pick(facts, which(0), 0), pick(facts, which(1), 0)])
    other_facts = plan.sibling(facts)
    facts = jnp.where(z // 2 == c, facts, other_facts)
    mine = pick(facts, z % 2, 0)
    marks = mine[:13]
    info = jnp.concatenate(
        [
            jnp.where(marks[:1] == marks[12:], 1, jnp.where(marks[12:] == marks[:1] + 12, 2, 0)),
            jnp.sum((marks[None, :] < marks[:, None]).astype(jnp.int32), axis=1),
            jnp.sum((marks[None, :] <= marks[:, None]).astype(jnp.int32), axis=1),
        ]
    )
    fraction = mine[13].astype(F32) / TSTEPS

    stays = z // 2 == c

    def exchange(parts):
        got = [
            plan.send(v, lambda y, x, c, z, j=j: (y, x, z // 2, 2 * c + (z + j) % 2))
            for j, v in enumerate(parts)
        ]
        return [(got[0], parts[0]), (got[1], None)]

    def arrived(got):
        return [jnp.where(stays, got[0][1], got[0][0]), got[1][0]]

    def gather_parts(array):
        return [pick(array, which((part + j) % 2), 0) for j in (0, 1)]

    def gather_end(got):
        got = arrived(got)
        return jnp.concatenate(
            [jnp.where(part == 0, got[0], got[1]), jnp.where(part == 0, got[1], got[0])], axis=0
        )

    def spread_parts(array):
        array = array.reshape(2, local_len, array.shape[-1])
        return [pick(array, (part + j) % 2, 0) for j in (0, 1)]

    def spread_end(got):
        got = arrived(got)
        swap = (part + first) % 2
        return jnp.stack(
            [jnp.where(swap == 0, got[0], got[1]), jnp.where(swap == 0, got[1], got[0])], axis=0
        )

    def whole(own, other):
        return jnp.where(c == 0, jnp.concatenate([own, other]), jnp.concatenate([other, own]))

    def halves(array, axis):
        shape = array.shape
        cut = shape[:axis] + (plan.ny * plan.nx, 2, -1) + shape[axis + 1 :]
        flat = shape[:axis] + (-1,) + shape[axis + 1 :]
        split = array.reshape(cut)
        return (
            pick(split, c, axis + 1).reshape(flat),
            pick(split, 1 - c, axis + 1).reshape(flat),
        )

    def blocks(array):
        return array.reshape(plan.ny, plan.nx, 2, 2, -1, array.shape[-1])

    model = inputs.shape[-1]
    half = model // 2
    quads = plan.ny * plan.nx
    core = jnp.stack([c]).astype(jnp.int32)
    away = 1 - core
    w_own, w_oth = split_columns(core, w_qkv, quads)
    bias = jnp.concatenate(
        [
            halves(b_query.astype(F32), 0)[0],
            jnp.zeros((half,), F32),
            halves(b_value.astype(F32), 0)[0],
        ]
    )
    w_out_four = w_out.reshape(quads, 2, -1, model)
    ahead = [range(0, quads // 2), range(quads // 2, quads)]
    groups = ahead
    own_inputs = gather_end(exchange(gather_parts(inputs)))
    vecs = jnp.stack(
        [v.astype(F32) for v in (w_time, b_time, b_out, ln1_gain, ln1_bias, b_down, ln2_gain, ln2_bias)]
    )
    cot_parts = gather_parts(cotangent)
    bias = bias[None]
    own_inputs, w_own, w_oth, vecs, info, bias, cot_parts = tie(
        own_inputs, w_own, w_oth, vecs, info, bias, cot_parts
    )
    sib_inputs = plan.sibling(own_inputs)
    cot_parts, sib_inputs = tie(cot_parts, sib_inputs)
    own_cotangent = gather_end(exchange(cot_parts))
    qkv, start_full = project(core, fraction[None], own_inputs, sib_inputs, vecs, w_own, bias)
    fwd = [attn_fwd(info, qkv, g.start, len(g)) for g in ahead]
    away_of = [
        plan.sibling(pick(f[0].reshape(2, rows, -1), 1 - c, 0)) for f in fwd
    ]
    result, normed_low, act, two_low, hid, grad_one, one_low, small_sums, up_sums = middle(
        core,
        fraction[None],
        own_inputs,
        [f[0] for f in fwd],
        away_of,
        own_cotangent,
        vecs,
        b_up.astype(F32)[None],
        w_out_four,
        w_up,
        w_down,
    )
    one_sib = plan.sibling(one_low)
    output_got = exchange(spread_parts(result))
    down_part = weight_grad(away, act, two_low, quads=quads)
    normed_low, down_part = tie(normed_low, down_part)
    down_got = plan.sibling(down_part)
    up_part = weight_grad(away, normed_low, hid, quads=quads)
    act, up_part = tie(act, up_part)
    up_got = plan.sibling(up_part)
    down_sum = weight_grad(core, act, two_low, down_got, quads=quads)
    normed_low, down_sum = tie(normed_low, down_sum)
    down = Sum(plan, blocks(down_sum), where).send("x")
    up_sum = weight_grad(core, normed_low, hid, up_got, quads=quads)
    one_low, one_sib, up_sum = tie(one_low, one_sib, up_sum)
    up = Sum(plan, blocks(up_sum), where).send("y")
    out_sum = out_grad(core, [f[0] for f in fwd], one_low, one_sib)
    one_low, one_sib, out_sum = tie(one_low, one_sib, out_sum)
    out = Sum(plan, blocks(out_sum), where).send("x")
    grad_context = context_grad(core, one_low, one_sib, w_out_four)

    def back(first, count, into=None):
        f = first // (quads // 2)
        start = ahead[f].start
        return attn_bwd(
            info,
            fwd[f][2],
            qkv,
            fwd[f][0],
            fwd[f][1],
            grad_context,
            first,
            count,
            first - start,
            quads // 2,
            first - start,
            into,
        )

    def away_rows(grads):
        return plan.sibling(pick(grads.reshape(3, 2, rows, -1), 1 - c, 1))

    def products(grads):
        cross_part = weight_grad(away, start_full, grads, quads=quads)
        grads, cross_part = tie(grads, cross_part)
        cross = plan.sibling(cross_part)
        keep = weight_grad(core, start_full, grads, quads=quads)
        return Sum(plan, blocks(cross), where), Sum(plan, blocks(keep), where)

    def settle(items, other):
        for item in items:
            item.got, other = tie(item.got, other)
            item.add()
            item.terms, other = tie(item.terms, other)
        return other

    grads, b_sum0 = back(0, quads // 2)
    got = away_rows(grads)
    output_got, grads = tie(output_got, grads)
    grads = settle([down, up, out], grads)
    down.send("y")
    up.send("x")
    out.send("y")
    cross0, keep0 = products(grads)
    got, cross0.terms, keep0.terms = tie(got, cross0.terms, keep0.terms)
    (grad_start,) = add_start(core, grad_one, grads, got, w_own, w_oth, 0, False)
    keep0.send("x")
    cross0.send("y")
    grad_context, grad_start = tie(grad_context, grad_start)
    grads, b_sum1 = back(quads // 2, quads // 4)
    grads = settle([down, up, out, keep0, cross0], grads)
    wide_rows = up.terms.shape[-2]
    slabs = [up.terms[..., i * model : (i + 1) * model] for i in range(up.terms.shape[-1] // model)]
    ffn = jnp.concatenate([down.terms, *slabs, out.terms], axis=2)
    ffn, grads = tie(ffn, grads)
    ffn = Sum(plan, ffn, where, "hl").send("l")
    keep0.send("y")
    cross0.send("x")
    grads, b_sum2 = back(quads // 2 + quads // 4, quads // 4, grads)
    got = away_rows(grads)
    grads = settle([ffn], grads)
    ffn.send("h")
    cross1, keep1 = products(grads)
    got, keep1.terms = tie(got, keep1.terms)
    keep1.send("x")
    cross1.send("y")
    grad_low, b_time_sum = add_start(core, grad_start, grads, got, w_own, w_oth, 1, True)
    in_parts, b_time_sum = tie(spread_parts(grad_low), b_time_sum)
    grad_inputs_got = exchange(in_parts)
    b_time_sum = settle([keep0, cross0, keep1, cross1], b_time_sum)
    ffn.got, b_time_sum = tie(ffn.got, b_time_sum)
    keep1.send("y")
    cross1.send("x")
    small_sums, up_sums, b_time_sum = tie(small_sums, up_sums, b_time_sum)
    b_sum = jnp.concatenate([b_sum0, b_sum1, b_sum2], axis=1)
    zero = jnp.zeros((quads, 2, half // quads), F32)

    def placed(v):
        return lax.dynamic_update_index_in_dim(zero, v.reshape(quads, half // quads), c, 1).reshape(-1)

    vectors = [small_sums[i] for i in range(6)]
    vectors += [placed(b_sum[0]), placed(b_sum[1]), fraction * b_time_sum[0], b_time_sum[0]]
    small = jnp.concatenate([v[:, None] for v in vectors] + [up_sums.reshape(model, -1)], axis=1)
    small_own, small_oth = halves(small, 0)
    small = Sum(plan, blocks(small_own + plan.sibling(small_oth)), where)
    small.send("x").add()
    small.send("y")
    keep1.got, cross1.got, small.got, grad_inputs_got = tie(
        keep1.got, cross1.got, small.got, grad_inputs_got
    )
    keep1.add()
    cross1.add()
    small.add()
    late = jnp.concatenate([i.terms for i in (keep0, cross0, keep1, cross1)], axis=3)
    late = Sum(plan, late, where, "hl").send("l")
    small.send("l")
    late.got, small.got = tie(late.got, small.got)
    late.add()
    small.add()
    late.send("h")
    small.send("h")
    small.add()
    small = small.terms
    late = late.add()
    wide = 3 * half // 2
    keeps = [late[:, :wide], late[:, 2 * wide : 3 * wide]]
    crosses = [late[:, wide : 2 * wide], late[:, 3 * wide : 4 * wide]]
    ffn = ffn.add()
    count = ffn.shape[0] - wide_rows * (len(slabs) + 1)
    sum_w_down, sum_w_out = ffn[:count], ffn[count + wide_rows * len(slabs) :]
    sum_w_up = jnp.concatenate(
        [ffn[count + i * wide_rows : count + (i + 1) * wide_rows] for i in range(len(slabs))], axis=1
    )
    output = spread_end(output_got)
    grad_inputs = spread_end(grad_inputs_got)
    split3 = lambda parts: jnp.concatenate(
        [p.reshape(p.shape[0], 3, len(g), -1) for p, g in zip(parts, groups)], axis=2
    )
    sum_own, sum_oth = split3(keeps), split3(crosses)
    pair = jnp.where(c == 0, jnp.stack([sum_own, sum_oth]), jnp.stack([sum_oth, sum_own]))
    sum_w_qkv = (
        pair.transpose(1, 2, 3, 0, 4).reshape(-1, 3 * model)
    )
    v = [small[:, i] for i in (6, 7, 0, 1, 2, 3, 4, 5, 8, 9)]
    return (
        output,
        grad_inputs,
        sum_w_qkv,
        v[0],
        v[1],
        sum_w_out,
        v[2],
        v[3],
        v[4],
        sum_w_up,
        small[:, 10:].reshape(-1),
        sum_w_down,
        v[5],
        v[6],
        v[7],
        v[8],
        v[9],
    )


def solution(mesh):
    placed = (
        P("batch", "seq", None),
        P("batch"),
        P("batch", None),
        P("batch", "seq", None),
        P(),
        P(),
        P(),
        P(),
        P(),
        P(),
        P(),
        P(),
        P(),
        P(),
        P(),
        P(),
        P(),
        P(),
        P(),
    )
    sizes = dict(mesh.shape)
    body = per_device
    if sizes["seq"] == 4 and sizes["batch"] % 2 == 0:
        body = functools.partial(per_chip, Plan(mesh))
    return jax.shard_map(
        body,
        mesh=mesh,
        in_specs=placed,
        out_specs=(
            P("batch", "seq", None),
            P("batch", "seq", None),
            P(("batch", "seq"), None),
            P(("batch", "seq")),
            P(("batch", "seq")),
            P(("batch", "seq"), None),
            P(("batch", "seq")),
            P(("batch", "seq")),
            P(("batch", "seq")),
            P(("batch", "seq"), None),
            P(("batch", "seq")),
            P(("batch", "seq"), None),
            P(("batch", "seq")),
            P(("batch", "seq")),
            P(("batch", "seq")),
            P(("batch", "seq")),
            P(("batch", "seq")),
        ),
        check_vma=False,
    )
```

```python
import functools

import jax
import jax.numpy as jnp
from jax import lax
from jax.experimental import pallas as pl
from jax.experimental.pallas import tpu as pltpu
from jax.sharding import PartitionSpec as P

D = 1024
HEADS = 16
TSTEPS = 5000
AXES = ("batch", "seq")


BF=jnp.bfloat16; F32=jnp.float32
NT=(((1,),(1,)),((),())); NN=(((1,),(0,)),((),())); TN=(((0,),(0,)),((),()))
def dot(a,b,d): return lax.dot_general(a,b,d,preferred_element_type=F32)
PHASE=1
FILLED=1664; PAD=64
def lanes(rows):
    return lax.broadcasted_iota(jnp.int32,(rows,128),1)
def parts3(x):
    a=x.astype(BF).astype(F32); r=x-a; b=r.astype(BF).astype(F32); c=r-b
    return a,b,c
def augment(base,h,x,lane):
    a,b,c=parts3(x)
    o=(1-h)*64
    f=base.astype(F32)
    f=jnp.where((lane>=o)&(lane<o+64),jnp.where(lane==o,a,jnp.where(lane==o+1,b,jnp.where(lane==o+2,c,0.0))),f)
    return f.astype(BF)
def ones3(base,h,lane,n=3):
    o=(1-h)*64
    f=base.astype(F32)
    f=jnp.where((lane>=o)&(lane<o+64),jnp.where(lane<o+n,1.0,0.0),f)
    return f.astype(BF)
def spread(base,h,x,lane):
    a=x.astype(BF).astype(F32); r=x-a; b=r.astype(BF).astype(F32); c=r-b
    o=(1-h)*64
    f=jnp.where(lane==o,a,jnp.where(lane==o+1,b,jnp.where(lane==o+2,c,0.0)))
    return jnp.where((lane//64)==h,base.astype(F32),f).astype(BF)
def fwd_tiles(tasks,lane):
    scores=[]
    for q,k,vs,keep in tasks:
        for h in (0,1):
            qh=jnp.where((lane//64)==h,q.astype(F32),0.0).astype(BF)
            s=dot(qh,k,NT)
            scores.append(s if keep is None else jnp.where(keep,s,-1e30))
    tops=[];outs=[]
    depth=PHASE
    n=len(scores)
    def soft(i):
        m=jnp.max(scores[i],axis=1,keepdims=True)
        tops.append(m)
        return jnp.exp2(scores[i]-m).astype(BF)
    ps=[]
    for i in range(n+depth):
        if i<n: ps.append(soft(i))
        if i>=depth: outs.append(dot(ps[i-depth],tasks[(i-depth)//2][2][(i-depth)%2],NN))
    done=[]
    for t,(q,_,_,_) in enumerate(tasks):
        os=[];augs=[]
        for h in (0,1):
            o=outs[2*t+h]
            os.append(o/pltpu.roll(o,64,1))
            augs.append(spread(q,h,-(tops[2*t+h]+jnp.log2(o)),lane))
        done.append((jnp.where(lane<64,os[0],os[1]),augs))
    return done
def fwd_store(refs,rows,o,augs):
    o_ref,ol_ref,qa_ref=refs
    o_ref[rows,:]=o.astype(BF)
    ol_ref[rows,:]=(o-o.astype(BF).astype(F32)).astype(BF)
    for h in (0,1): qa_ref[h,rows,:]=augs[h]
def fwd_kernel(bq,info,q_ref,k_ref,v_ref,*refs):
    *refs,vs_ref=refs
    single=info[0]==1
    @pl.when(single)
    def _():
        v=v_ref[0:FILLED,:]
        for h in (0,1): vs_ref[h,...]=ones3(v,h,lanes(FILLED),64)
        lq=lanes(bq)
        @pl.loop(0,FILLED//bq)
        def _(r):
            rows=pl.ds(pl.multiple_of(r*bq,bq),bq)
            (o,augs),=fwd_tiles([(q_ref[rows,:],k_ref[0:FILLED,:],(vs_ref[0],vs_ref[1]),None)],lq)
            fwd_store(refs,rows,o,augs)
    @pl.when(info[0]==2)
    def _():
        lq=lanes(128)
        each=[slice(i*128,i*128+128) for i in range(13)]
        tasks=[(q_ref[r,:],k_ref[r,:],[ones3(v_ref[r,:],h,lq,64) for h in (0,1)],None) for r in each]
        for r,(o,augs) in zip(each,fwd_tiles(tasks,lq)): fwd_store(refs,r,o,augs)
    @pl.when(info[0]==0)
    def _():
        col=lax.broadcasted_iota(jnp.int32,(128,512),1)
        lw=lanes(512); lq=lanes(128)
        @pl.loop(0,13)
        def _(i):
            lo=info[1+i]; hi=info[14+i]
            at=jnp.minimum(lo,9)
            window=pl.ds(pl.multiple_of(at*128,128),512)
            k=k_ref[window,:]; v=v_ref[window,:]
            vs=[ones3(v,h,lw,64) for h in (0,1)]
            keep=(col>=(lo-at)*128)&(col<(hi-at)*128)
            rows=pl.ds(pl.multiple_of(i*128,128),128)
            (o,augs),=fwd_tiles([(q_ref[rows,:],k,vs,keep)],lq)
            fwd_store(refs,rows,o,augs)
    rows=slice(FILLED,FILLED+PAD)
    lp=lanes(PAD)
    v=v_ref[rows,:]
    (o,augs),=fwd_tiles([(q_ref[rows,:],k_ref[rows,:],[ones3(v,h,lp,64) for h in (0,1)],None)],lp)
    fwd_store(refs,rows,o,augs)
def attn_fwd(info,qkv,first,count,bq=832):
    L,W3=qkv.shape; n=W3//384
    spec=lambda j: pl.BlockSpec((L,128),lambda p,s,j=j:(0,p+first+j*n))
    one=pl.BlockSpec((L,128),lambda p,s:(0,p))
    return pl.pallas_call(functools.partial(fwd_kernel,bq),
        out_shape=(jax.ShapeDtypeStruct((L,count*128),BF),)*2+(jax.ShapeDtypeStruct((2*count,L,128),BF),),
        grid_spec=pltpu.PrefetchScalarGridSpec(num_scalar_prefetch=1,grid=(count,),
            in_specs=[spec(0),spec(1),spec(2)],
            out_specs=(one,one,pl.BlockSpec((2,L,128),lambda p,s:(p,0,0))),
            scratch_shapes=[pltpu.VMEM((2,FILLED,128),BF)]),
        compiler_params=pltpu.CompilerParams(vmem_limit_bytes=50<<20),name="attn_forward",
        cost_estimate=pl.CostEstimate(flops=8*count*L*L*256,bytes_accessed=10*L*count*128,transcendentals=2*count*L*L))(info,qkv,qkv,qkv)
def deltas(g,o,ol,lane):
    prod=g.astype(F32)*(o.astype(F32)+ol.astype(F32))
    return [augment(g,h,-jnp.sum(jnp.where((lane//64)==h,prod,0.0),axis=1,keepdims=True),lane) for h in (0,1)]
def bwd_tiles(tasks,lane,turned=None):
    khs=[ones3(t[1],t[4],lane) for t in tasks]
    ps=[dot(kh,t[0],NT) for kh,t in zip(khs,tasks)]
    ds=[dot(ones3(t[2],t[4],lane),t[3],NT) for t in tasks]
    done=[]
    for kh,p,d,(qa,_,_,ga,h,keep) in zip(khs,ps,ds,tasks):
        p=jnp.exp2(p)
        if keep is not None: p=jnp.where(keep,p,0.0)
        d=(p*d).astype(BF)
        done.append((kh,p.astype(BF),d,qa,ga))
    back=lambda i,kh,d: dot(d,kh,TN) if turned is None else dot(turned[i*64:i*64+64,:],d,NN)
    return [(back(i,kh,d),dot(d,qa,NN),dot(p,ga,NN)) for i,(kh,p,d,qa,ga) in enumerate(done)]
LN2=0.6931471805599453
def both(a,lane): return jnp.where(lane<64,a[0],a[1])
def bwd_alone(each,lane,qa_ref,k_ref,v_ref,o_ref,ol_ref,g_ref,dq_ref,dk_ref,dv_ref):
    tasks=[]
    for r in each:
        gas=deltas(g_ref[r,:],o_ref[r,:],ol_ref[r,:],lane)
        tasks+=[(qa_ref[h,r,:],k_ref[r,:],v_ref[r,:],gas[h],h,None) for h in (0,1)]
    got=bwd_tiles(tasks,lane)
    for i,r in enumerate(each):
        x,y=got[2*i],got[2*i+1]
        dq_ref[r,:]=(both((x[0],y[0]),lane)*0.125).astype(BF)
        dk_ref[r,:]=(both((x[1],y[1]),lane)*LN2).astype(BF)
        dv_ref[r,:]=both((x[2],y[2]),lane).astype(BF)
def bwd_kernel(bk,joined,info,qa_ref,k_ref,v_ref,o_ref,ol_ref,g_ref,*rest):
    d_ref,sum_ref,acc,acc_k,acc_v,ga_ref=rest[1:] if joined else rest
    dq_ref,dk_ref,dv_ref=d_ref.at[0],d_ref.at[1],d_ref.at[2]
    tile_refs=(qa_ref,k_ref,v_ref,o_ref,ol_ref,g_ref,dq_ref,dk_ref,dv_ref)
    single=info[0]==1
    @pl.when(single)
    def _():
        lf=lanes(FILLED)
        gas=deltas(g_ref[0:FILLED,:],o_ref[0:FILLED,:],ol_ref[0:FILLED,:],lf)
        acc[...]=jnp.zeros_like(acc)
        lb=lanes(bk)
        ga_ref[0,...]=gas[0]; ga_ref[1,...]=gas[1]
        @pl.loop(0,FILLED//bk)
        def _(r):
            rows=pl.ds(pl.multiple_of(r*bk,bk),bk)
            k=k_ref[rows,:]; v=v_ref[rows,:]
            dks=[];dvs=[]
            got=bwd_tiles([(qa_ref[h,0:FILLED,:],k,v,ga_ref[h],h,None) for h in (0,1)],lb,k.astype(F32).T.astype(BF))
            for h in (0,1):
                dq,dk,dv=got[h]
                acc[h*64:h*64+64,:]+=dq
                dks.append(dk); dvs.append(dv)
            dk_ref[rows,:]=(both(dks,lb)*LN2).astype(BF)
            dv_ref[rows,:]=both(dvs,lb).astype(BF)
        dq_ref[0:FILLED,:]=(acc[...].T*0.125).astype(BF)
    @pl.when(info[0]==2)
    def _():
        lq=lanes(128)
        bwd_alone([slice(i*128,i*128+128) for i in range(13)],lq,*tile_refs)
    @pl.when(info[0]==0)
    def _():
        row=lax.broadcasted_iota(jnp.int32,(512,128),0)
        lw=lanes(512); lq=lanes(128)
        acc_k[...]=jnp.zeros_like(acc_k); acc_v[...]=jnp.zeros_like(acc_v)
        @pl.loop(0,13)
        def _(i):
            lo=info[1+i]; hi=info[14+i]
            at=jnp.minimum(lo,9)
            window=pl.ds(pl.multiple_of(at*128,128),512)
            k=k_ref[window,:]; v=v_ref[window,:]
            keep=(row>=(lo-at)*128)&(row<(hi-at)*128)
            rows=pl.ds(pl.multiple_of(i*128,128),128)
            gas=deltas(g_ref[rows,:],o_ref[rows,:],ol_ref[rows,:],lq)
            dqs=[]
            got=bwd_tiles([(qa_ref[h,rows,:],k,v,gas[h],h,keep) for h in (0,1)],lw)
            for h in (0,1):
                dq,dk,dv=got[h]
                dqs.append(dq)
                acc_k[h,window,:]+=dk
                acc_v[h,window,:]+=dv
            dq_ref[rows,:]=(both(dqs,lq)*0.125).astype(BF)
        lf=lanes(FILLED)
        dk_ref[0:FILLED,:]=(jnp.where(lf<64,acc_k[0],acc_k[1])*LN2).astype(BF)
        dv_ref[0:FILLED,:]=jnp.where(lf<64,acc_v[0],acc_v[1]).astype(BF)
    bwd_alone([slice(FILLED,FILLED+PAD)],lanes(PAD),*tile_refs)
    sum_ref[0:1,:]=jnp.sum(dq_ref[...].astype(F32),axis=0,keepdims=True)
    sum_ref[1:2,:]=jnp.sum(dv_ref[...].astype(F32),axis=0,keepdims=True)
def attn_bwd(info,qa,qkv,o,ol,g,first,count,inner,wide,at,into=None,bk=416):
    L,W3=qkv.shape; n=W3//384
    spec=lambda j: pl.BlockSpec((L,128),lambda p,s,j=j:(0,p+first+j*n))
    one=pl.BlockSpec((L,128),lambda p,s:(0,p))
    part=pl.BlockSpec((L,128),lambda p,s:(0,p+inner))
    every=pl.BlockSpec((L,128),lambda p,s:(0,p+first))
    return pl.pallas_call(functools.partial(bwd_kernel,bk,into is not None),
        input_output_aliases={} if into is None else {7:0},
        out_shape=(jax.ShapeDtypeStruct((3,L,wide*128),BF),jax.ShapeDtypeStruct((2,count*128),F32)),
        grid_spec=pltpu.PrefetchScalarGridSpec(num_scalar_prefetch=1,grid=(count,),
            in_specs=[pl.BlockSpec((2,L,128),lambda p,s:(p+inner,0,0)),spec(1),spec(2),part,part,every]+([] if into is None else [pl.BlockSpec(memory_space=pl.ANY)]),
            out_specs=(pl.BlockSpec((3,L,128),lambda p,s:(0,0,p+at)),pl.BlockSpec((2,128),lambda p,s:(0,p))),
            scratch_shapes=[pltpu.VMEM((128,FILLED),F32)]+[pltpu.VMEM((2,FILLED,128),F32)]*2+[pltpu.VMEM((2,FILLED,128),BF)]),
        compiler_params=pltpu.CompilerParams(vmem_limit_bytes=56<<20),name="attn_backward",
        cost_estimate=pl.CostEstimate(flops=20*count*L*L*256,bytes_accessed=16*L*count*128,transcendentals=2*count*L*L))(*((info,qa,qkv,qkv,o,ol,g) if into is None else (info,qa,qkv,qkv,o,ol,g,into)))


def gelu_exact(values):
    return jax.nn.gelu(values, approximate=False)


def norm_forward(values, gain, shift):
    centered = values - jnp.mean(values, axis=-1, keepdims=True)
    inverse = lax.rsqrt(jnp.mean(centered * centered, axis=-1, keepdims=True) + 1e-05)
    unit_part = centered * inverse
    return (unit_part * gain + shift, unit_part, inverse)


def norm_backward(grad_out, unit_part, inverse, gain):
    scaled = grad_out * gain
    centered = scaled - jnp.mean(scaled, axis=-1, keepdims=True)
    grad_in = inverse * (
        centered - unit_part * jnp.mean(scaled * unit_part, axis=-1, keepdims=True)
    )
    return (grad_in, jnp.sum(grad_out * unit_part, axis=0), jnp.sum(grad_out, axis=0))


def attention_forward(query_all, key_all, value_all, segments, head_dim):
    length, local_width = (query_all.shape[1], query_all.shape[2])
    head_count = local_width // head_dim
    block_len = length // 3
    score_scale = head_dim ** (-0.5)

    def per_sequence(pieces):
        queries, key_rows, value_rows, seq_ids = pieces
        key_heads = key_rows.reshape(length, head_count, head_dim)
        value_heads = value_rows.reshape(length, head_count, head_dim)

        def per_block(block_pieces):
            query_part, id_part = block_pieces
            query_heads = query_part.reshape(block_len, head_count, head_dim)
            scores = (
                jnp.einsum(
                    "qhd,khd->hqk", query_heads, key_heads, preferred_element_type=jnp.float32
                )
                * score_scale
            )
            masked = jnp.where(id_part[None, :, None] == seq_ids[None, None, :], scores, -1e30)
            maxima = jnp.max(masked, axis=-1, keepdims=True)
            exp_scores = jnp.exp(masked - maxima)
            totals = jnp.sum(exp_scores, axis=-1, keepdims=True)
            weights_low = (exp_scores / totals).astype(jnp.bfloat16)
            context = jnp.einsum(
                "hqk,khd->qhd", weights_low, value_heads, preferred_element_type=jnp.float32
            )
            return (
                context.astype(jnp.bfloat16).reshape(block_len, local_width),
                (maxima + jnp.log(totals))[..., 0],
            )

        contexts, logsums = lax.map(
            per_block, (queries.reshape(3, block_len, local_width), seq_ids.reshape(3, block_len))
        )
        return (contexts.reshape(length, local_width), logsums)

    return lax.map(per_sequence, (query_all, key_all, value_all, segments))


def attention_backward(query_all, key_all, value_all, segments, logsums, grad_all, head_dim):
    length, local_width = (query_all.shape[1], query_all.shape[2])
    head_count = local_width // head_dim
    block_len = length // 3
    score_scale = head_dim ** (-0.5)

    def per_sequence(pieces):
        queries, key_rows, value_rows, seq_ids, sum_rows, grad_rows = pieces
        key_heads = key_rows.reshape(length, head_count, head_dim)
        value_heads = value_rows.reshape(length, head_count, head_dim)

        def per_block(carry, block_pieces):
            key_total, value_total = carry
            query_part, id_part, sum_part, grad_part = block_pieces
            query_heads = query_part.reshape(block_len, head_count, head_dim)
            grad_heads = grad_part.reshape(block_len, head_count, head_dim)
            scores = (
                jnp.einsum(
                    "qhd,khd->hqk", query_heads, key_heads, preferred_element_type=jnp.float32
                )
                * score_scale
            )
            allowed = id_part[None, :, None] == seq_ids[None, None, :]
            prob_weights = jnp.where(allowed, jnp.exp(scores - sum_part[:, :, None]), 0.0)
            grad_probs = jnp.einsum(
                "qhd,khd->hqk", grad_heads, value_heads, preferred_element_type=jnp.float32
            )
            delta = jnp.sum(prob_weights * grad_probs, axis=-1, keepdims=True)
            grad_scores = (prob_weights * (grad_probs - delta)).astype(jnp.bfloat16)
            query_grad = (
                jnp.einsum(
                    "hqk,khd->qhd", grad_scores, key_heads, preferred_element_type=jnp.float32
                )
                * score_scale
            )
            key_total = (
                key_total
                + jnp.einsum(
                    "hqk,qhd->khd", grad_scores, query_heads, preferred_element_type=jnp.float32
                )
                * score_scale
            )
            value_total = value_total + jnp.einsum(
                "hqk,qhd->khd",
                prob_weights.astype(jnp.bfloat16),
                grad_heads,
                preferred_element_type=jnp.float32,
            )
            return (
                (key_total, value_total),
                query_grad.astype(jnp.bfloat16).reshape(block_len, local_width),
            )

        zero_heads = jnp.zeros((length, head_count, head_dim), jnp.float32)
        (key_total, value_total), query_grads = lax.scan(
            per_block,
            (zero_heads, zero_heads),
            (
                queries.reshape(3, block_len, local_width),
                seq_ids.reshape(3, block_len),
                sum_rows,
                grad_rows.reshape(3, block_len, local_width),
            ),
        )
        return (
            query_grads.reshape(length, local_width),
            key_total.astype(jnp.bfloat16).reshape(length, local_width),
            value_total.astype(jnp.bfloat16).reshape(length, local_width),
        )

    return lax.map(per_sequence, (query_all, key_all, value_all, segments, logsums, grad_all))


def per_device(
    inputs,
    timesteps,
    segments,
    cotangent,
    w_qkv,
    b_query,
    b_value,
    w_out,
    b_out,
    ln1_gain,
    ln1_bias,
    w_up,
    b_up,
    w_down,
    b_down,
    ln2_gain,
    ln2_bias,
    w_time,
    b_time,
):
    groups, local_len, model_width = inputs.shape
    row_count = groups * local_len
    head_dim = D // HEADS
    fraction = timesteps.astype(jnp.float32) / TSTEPS
    start_sum = (
        inputs.astype(jnp.float32)
        + fraction[:, None, None] * w_time.astype(jnp.float32)
        + b_time.astype(jnp.float32)
    )
    start_low = start_sum.astype(jnp.bfloat16)
    projected = jnp.einsum("bld,de->ble", start_low, w_qkv, preferred_element_type=jnp.float32)
    query_low = (projected[..., :model_width] + b_query.astype(jnp.float32)).astype(jnp.bfloat16)
    key_low = projected[..., model_width : 2 * model_width].astype(jnp.bfloat16)
    value_low = (projected[..., 2 * model_width :] + b_value.astype(jnp.float32)).astype(
        jnp.bfloat16
    )
    query_all, key_all, value_all = (
        lax.all_to_all(query_low, "seq", split_axis=2, concat_axis=1, tiled=True),
        lax.all_to_all(key_low, "seq", split_axis=2, concat_axis=1, tiled=True),
        lax.all_to_all(value_low, "seq", split_axis=2, concat_axis=1, tiled=True),
    )
    context_heads, logsums = attention_forward(query_all, key_all, value_all, segments, head_dim)
    context = lax.all_to_all(context_heads, "seq", split_axis=1, concat_axis=2, tiled=True)
    context_rows = context.reshape(row_count, model_width)
    start_rows = start_sum.reshape(row_count, model_width)
    residual_one = (
        start_rows
        + jnp.dot(context_rows, w_out, preferred_element_type=jnp.float32)
        + b_out.astype(jnp.float32)
    )
    normed, unit_one, inverse_one = norm_forward(
        residual_one, ln1_gain.astype(jnp.float32), ln1_bias.astype(jnp.float32)
    )
    normed_low = normed.astype(jnp.bfloat16)
    hidden_pre = jnp.dot(normed_low, w_up, preferred_element_type=jnp.float32) + b_up.astype(
        jnp.float32
    )
    activated, gelu_pull = jax.vjp(gelu_exact, hidden_pre)
    activated_low = activated.astype(jnp.bfloat16)
    residual_two = (
        normed
        + jnp.dot(activated_low, w_down, preferred_element_type=jnp.float32)
        + b_down.astype(jnp.float32)
    )
    result, unit_two, inverse_two = norm_forward(
        residual_two, ln2_gain.astype(jnp.float32), ln2_bias.astype(jnp.float32)
    )
    output = result.astype(jnp.bfloat16).reshape(groups, local_len, model_width)
    grad_result = cotangent.reshape(row_count, model_width).astype(jnp.float32)
    grad_two, grad_ln2_gain, grad_ln2_bias = norm_backward(
        grad_result, unit_two, inverse_two, ln2_gain.astype(jnp.float32)
    )
    grad_b_down = jnp.sum(grad_two, axis=0)
    grad_two_low = grad_two.astype(jnp.bfloat16)
    grad_w_down = jnp.einsum(
        "rf,rd->fd", activated_low, grad_two_low, preferred_element_type=jnp.float32
    )
    grad_activated = jnp.einsum(
        "rd,fd->rf", grad_two_low, w_down, preferred_element_type=jnp.float32
    )
    grad_hidden = gelu_pull(grad_activated)[0]
    grad_b_up = jnp.sum(grad_hidden, axis=0)
    grad_hidden_low = grad_hidden.astype(jnp.bfloat16)
    grad_w_up = jnp.einsum(
        "rd,rf->df", normed_low, grad_hidden_low, preferred_element_type=jnp.float32
    )
    grad_normed = grad_two + jnp.einsum(
        "rf,df->rd", grad_hidden_low, w_up, preferred_element_type=jnp.float32
    )
    grad_one, grad_ln1_gain, grad_ln1_bias = norm_backward(
        grad_normed, unit_one, inverse_one, ln1_gain.astype(jnp.float32)
    )
    grad_b_out = jnp.sum(grad_one, axis=0)
    grad_one_low = grad_one.astype(jnp.bfloat16)
    grad_w_out = jnp.einsum(
        "rd,re->de", context_rows, grad_one_low, preferred_element_type=jnp.float32
    )
    grad_context = (
        jnp.einsum("re,de->rd", grad_one_low, w_out, preferred_element_type=jnp.float32)
        .astype(jnp.bfloat16)
        .reshape(groups, local_len, model_width)
    )
    grad_context_heads = lax.all_to_all(
        grad_context, "seq", split_axis=2, concat_axis=1, tiled=True
    )
    query_grads, key_grads, value_grads = attention_backward(
        query_all, key_all, value_all, segments, logsums, grad_context_heads, head_dim
    )
    grad_query, grad_key, grad_value = (
        lax.all_to_all(query_grads, "seq", split_axis=1, concat_axis=2, tiled=True),
        lax.all_to_all(key_grads, "seq", split_axis=1, concat_axis=2, tiled=True),
        lax.all_to_all(value_grads, "seq", split_axis=1, concat_axis=2, tiled=True),
    )
    grad_projected = jnp.concatenate((grad_query, grad_key, grad_value), axis=2).reshape(
        row_count, 3 * model_width
    )
    grad_w_qkv = jnp.einsum(
        "rd,re->de",
        start_low.reshape(row_count, model_width),
        grad_projected,
        preferred_element_type=jnp.float32,
    )
    grad_b_query = jnp.sum(grad_query.astype(jnp.float32), axis=(0, 1))
    grad_b_value = jnp.sum(grad_value.astype(jnp.float32), axis=(0, 1))
    grad_start = grad_one + jnp.einsum(
        "re,de->rd", grad_projected, w_qkv, preferred_element_type=jnp.float32
    )
    grad_inputs = grad_start.astype(jnp.bfloat16).reshape(groups, local_len, model_width)
    per_sequence_grad = jnp.sum(grad_start.reshape(groups, local_len, model_width), axis=1)
    grad_w_time = jnp.einsum("g,gd->d", fraction, per_sequence_grad)
    grad_b_time = jnp.sum(per_sequence_grad, axis=0)
    (
        sum_w_qkv,
        sum_b_query,
        sum_b_value,
        sum_w_out,
        sum_b_out,
        sum_ln1_gain,
        sum_ln1_bias,
        sum_w_up,
        sum_b_up,
        sum_w_down,
        sum_b_down,
        sum_ln2_gain,
        sum_ln2_bias,
        sum_w_time,
        sum_b_time,
    ) = (
        lax.psum_scatter(grad_w_qkv, ("batch", "seq"), scatter_dimension=0, tiled=True),
        lax.psum_scatter(grad_b_query, ("batch", "seq"), scatter_dimension=0, tiled=True),
        lax.psum_scatter(grad_b_value, ("batch", "seq"), scatter_dimension=0, tiled=True),
        lax.psum_scatter(grad_w_out, ("batch", "seq"), scatter_dimension=0, tiled=True),
        lax.psum_scatter(grad_b_out, ("batch", "seq"), scatter_dimension=0, tiled=True),
        lax.psum_scatter(grad_ln1_gain, ("batch", "seq"), scatter_dimension=0, tiled=True),
        lax.psum_scatter(grad_ln1_bias, ("batch", "seq"), scatter_dimension=0, tiled=True),
        lax.psum_scatter(grad_w_up, ("batch", "seq"), scatter_dimension=0, tiled=True),
        lax.psum_scatter(grad_b_up, ("batch", "seq"), scatter_dimension=0, tiled=True),
        lax.psum_scatter(grad_w_down, ("batch", "seq"), scatter_dimension=0, tiled=True),
        lax.psum_scatter(grad_b_down, ("batch", "seq"), scatter_dimension=0, tiled=True),
        lax.psum_scatter(grad_ln2_gain, ("batch", "seq"), scatter_dimension=0, tiled=True),
        lax.psum_scatter(grad_ln2_bias, ("batch", "seq"), scatter_dimension=0, tiled=True),
        lax.psum_scatter(grad_w_time, ("batch", "seq"), scatter_dimension=0, tiled=True),
        lax.psum_scatter(grad_b_time, ("batch", "seq"), scatter_dimension=0, tiled=True),
    )
    return (
        output,
        grad_inputs,
        sum_w_qkv,
        sum_b_query,
        sum_b_value,
        sum_w_out,
        sum_b_out,
        sum_ln1_gain,
        sum_ln1_bias,
        sum_w_up,
        sum_b_up,
        sum_w_down,
        sum_b_down,
        sum_ln2_gain,
        sum_ln2_bias,
        sum_w_time,
        sum_b_time,
    )


SLOPE = F32
PIECES = 8
LOG2E = 1.4426950408889634


def layer_norm(values):
    centered = values - jnp.mean(values, axis=1, keepdims=True)
    inverse = lax.rsqrt(jnp.mean(centered * centered, axis=1, keepdims=True) + 1e-05)
    return centered * inverse, inverse


def layer_norm_back(scaled, unit_part, inverse):
    return inverse * (
        scaled
        - jnp.mean(scaled, axis=1, keepdims=True)
        - unit_part * jnp.mean(scaled * unit_part, axis=1, keepdims=True)
    )


def gelu_pair(v):
    bell = jnp.exp2(v * v * (-0.5 * LOG2E))
    base = 1.0 + 0.2316418882663604 * jnp.abs(v)
    t = pltpu.reciprocal(base, approx=True)
    t = t * (2.0 - base * t)
    tail = t * (
        0.127414796
        + t * (-0.142248368 + t * (0.7107068705 + t * (-0.7265760135 + t * 0.5307027145)))
    )
    tail = tail * bell
    cover = jnp.where(v >= 0, 1.0 - tail, tail)
    return v * cover, cover + v * bell * 0.3989422804014327


def middle_kernel(
    fc,
    sel_ref,
    frac_ref,
    inp_ref,
    ctx_a0_ref,
    ctx_a1_ref,
    ctx_b0_ref,
    ctx_b1_ref,
    cot_ref,
    vec_ref,
    b_up_ref,
    wo_a_ref,
    wo_b_ref,
    w_up_hbm,
    w_down_hbm,
    out_ref,
    norm_ref,
    act_ref,
    two_ref,
    hid_ref,
    one_ref,
    onel_ref,
    small_ref,
    smallup_ref,
    w_up,
    w_down,
    slope,
    sems,
):
    step = pl.program_id(0)
    def pieces(i, source, target):
        size = source.shape[0] // PIECES
        return [
            pltpu.make_async_copy(
                source.at[pl.ds(j * size, size)],
                target.at[pl.ds(j * size, size)],
                sems.at[i * PIECES + j],
            )
            for j in range(PIECES)
        ]

    copies = pieces(0, w_up_hbm, w_up) + pieces(1, w_down_hbm, w_down)

    @pl.when(step == 0)
    def _():
        for copy in copies:
            copy.start()
        small_ref[...] = jnp.zeros_like(small_ref)
        smallup_ref[...] = jnp.zeros_like(smallup_ref)

    vec = lambda i: vec_ref[i : i + 1, :]
    start = inp_ref[...].astype(F32) + (frac_ref[0] * vec(0) + vec(1))
    residual = (
        start
        + dot(jnp.concatenate([ctx_a0_ref[...], ctx_a1_ref[...]], axis=1), wo_a_ref[...].reshape(-1, wo_a_ref.shape[-1]), NN)
        + dot(jnp.concatenate([ctx_b0_ref[...], ctx_b1_ref[...]], axis=1), wo_b_ref[...].reshape(-1, wo_b_ref.shape[-1]), NN)
        + vec(2)
    )
    unit_one, inverse_one = layer_norm(residual)
    normed = unit_one * vec(3) + vec(4)
    low = normed.astype(BF)
    norm_ref[...] = low

    @pl.when(step == 0)
    def _():
        for copy in copies:
            copy.wait()

    width = w_up.shape[1]
    total = normed + vec(5)
    for f in range(0, width, fc):
        cols = slice(f, f + fc)
        v = dot(low, w_up[:, cols], NN) + b_up_ref[:, cols]
        a, g = gelu_pair(v)
        a = a.astype(BF)
        act_ref[:, cols] = a
        slope[:, cols] = g.astype(slope.dtype)
        total = total + dot(a, w_down[cols, :], NN)
    unit_two, inverse_two = layer_norm(total)
    out_ref[...] = (unit_two * vec(6) + vec(7)).astype(BF)
    cot = cot_ref[...].astype(F32)
    two = layer_norm_back(cot * vec(6), unit_two, inverse_two)
    add = lambda v: jnp.sum(v, axis=0, keepdims=True)
    small_ref[3:4, :] += add(two)
    small_ref[4:5, :] += add(cot * unit_two)
    small_ref[5:6, :] += add(cot)
    two_low = two.astype(BF)
    two_ref[...] = two_low
    total = two
    for f in range(0, width, fc):
        cols = slice(f, f + fc)
        d = dot(two_low, w_down[cols, :], NT) * slope[:, cols].astype(F32)
        smallup_ref[:, cols] += add(d)
        d = d.astype(BF)
        hid_ref[:, cols] = d
        total = total + dot(d, w_up[:, cols], NT)
    small_ref[1:2, :] += add(total * unit_one)
    small_ref[2:3, :] += add(total)
    one = layer_norm_back(total * vec(3), unit_one, inverse_one)
    small_ref[0:1, :] += add(one)
    one_ref[...] = one
    onel_ref[...] = one.astype(BF)


def middle(core, fraction, inp, ctx_a, ctx_b, cot, vecs, b_up, w_out, w_up, w_down, br=288, fc=2048):
    rows, model = inp.shape
    width = w_up.shape[1]
    half = model // 2
    quads = w_out.shape[0]
    row = lambda w: pl.BlockSpec((br, w), lambda i, s: (i, 0))
    fixed = lambda shape: pl.BlockSpec(shape, lambda i, s: (0,) * len(shape))
    here = pl.BlockSpec((br, half // 2), lambda i, s: (s[0] * (rows // br) + i, 0))
    wo = lambda flip: pl.BlockSpec(
        (quads, 1, model // quads // 2, model),
        (lambda i, s: (0, s[0], 0, 0)) if not flip else (lambda i, s: (0, 1 - s[0], 0, 0)),
    )
    out = lambda w, t: jax.ShapeDtypeStruct((rows, w), t)
    return pl.pallas_call(
        functools.partial(middle_kernel, fc),
        out_shape=(
            out(model, BF),
            out(model, BF),
            out(width, BF),
            out(model, BF),
            out(width, BF),
            out(model, F32),
            out(model, BF),
            jax.ShapeDtypeStruct((8, model), F32),
            jax.ShapeDtypeStruct((1, width), F32),
        ),
        grid_spec=pltpu.PrefetchScalarGridSpec(
            num_scalar_prefetch=1,
            grid=(rows // br,),
            in_specs=[
                pl.BlockSpec(memory_space=pltpu.SMEM),
                row(model),
                here,
                here,
                row(half // 2),
                row(half // 2),
                row(model),
                fixed((8, model)),
                fixed((1, width)),
                wo(False),
                wo(True),
                pl.BlockSpec(memory_space=pl.ANY),
                pl.BlockSpec(memory_space=pl.ANY),
            ],
            out_specs=(
                row(model),
                row(model),
                row(width),
                row(model),
                row(width),
                row(model),
                row(model),
                fixed((8, model)),
                fixed((1, width)),
            ),
            scratch_shapes=[
                pltpu.VMEM(w_up.shape, BF),
                pltpu.VMEM(w_down.shape, BF),
                pltpu.VMEM((br, width), SLOPE),
                pltpu.SemaphoreType.DMA((2 * PIECES,)),
            ],
        ),
        compiler_params=pltpu.CompilerParams(vmem_limit_bytes=60 << 20),
        cost_estimate=pl.CostEstimate(
            flops=4 * rows * model * (model // 2 + 2 * width),
            bytes_accessed=4 * model * width + rows * (16 * model + 4 * width),
            transcendentals=rows * width * 2,
        ),
        name="middle",
    )(core, fraction, inp, *ctx_a, *ctx_b, cot, vecs, b_up, w_out, w_out, w_up, w_down)


def grad_kernel(count, extra, *refs):
    lhs = [r[...] for r in refs[1 : 1 + count]]
    rhs_ref = refs[1 + count]
    out_ref = refs[-1]
    left = lhs[0] if count == 1 else jnp.concatenate(lhs, axis=1)
    right = rhs_ref[0] if len(rhs_ref.shape) == 3 else rhs_ref[...]
    total = dot(left, right, TN)
    if extra:
        total = total + refs[2 + count][...].astype(F32)
    out_ref[...] = total.astype(BF)


def weight_grad(sel, lhs, rhs, add=None, cols=1024, quads=4, pairs=2):
    depth, width = lhs.shape
    three = rhs.ndim == 3
    n = rhs.shape[0] * rhs.shape[2] if three else rhs.shape[1]
    cols = rhs.shape[2] if three else cols
    w = width // (quads * pairs)
    extra = add is not None
    if w >= 512:
        grid, count = (quads,), 1
        ins = [
            pl.BlockSpec((depth, w), lambda i, s: (0, pairs * i + s[0])),
            pl.BlockSpec((depth, n), lambda i, s: (0, 0)),
        ]
        out = pl.BlockSpec((w, n), lambda i, s: (i, 0))
        args = [lhs, rhs]
    else:
        grid, count = (n // cols,), quads
        ins = [
            pl.BlockSpec((depth, w), lambda i, s, q=q: (0, pairs * q + s[0])) for q in range(quads)
        ] + [
            pl.BlockSpec((1, depth, cols), lambda i, s: (i, 0, 0))
            if three
            else pl.BlockSpec((depth, cols), lambda i, s: (0, i))
        ]
        out = pl.BlockSpec((quads * w, cols), lambda i, s: (0, i))
        args = [lhs] * quads + [rhs]
    if extra:
        ins.append(out)
        args.append(add)
    total = quads * w
    return pl.pallas_call(
        functools.partial(grad_kernel, count, extra),
        out_shape=jax.ShapeDtypeStruct((total, n), BF),
        grid_spec=pltpu.PrefetchScalarGridSpec(
            num_scalar_prefetch=1, grid=grid, in_specs=ins, out_specs=out
        ),
        compiler_params=pltpu.CompilerParams(vmem_limit_bytes=48 << 20),
        cost_estimate=pl.CostEstimate(
            flops=2 * depth * total * n,
            bytes_accessed=2 * depth * (total + n) + (4 if extra else 2) * total * n,
            transcendentals=0,
        ),
        name="weight_grad",
    )(sel, *args)


def columns_kernel(sel_ref, a_ref, b_ref, own_ref, oth_ref):
    own_ref[...] = a_ref[...]
    oth_ref[...] = b_ref[...]


def split_columns(core, w, quads):
    model, wide = w.shape
    width = wide // 6 // quads
    at = lambda flip: lambda i, s: (
        0,
        (i // quads) * 2 * quads + 2 * (i % quads) + (1 - s[0] if flip else s[0]),
    )
    out = pl.BlockSpec((model, width), lambda i, s: (0, i))
    return pl.pallas_call(
        columns_kernel,
        out_shape=(jax.ShapeDtypeStruct((model, wide // 2), BF),) * 2,
        grid_spec=pltpu.PrefetchScalarGridSpec(
            num_scalar_prefetch=1,
            grid=(3 * quads,),
            in_specs=[pl.BlockSpec((model, width), at(False)), pl.BlockSpec((model, width), at(True))],
            out_specs=(out, out),
        ),
        compiler_params=pltpu.CompilerParams(vmem_limit_bytes=8 << 20),
        cost_estimate=pl.CostEstimate(flops=0, bytes_accessed=4 * model * wide, transcendentals=0),
        name="split_columns",
    )(core, w, w)


def chosen(sel_ref, own_ref, oth_ref):
    mine = pl.program_id(0) // 2 == sel_ref[0]
    return jnp.where(mine, own_ref[...].astype(F32), oth_ref[...].astype(F32))


def project_kernel(sel_ref, frac_ref, own_ref, oth_ref, vec_ref, w_ref, bias_ref, qkv_ref, start_ref):
    start = chosen(sel_ref, own_ref, oth_ref) + (frac_ref[0] * vec_ref[0:1, :] + vec_ref[1:2, :])
    start = start.astype(BF)
    start_ref[...] = start
    half = w_ref.shape[1] // 3
    out = dot(start, w_ref[...], NN) + bias_ref[...]
    qkv_ref[:, :half] = (out[:, :half] * (0.125 * LOG2E)).astype(BF)
    qkv_ref[:, half:] = out[:, half:].astype(BF)


def project(core, fraction, own, oth, vecs, w, bias):
    rows, model = own.shape
    br = rows // 2
    fixed = lambda shape: pl.BlockSpec(shape, lambda i, s: (0, 0))
    part = pl.BlockSpec((br, model), lambda i, s: (i % 2, 0))
    out = lambda w: pl.BlockSpec((br, w), lambda i, s: (i, 0))
    return pl.pallas_call(
        project_kernel,
        out_shape=(
            jax.ShapeDtypeStruct((2 * rows, w.shape[1]), BF),
            jax.ShapeDtypeStruct((2 * rows, model), BF),
        ),
        grid_spec=pltpu.PrefetchScalarGridSpec(
            num_scalar_prefetch=1,
            grid=(4,),
            in_specs=[
                pl.BlockSpec(memory_space=pltpu.SMEM),
                part,
                part,
                fixed(vecs.shape),
                fixed(w.shape),
                fixed(bias.shape),
            ],
            out_specs=(out(w.shape[1]), out(model)),
        ),
        compiler_params=pltpu.CompilerParams(vmem_limit_bytes=40 << 20),
        cost_estimate=pl.CostEstimate(
            flops=4 * rows * model * w.shape[1],
            bytes_accessed=4 * rows * (2 * model + w.shape[1]) + 2 * model * w.shape[1],
            transcendentals=0,
        ),
        name="project",
    )(core, fraction, own, oth, vecs, w, bias)


def context_grad_kernel(sel_ref, own_ref, oth_ref, w_ref, out_ref):
    rows = chosen(sel_ref, own_ref, oth_ref).astype(BF)
    out_ref[...] = dot(rows, w_ref[...].reshape(-1, w_ref.shape[-1]), NT).astype(BF)


def context_grad(core, own, oth, w_out):
    rows, model = own.shape
    br = rows // 2
    quads, _, w, _ = w_out.shape
    part = pl.BlockSpec((br, model), lambda i, s: (i % 2, 0))
    return pl.pallas_call(
        context_grad_kernel,
        out_shape=jax.ShapeDtypeStruct((2 * rows, quads * w), BF),
        grid_spec=pltpu.PrefetchScalarGridSpec(
            num_scalar_prefetch=1,
            grid=(4,),
            in_specs=[
                part,
                part,
                pl.BlockSpec((quads, 1, w, model), lambda i, s: (0, s[0], 0, 0)),
            ],
            out_specs=pl.BlockSpec((br, quads * w), lambda i, s: (i, 0)),
        ),
        compiler_params=pltpu.CompilerParams(vmem_limit_bytes=32 << 20),
        cost_estimate=pl.CostEstimate(
            flops=4 * rows * model * quads * w,
            bytes_accessed=4 * rows * (model + quads * w) + 2 * quads * w * model,
            transcendentals=0,
        ),
        name="context_grad",
    )(core, own, oth, w_out)


def out_grad_kernel(sel_ref, a0, b0, a1, b1, own_ref, oth_ref, out_ref):
    w = a0.shape[1]
    out_ref[:w, :] = (dot(a0[...], own_ref[...], TN) + dot(b0[...], oth_ref[...], TN)).astype(BF)
    out_ref[w:, :] = (dot(a1[...], own_ref[...], TN) + dot(b1[...], oth_ref[...], TN)).astype(BF)


def out_grad(core, contexts, own, oth):
    rows, model = own.shape
    w = contexts[0].shape[1]
    here = pl.BlockSpec((rows, w), lambda i, s: (s[0], 0))
    there = pl.BlockSpec((rows, w), lambda i, s: (1 - s[0], 0))
    full = pl.BlockSpec((rows, model), lambda i, s: (0, 0))
    return pl.pallas_call(
        out_grad_kernel,
        out_shape=jax.ShapeDtypeStruct((2 * w, model), BF),
        grid_spec=pltpu.PrefetchScalarGridSpec(
            num_scalar_prefetch=1,
            grid=(1,),
            in_specs=[here, there, here, there, full, full],
            out_specs=pl.BlockSpec((2 * w, model), lambda i, s: (0, 0)),
        ),
        compiler_params=pltpu.CompilerParams(vmem_limit_bytes=40 << 20),
        cost_estimate=pl.CostEstimate(
            flops=8 * rows * model * w, bytes_accessed=8 * rows * (model + w), transcendentals=0
        ),
        name="out_grad",
    )(core, contexts[0], contexts[0], contexts[1], contexts[1], own, oth)


def finish_kernel(sel_ref, base_ref, mine_ref, got_ref, wm0, wm1, wm2, wg0, wg1, wg2, out_ref, *rest):
    total = base_ref[...]
    for t, (wm, wg) in enumerate(((wm0, wg0), (wm1, wg1), (wm2, wg2))):
        total = total + dot(mine_ref[t], wm[...], NT)
        total = total + dot(got_ref[t], wg[...], NT)
    out_ref[...] = total.astype(out_ref.dtype)
    if rest:
        step = pl.program_id(0)

        @pl.when(step == 0)
        def _():
            rest[0][...] = jnp.zeros_like(rest[0])

        rest[0][...] += jnp.sum(total, axis=0, keepdims=True)


def add_start(core, base, grads, got, w_mine, w_got, group, last, br=288):
    rows, model = base.shape
    n = got.shape[2]
    steps = rows // br
    every = w_mine.shape[1] // (3 * n)
    cols = [pl.BlockSpec((model, n), lambda i, s, t=t: (0, t * every + group)) for t in range(3)]
    row = pl.BlockSpec((br, model), lambda i, s: (i, 0))
    outs = [jax.ShapeDtypeStruct((rows, model), BF if last else F32)]
    specs = [row]
    if last:
        outs.append(jax.ShapeDtypeStruct((1, model), F32))
        specs.append(pl.BlockSpec((1, model), lambda i, s: (0, 0)))
    return pl.pallas_call(
        finish_kernel,
        out_shape=tuple(outs),
        grid_spec=pltpu.PrefetchScalarGridSpec(
            num_scalar_prefetch=1,
            grid=(steps,),
            in_specs=[
                row,
                pl.BlockSpec((3, br, n), lambda i, s: (0, s[0] * steps + i, 0)),
                pl.BlockSpec((3, br, n), lambda i, s: (0, i, 0)),
                *cols,
                *cols,
            ],
            out_specs=tuple(specs),
        ),
        compiler_params=pltpu.CompilerParams(vmem_limit_bytes=40 << 20),
        cost_estimate=pl.CostEstimate(
            flops=12 * rows * n * model,
            bytes_accessed=8 * rows * model + 12 * n * (rows + model),
            transcendentals=0,
        ),
        name="add_start",
    )(core, base, grads, got, *(w_mine,) * 3, *(w_got,) * 3)


class Plan:
    def __init__(self, mesh):
        sizes = dict(mesh.shape)
        self.batch, self.depth = sizes["batch"], sizes["seq"]
        chips = self.batch // 2
        side = 1
        while side * side < chips:
            side *= 2
        self.nx, self.ny = side, chips // side

    def perm(self, target):
        pairs = []
        for y in range(self.ny):
            for x in range(self.nx):
                for c in range(2):
                    for z in range(self.depth):
                        to = target(y, x, c, z)
                        if to != (y, x, c, z):
                            pairs.append((self.index(y, x, c, z), self.index(*to)))
        return pairs

    def index(self, y, x, c, z):
        return ((y * self.nx + x) * 2 + c) * self.depth + z

    def send(self, value, target):
        return lax.ppermute(value, AXES, self.perm(target))

    def sibling(self, value):
        return self.send(value, lambda y, x, c, z: (y, x, 1 - c, z))


def pick(array, index, axis):
    return lax.dynamic_index_in_dim(array, index, axis, keepdims=False)


def tie(*values):
    return lax.optimization_barrier(values)


class Sum:
    def __init__(self, plan, terms, where, axes="yxhl"):
        self.plan, self.terms, self.axes = plan, terms, axes
        y, x, z = where
        self.where = {"y": y, "x": x, "h": z // 2, "l": z % 2}

    def send(self, axis):
        plan, terms = self.plan, self.terms
        self.axis, self.at = axis, self.axes.index(axis)
        self.axes = self.axes.replace(axis, "")
        size = {"x": plan.nx, "y": plan.ny}.get(axis, 2)
        here = self.where[axis]
        self.got = []
        for r in range(1, size):

            def target(y, x, c, z, r=r):
                at = {"y": y, "x": x, "h": z // 2, "l": z % 2}
                at[axis] = (at[axis] + r) % size
                return at["y"], at["x"], c, 2 * at["h"] + at["l"]

            self.got.append(plan.send(pick(terms, (here + r) % size, self.at), target))
        return self

    def add(self):
        total = pick(self.terms, self.where[self.axis], self.at).astype(F32)
        for got in self.got:
            total = total + got.astype(F32)
        self.terms = total.astype(self.terms.dtype) if self.axes else total
        return self.terms

    def hold(self, *others):
        self.terms, *rest = tie(self.terms, *others)
        return rest


def per_chip(
    plan,
    inputs,
    timesteps,
    segments,
    cotangent,
    w_qkv,
    b_query,
    b_value,
    w_out,
    b_out,
    ln1_gain,
    ln1_bias,
    w_up,
    b_up,
    w_down,
    b_down,
    ln2_gain,
    ln2_bias,
    w_time,
    b_time,
):
    local_len = inputs.shape[1]
    rows = 2 * local_len
    length = segments.shape[1]
    b = lax.axis_index("batch")
    z = lax.axis_index("seq")
    c, x, y = b % 2, (b // 2) % plan.nx, b // 2 // plan.nx
    part = z % 2
    where = (y, x, z)
    first = (segments[1, 0] == segments[1, 128 * 12]).astype(jnp.int32)
    which = lambda s: (first + s) % 2
    facts = jnp.concatenate(
        [segments[:, : 128 * 13 : 128], timesteps[:, None], jnp.zeros((2, 2), jnp.int32)], axis=1
    )
    facts = jnp.stack([pick(facts, which(0), 0), pick(facts, which(1), 0)])
    other_facts = plan.sibling(facts)
    facts = jnp.where(z // 2 == c, facts, other_facts)
    mine = pick(facts, z % 2, 0)
    marks = mine[:13]
    info = jnp.concatenate(
        [
            jnp.where(marks[:1] == marks[12:], 1, jnp.where(marks[12:] == marks[:1] + 12, 2, 0)),
            jnp.sum((marks[None, :] < marks[:, None]).astype(jnp.int32), axis=1),
            jnp.sum((marks[None, :] <= marks[:, None]).astype(jnp.int32), axis=1),
        ]
    )
    fraction = mine[13].astype(F32) / TSTEPS

    stays = z // 2 == c

    def exchange(parts):
        got = [
            plan.send(v, lambda y, x, c, z, j=j: (y, x, z // 2, 2 * c + (z + j) % 2))
            for j, v in enumerate(parts)
        ]
        return [(got[0], parts[0]), (got[1], None)]

    def arrived(got):
        return [jnp.where(stays, got[0][1], got[0][0]), got[1][0]]

    def gather_parts(array):
        return [pick(array, which((part + j) % 2), 0) for j in (0, 1)]

    def gather_end(got):
        got = arrived(got)
        return jnp.concatenate(
            [jnp.where(part == 0, got[0], got[1]), jnp.where(part == 0, got[1], got[0])], axis=0
        )

    def spread_parts(array):
        array = array.reshape(2, local_len, array.shape[-1])
        return [pick(array, (part + j) % 2, 0) for j in (0, 1)]

    def spread_end(got):
        got = arrived(got)
        swap = (part + first) % 2
        return jnp.stack(
            [jnp.where(swap == 0, got[0], got[1]), jnp.where(swap == 0, got[1], got[0])], axis=0
        )

    def whole(own, other):
        return jnp.where(c == 0, jnp.concatenate([own, other]), jnp.concatenate([other, own]))

    def halves(array, axis):
        shape = array.shape
        cut = shape[:axis] + (plan.ny * plan.nx, 2, -1) + shape[axis + 1 :]
        flat = shape[:axis] + (-1,) + shape[axis + 1 :]
        split = array.reshape(cut)
        return (
            pick(split, c, axis + 1).reshape(flat),
            pick(split, 1 - c, axis + 1).reshape(flat),
        )

    def blocks(array):
        return array.reshape(plan.ny, plan.nx, 2, 2, -1, array.shape[-1])

    model = inputs.shape[-1]
    half = model // 2
    quads = plan.ny * plan.nx
    core = jnp.stack([c]).astype(jnp.int32)
    away = 1 - core
    w_own, w_oth = split_columns(core, w_qkv, quads)
    bias = jnp.concatenate(
        [
            halves(b_query.astype(F32), 0)[0],
            jnp.zeros((half,), F32),
            halves(b_value.astype(F32), 0)[0],
        ]
    )
    w_out_four = w_out.reshape(quads, 2, -1, model)
    ahead = [range(0, quads // 2), range(quads // 2, quads)]
    groups = ahead
    own_inputs = gather_end(exchange(gather_parts(inputs)))
    vecs = jnp.stack(
        [v.astype(F32) for v in (w_time, b_time, b_out, ln1_gain, ln1_bias, b_down, ln2_gain, ln2_bias)]
    )
    cot_parts = gather_parts(cotangent)
    bias = bias[None]
    own_inputs, w_own, w_oth, vecs, info, bias, cot_parts = tie(
        own_inputs, w_own, w_oth, vecs, info, bias, cot_parts
    )
    sib_inputs = plan.sibling(own_inputs)
    cot_parts, sib_inputs = tie(cot_parts, sib_inputs)
    own_cotangent = gather_end(exchange(cot_parts))
    qkv, start_full = project(core, fraction[None], own_inputs, sib_inputs, vecs, w_own, bias)
    fwd = [attn_fwd(info, qkv, g.start, len(g)) for g in ahead]
    away_of = [
        plan.sibling(pick(f[0].reshape(2, rows, -1), 1 - c, 0)) for f in fwd
    ]
    result, normed_low, act, two_low, hid, grad_one, one_low, small_sums, up_sums = middle(
        core,
        fraction[None],
        own_inputs,
        [f[0] for f in fwd],
        away_of,
        own_cotangent,
        vecs,
        b_up.astype(F32)[None],
        w_out_four,
        w_up,
        w_down,
    )
    one_sib = plan.sibling(one_low)
    output_got = exchange(spread_parts(result))
    down_part = weight_grad(away, act, two_low, quads=quads)
    normed_low, down_part = tie(normed_low, down_part)
    down_got = plan.sibling(down_part)
    up_part = weight_grad(away, normed_low, hid, quads=quads)
    act, up_part = tie(act, up_part)
    up_got = plan.sibling(up_part)
    down_sum = weight_grad(core, act, two_low, down_got, quads=quads)
    normed_low, down_sum = tie(normed_low, down_sum)
    down = Sum(plan, blocks(down_sum), where).send("x")
    up_sum = weight_grad(core, normed_low, hid, up_got, quads=quads)
    one_low, one_sib, up_sum = tie(one_low, one_sib, up_sum)
    up = Sum(plan, blocks(up_sum), where).send("y")
    out_sum = out_grad(core, [f[0] for f in fwd], one_low, one_sib)
    one_low, one_sib, out_sum = tie(one_low, one_sib, out_sum)
    out = Sum(plan, blocks(out_sum), where).send("x")
    grad_context = context_grad(core, one_low, one_sib, w_out_four)

    def back(first, count, into=None):
        f = first // (quads // 2)
        start = ahead[f].start
        return attn_bwd(
            info,
            fwd[f][2],
            qkv,
            fwd[f][0],
            fwd[f][1],
            grad_context,
            first,
            count,
            first - start,
            quads // 2,
            first - start,
            into,
        )

    def away_rows(grads):
        return plan.sibling(pick(grads.reshape(3, 2, rows, -1), 1 - c, 1))

    def products(grads):
        cross_part = weight_grad(away, start_full, grads, quads=quads)
        grads, cross_part = tie(grads, cross_part)
        cross = plan.sibling(cross_part)
        keep = weight_grad(core, start_full, grads, quads=quads)
        return Sum(plan, blocks(cross), where), Sum(plan, blocks(keep), where)

    def settle(items, other):
        for item in items:
            item.got, other = tie(item.got, other)
            item.add()
            item.terms, other = tie(item.terms, other)
        return other

    grads0, b_sum0 = back(0, quads // 2)
    got0 = away_rows(grads0)
    output_got, grads0 = tie(output_got, grads0)
    cross0, keep0 = products(grads0)
    cross0.terms, keep0.terms, grad_context = tie(cross0.terms, keep0.terms, grad_context)
    down.got, up.got, keep0.terms = tie(down.got, up.got, keep0.terms)
    down.add()
    up.add()
    down.terms, up.terms, grad_context = tie(down.terms, up.terms, grad_context)
    down.send("y")
    up.send("x")
    keep0.send("x")
    cross0.send("y")
    grads, b_sum1 = back(quads // 2, quads // 4)
    grads, grads0, got0 = tie(grads, grads0, got0)
    (grad_start,) = add_start(core, grad_one, grads0, got0, w_own, w_oth, 0, False)
    grad_start = settle([down, up, out], grad_start)
    out.send("y")
    wide_rows = up.terms.shape[-2]
    slabs = [up.terms[..., i * model : (i + 1) * model] for i in range(up.terms.shape[-1] // model)]
    ffn = jnp.concatenate([down.terms, *slabs], axis=2)
    ffn, grads, grad_start = tie(ffn, grads, grad_start)
    ffn = Sum(plan, ffn, where, "hl").send("l")
    grads, b_sum2 = back(quads // 2 + quads // 4, quads // 4, grads)
    got = away_rows(grads)
    grads = settle([ffn, keep0, cross0, out], grads)
    ffn.send("h")
    keep0.send("y")
    cross0.send("x")
    cross1, keep1 = products(grads)
    got, keep1.terms = tie(got, keep1.terms)
    keep1.send("x")
    cross1.send("y")
    grad_low, b_time_sum = add_start(core, grad_start, grads, got, w_own, w_oth, 1, True)
    in_parts, b_time_sum = tie(spread_parts(grad_low), b_time_sum)
    grad_inputs_got = exchange(in_parts)
    b_time_sum = settle([keep0, cross0, keep1, cross1], b_time_sum)
    ffn.got, b_time_sum = tie(ffn.got, b_time_sum)
    keep1.send("y")
    cross1.send("x")
    small_sums, up_sums, b_time_sum = tie(small_sums, up_sums, b_time_sum)
    b_sum = jnp.concatenate([b_sum0, b_sum1, b_sum2], axis=1)
    zero = jnp.zeros((quads, 2, half // quads), F32)

    def placed(v):
        return lax.dynamic_update_index_in_dim(zero, v.reshape(quads, half // quads), c, 1).reshape(-1)

    vectors = [small_sums[i] for i in range(6)]
    vectors += [placed(b_sum[0]), placed(b_sum[1]), fraction * b_time_sum[0], b_time_sum[0]]
    small = jnp.concatenate([v[:, None] for v in vectors] + [up_sums.reshape(model, -1)], axis=1)
    small_own, small_oth = halves(small, 0)
    small = Sum(plan, blocks(small_own + plan.sibling(small_oth)), where)
    small.send("x").add()
    small.send("y")
    keep1.got, cross1.got, small.got, grad_inputs_got = tie(
        keep1.got, cross1.got, small.got, grad_inputs_got
    )
    keep1.add()
    cross1.add()
    small.add()
    late = jnp.concatenate([i.terms for i in (keep0, cross0, keep1, cross1, out)], axis=3)
    late = Sum(plan, late, where, "hl").send("l")
    small.send("l")
    late.got, small.got = tie(late.got, small.got)
    late.add()
    small.add()
    late.send("h")
    small.send("h")
    small.add()
    small = small.terms
    late = late.add()
    wide = 3 * half // 2
    keeps = [late[:, :wide], late[:, 2 * wide : 3 * wide]]
    crosses = [late[:, wide : 2 * wide], late[:, 3 * wide : 4 * wide]]
    ffn = ffn.add()
    count = ffn.shape[0] - wide_rows * len(slabs)
    sum_w_down, sum_w_out = ffn[:count], late[:, 4 * wide :]
    sum_w_up = jnp.concatenate(
        [ffn[count + i * wide_rows : count + (i + 1) * wide_rows] for i in range(len(slabs))], axis=1
    )
    output = spread_end(output_got)
    grad_inputs = spread_end(grad_inputs_got)
    split3 = lambda parts: jnp.concatenate(
        [p.reshape(p.shape[0], 3, len(g), -1) for p, g in zip(parts, groups)], axis=2
    )
    sum_own, sum_oth = split3(keeps), split3(crosses)
    pair = jnp.where(c == 0, jnp.stack([sum_own, sum_oth]), jnp.stack([sum_oth, sum_own]))
    sum_w_qkv = (
        pair.transpose(1, 2, 3, 0, 4).reshape(-1, 3 * model)
    )
    v = [small[:, i] for i in (6, 7, 0, 1, 2, 3, 4, 5, 8, 9)]
    return (
        output,
        grad_inputs,
        sum_w_qkv,
        v[0],
        v[1],
        sum_w_out,
        v[2],
        v[3],
        v[4],
        sum_w_up,
        small[:, 10:].reshape(-1),
        sum_w_down,
        v[5],
        v[6],
        v[7],
        v[8],
        v[9],
    )


def solution(mesh):
    placed = (
        P("batch", "seq", None),
        P("batch"),
        P("batch", None),
        P("batch", "seq", None),
        P(),
        P(),
        P(),
        P(),
        P(),
        P(),
        P(),
        P(),
        P(),
        P(),
        P(),
        P(),
        P(),
        P(),
        P(),
    )
    sizes = dict(mesh.shape)
    body = per_device
    if sizes["seq"] == 4 and sizes["batch"] % 2 == 0:
        body = functools.partial(per_chip, Plan(mesh))
    return jax.shard_map(
        body,
        mesh=mesh,
        in_specs=placed,
        out_specs=(
            P("batch", "seq", None),
            P("batch", "seq", None),
            P(("batch", "seq"), None),
            P(("batch", "seq")),
            P(("batch", "seq")),
            P(("batch", "seq"), None),
            P(("batch", "seq")),
            P(("batch", "seq")),
            P(("batch", "seq")),
            P(("batch", "seq"), None),
            P(("batch", "seq")),
            P(("batch", "seq"), None),
            P(("batch", "seq")),
            P(("batch", "seq")),
            P(("batch", "seq")),
            P(("batch", "seq")),
            P(("batch", "seq")),
        ),
        check_vma=False,
    )
```

```python
import functools

import jax
import jax.numpy as jnp
from jax import lax
from jax.experimental import pallas as pl
from jax.experimental.pallas import tpu as pltpu
from jax.sharding import PartitionSpec as P

D = 1024
HEADS = 16
TSTEPS = 5000
AXES = ("batch", "seq")


BF=jnp.bfloat16; F32=jnp.float32
NT=(((1,),(1,)),((),())); NN=(((1,),(0,)),((),())); TN=(((0,),(0,)),((),()))
def dot(a,b,d): return lax.dot_general(a,b,d,preferred_element_type=F32)
PHASE=1
FILLED=1664; PAD=64
def lanes(rows):
    return lax.broadcasted_iota(jnp.int32,(rows,128),1)
def parts3(x):
    a=x.astype(BF).astype(F32); r=x-a; b=r.astype(BF).astype(F32); c=r-b
    return a,b,c
def augment(base,h,x,lane):
    a,b,c=parts3(x)
    o=(1-h)*64
    f=base.astype(F32)
    f=jnp.where((lane>=o)&(lane<o+64),jnp.where(lane==o,a,jnp.where(lane==o+1,b,jnp.where(lane==o+2,c,0.0))),f)
    return f.astype(BF)
def ones3(base,h,lane,n=3):
    o=(1-h)*64
    f=base.astype(F32)
    f=jnp.where((lane>=o)&(lane<o+64),jnp.where(lane<o+n,1.0,0.0),f)
    return f.astype(BF)
def spread(base,h,x,lane):
    a=x.astype(BF).astype(F32); r=x-a; b=r.astype(BF).astype(F32); c=r-b
    o=(1-h)*64
    f=jnp.where(lane==o,a,jnp.where(lane==o+1,b,jnp.where(lane==o+2,c,0.0)))
    return jnp.where((lane//64)==h,base.astype(F32),f).astype(BF)
def fwd_tiles(tasks,lane):
    scores=[]
    for q,k,vs,keep in tasks:
        for h in (0,1):
            qh=jnp.where((lane//64)==h,q.astype(F32),0.0).astype(BF)
            s=dot(qh,k,NT)
            scores.append(s if keep is None else jnp.where(keep,s,-1e30))
    tops=[];outs=[]
    depth=PHASE
    n=len(scores)
    def soft(i):
        m=jnp.max(scores[i],axis=1,keepdims=True)
        tops.append(m)
        return jnp.exp2(scores[i]-m).astype(BF)
    ps=[]
    for i in range(n+depth):
        if i<n: ps.append(soft(i))
        if i>=depth: outs.append(dot(ps[i-depth],tasks[(i-depth)//2][2][(i-depth)%2],NN))
    done=[]
    for t,(q,_,_,_) in enumerate(tasks):
        os=[];augs=[]
        for h in (0,1):
            o=outs[2*t+h]
            os.append(o/pltpu.roll(o,64,1))
            augs.append(spread(q,h,-(tops[2*t+h]+jnp.log2(o)),lane))
        done.append((jnp.where(lane<64,os[0],os[1]),augs))
    return done
def fwd_store(refs,rows,o,augs):
    o_ref,ol_ref,qa_ref=refs
    o_ref[rows,:]=o.astype(BF)
    ol_ref[rows,:]=(o-o.astype(BF).astype(F32)).astype(BF)
    for h in (0,1): qa_ref[h,rows,:]=augs[h]
def fwd_kernel(bq,info,q_ref,k_ref,v_ref,*refs):
    *refs,vs_ref=refs
    single=info[0]==1
    @pl.when(single)
    def _():
        v=v_ref[0:FILLED,:]
        for h in (0,1): vs_ref[h,...]=ones3(v,h,lanes(FILLED),64)
        lq=lanes(bq)
        @pl.loop(0,FILLED//bq)
        def _(r):
            rows=pl.ds(pl.multiple_of(r*bq,bq),bq)
            (o,augs),=fwd_tiles([(q_ref[rows,:],k_ref[0:FILLED,:],(vs_ref[0],vs_ref[1]),None)],lq)
            fwd_store(refs,rows,o,augs)
    @pl.when(info[0]==2)
    def _():
        lq=lanes(128)
        each=[slice(i*128,i*128+128) for i in range(13)]
        tasks=[(q_ref[r,:],k_ref[r,:],[ones3(v_ref[r,:],h,lq,64) for h in (0,1)],None) for r in each]
        for r,(o,augs) in zip(each,fwd_tiles(tasks,lq)): fwd_store(refs,r,o,augs)
    @pl.when(info[0]==0)
    def _():
        col=lax.broadcasted_iota(jnp.int32,(128,512),1)
        lw=lanes(512); lq=lanes(128)
        @pl.loop(0,13)
        def _(i):
            lo=info[1+i]; hi=info[14+i]
            at=jnp.minimum(lo,9)
            window=pl.ds(pl.multiple_of(at*128,128),512)
            k=k_ref[window,:]; v=v_ref[window,:]
            vs=[ones3(v,h,lw,64) for h in (0,1)]
            keep=(col>=(lo-at)*128)&(col<(hi-at)*128)
            rows=pl.ds(pl.multiple_of(i*128,128),128)
            (o,augs),=fwd_tiles([(q_ref[rows,:],k,vs,keep)],lq)
            fwd_store(refs,rows,o,augs)
    rows=slice(FILLED,FILLED+PAD)
    lp=lanes(PAD)
    v=v_ref[rows,:]
    (o,augs),=fwd_tiles([(q_ref[rows,:],k_ref[rows,:],[ones3(v,h,lp,64) for h in (0,1)],None)],lp)
    fwd_store(refs,rows,o,augs)
def attn_fwd(info,qkv,first,count,bq=832):
    L,W3=qkv.shape; n=W3//384
    spec=lambda j: pl.BlockSpec((L,128),lambda p,s,j=j:(0,p+first+j*n))
    one=pl.BlockSpec((L,128),lambda p,s:(0,p))
    return pl.pallas_call(functools.partial(fwd_kernel,bq),
        out_shape=(jax.ShapeDtypeStruct((L,count*128),BF),)*2+(jax.ShapeDtypeStruct((2*count,L,128),BF),),
        grid_spec=pltpu.PrefetchScalarGridSpec(num_scalar_prefetch=1,grid=(count,),
            in_specs=[spec(0),spec(1),spec(2)],
            out_specs=(one,one,pl.BlockSpec((2,L,128),lambda p,s:(p,0,0))),
            scratch_shapes=[pltpu.VMEM((2,FILLED,128),BF)]),
        compiler_params=pltpu.CompilerParams(vmem_limit_bytes=50<<20),name="attn_forward",
        cost_estimate=pl.CostEstimate(flops=8*count*L*L*256,bytes_accessed=10*L*count*128,transcendentals=2*count*L*L))(info,qkv,qkv,qkv)
def deltas(g,o,ol,lane):
    prod=g.astype(F32)*(o.astype(F32)+ol.astype(F32))
    return [augment(g,h,-jnp.sum(jnp.where((lane//64)==h,prod,0.0),axis=1,keepdims=True),lane) for h in (0,1)]
def bwd_tiles(tasks,lane,turned=None):
    khs=[ones3(t[1],t[4],lane) for t in tasks]
    ps=[dot(kh,t[0],NT) for kh,t in zip(khs,tasks)]
    ds=[dot(ones3(t[2],t[4],lane),t[3],NT) for t in tasks]
    done=[]
    for kh,p,d,(qa,_,_,ga,h,keep) in zip(khs,ps,ds,tasks):
        p=jnp.exp2(p)
        if keep is not None: p=jnp.where(keep,p,0.0)
        d=(p*d).astype(BF)
        done.append((kh,p.astype(BF),d,qa,ga))
    back=lambda i,kh,d: dot(d,kh,TN) if turned is None else dot(turned[i*64:i*64+64,:],d,NN)
    return [(back(i,kh,d),dot(d,qa,NN),dot(p,ga,NN)) for i,(kh,p,d,qa,ga) in enumerate(done)]
LN2=0.6931471805599453
def both(a,lane): return jnp.where(lane<64,a[0],a[1])
def bwd_alone(each,lane,qa_ref,k_ref,v_ref,o_ref,ol_ref,g_ref,dq_ref,dk_ref,dv_ref):
    tasks=[]
    for r in each:
        gas=deltas(g_ref[r,:],o_ref[r,:],ol_ref[r,:],lane)
        tasks+=[(qa_ref[h,r,:],k_ref[r,:],v_ref[r,:],gas[h],h,None) for h in (0,1)]
    got=bwd_tiles(tasks,lane)
    for i,r in enumerate(each):
        x,y=got[2*i],got[2*i+1]
        dq_ref[r,:]=(both((x[0],y[0]),lane)*0.125).astype(BF)
        dk_ref[r,:]=(both((x[1],y[1]),lane)*LN2).astype(BF)
        dv_ref[r,:]=both((x[2],y[2]),lane).astype(BF)
def bwd_kernel(bk,joined,info,qa_ref,k_ref,v_ref,o_ref,ol_ref,g_ref,*rest):
    d_ref,sum_ref,acc,acc_k,acc_v,ga_ref=rest[1:] if joined else rest
    dq_ref,dk_ref,dv_ref=d_ref.at[0],d_ref.at[1],d_ref.at[2]
    tile_refs=(qa_ref,k_ref,v_ref,o_ref,ol_ref,g_ref,dq_ref,dk_ref,dv_ref)
    single=info[0]==1
    @pl.when(single)
    def _():
        lf=lanes(FILLED)
        gas=deltas(g_ref[0:FILLED,:],o_ref[0:FILLED,:],ol_ref[0:FILLED,:],lf)
        acc[...]=jnp.zeros_like(acc)
        lb=lanes(bk)
        ga_ref[0,...]=gas[0]; ga_ref[1,...]=gas[1]
        @pl.loop(0,FILLED//bk)
        def _(r):
            rows=pl.ds(pl.multiple_of(r*bk,bk),bk)
            k=k_ref[rows,:]; v=v_ref[rows,:]
            dks=[];dvs=[]
            got=bwd_tiles([(qa_ref[h,0:FILLED,:],k,v,ga_ref[h],h,None) for h in (0,1)],lb,k.astype(F32).T.astype(BF))
            for h in (0,1):
                dq,dk,dv=got[h]
                acc[h*64:h*64+64,:]+=dq
                dks.append(dk); dvs.append(dv)
            dk_ref[rows,:]=(both(dks,lb)*LN2).astype(BF)
            dv_ref[rows,:]=both(dvs,lb).astype(BF)
        dq_ref[0:FILLED,:]=(acc[...].T*0.125).astype(BF)
    @pl.when(info[0]==2)
    def _():
        lq=lanes(128)
        bwd_alone([slice(i*128,i*128+128) for i in range(13)],lq,*tile_refs)
    @pl.when(info[0]==0)
    def _():
        row=lax.broadcasted_iota(jnp.int32,(512,128),0)
        lw=lanes(512); lq=lanes(128)
        acc_k[...]=jnp.zeros_like(acc_k); acc_v[...]=jnp.zeros_like(acc_v)
        @pl.loop(0,13)
        def _(i):
            lo=info[1+i]; hi=info[14+i]
            at=jnp.minimum(lo,9)
            window=pl.ds(pl.multiple_of(at*128,128),512)
            k=k_ref[window,:]; v=v_ref[window,:]
            keep=(row>=(lo-at)*128)&(row<(hi-at)*128)
            rows=pl.ds(pl.multiple_of(i*128,128),128)
            gas=deltas(g_ref[rows,:],o_ref[rows,:],ol_ref[rows,:],lq)
            dqs=[]
            got=bwd_tiles([(qa_ref[h,rows,:],k,v,gas[h],h,keep) for h in (0,1)],lw)
            for h in (0,1):
                dq,dk,dv=got[h]
                dqs.append(dq)
                acc_k[h,window,:]+=dk
                acc_v[h,window,:]+=dv
            dq_ref[rows,:]=(both(dqs,lq)*0.125).astype(BF)
        lf=lanes(FILLED)
        dk_ref[0:FILLED,:]=(jnp.where(lf<64,acc_k[0],acc_k[1])*LN2).astype(BF)
        dv_ref[0:FILLED,:]=jnp.where(lf<64,acc_v[0],acc_v[1]).astype(BF)
    bwd_alone([slice(FILLED,FILLED+PAD)],lanes(PAD),*tile_refs)
    sum_ref[0:1,:]=jnp.sum(dq_ref[...].astype(F32),axis=0,keepdims=True)
    sum_ref[1:2,:]=jnp.sum(dv_ref[...].astype(F32),axis=0,keepdims=True)
def attn_bwd(info,qa,qkv,o,ol,g,first,count,inner,wide,at,into=None,bk=416):
    L,W3=qkv.shape; n=W3//384
    spec=lambda j: pl.BlockSpec((L,128),lambda p,s,j=j:(0,p+first+j*n))
    one=pl.BlockSpec((L,128),lambda p,s:(0,p))
    part=pl.BlockSpec((L,128),lambda p,s:(0,p+inner))
    every=pl.BlockSpec((L,128),lambda p,s:(0,p+first))
    return pl.pallas_call(functools.partial(bwd_kernel,bk,into is not None),
        input_output_aliases={} if into is None else {7:0},
        out_shape=(jax.ShapeDtypeStruct((3,L,wide*128),BF),jax.ShapeDtypeStruct((2,count*128),F32)),
        grid_spec=pltpu.PrefetchScalarGridSpec(num_scalar_prefetch=1,grid=(count,),
            in_specs=[pl.BlockSpec((2,L,128),lambda p,s:(p+inner,0,0)),spec(1),spec(2),part,part,every]+([] if into is None else [pl.BlockSpec(memory_space=pl.ANY)]),
            out_specs=(pl.BlockSpec((3,L,128),lambda p,s:(0,0,p+at)),pl.BlockSpec((2,128),lambda p,s:(0,p))),
            scratch_shapes=[pltpu.VMEM((128,FILLED),F32)]+[pltpu.VMEM((2,FILLED,128),F32)]*2+[pltpu.VMEM((2,FILLED,128),BF)]),
        compiler_params=pltpu.CompilerParams(vmem_limit_bytes=56<<20),name="attn_backward",
        cost_estimate=pl.CostEstimate(flops=20*count*L*L*256,bytes_accessed=16*L*count*128,transcendentals=2*count*L*L))(*((info,qa,qkv,qkv,o,ol,g) if into is None else (info,qa,qkv,qkv,o,ol,g,into)))


def gelu_exact(values):
    return jax.nn.gelu(values, approximate=False)


def norm_forward(values, gain, shift):
    centered = values - jnp.mean(values, axis=-1, keepdims=True)
    inverse = lax.rsqrt(jnp.mean(centered * centered, axis=-1, keepdims=True) + 1e-05)
    unit_part = centered * inverse
    return (unit_part * gain + shift, unit_part, inverse)


def norm_backward(grad_out, unit_part, inverse, gain):
    scaled = grad_out * gain
    centered = scaled - jnp.mean(scaled, axis=-1, keepdims=True)
    grad_in = inverse * (
        centered - unit_part * jnp.mean(scaled * unit_part, axis=-1, keepdims=True)
    )
    return (grad_in, jnp.sum(grad_out * unit_part, axis=0), jnp.sum(grad_out, axis=0))


def attention_forward(query_all, key_all, value_all, segments, head_dim):
    length, local_width = (query_all.shape[1], query_all.shape[2])
    head_count = local_width // head_dim
    block_len = length // 3
    score_scale = head_dim ** (-0.5)

    def per_sequence(pieces):
        queries, key_rows, value_rows, seq_ids = pieces
        key_heads = key_rows.reshape(length, head_count, head_dim)
        value_heads = value_rows.reshape(length, head_count, head_dim)

        def per_block(block_pieces):
            query_part, id_part = block_pieces
            query_heads = query_part.reshape(block_len, head_count, head_dim)
            scores = (
                jnp.einsum(
                    "qhd,khd->hqk", query_heads, key_heads, preferred_element_type=jnp.float32
                )
                * score_scale
            )
            masked = jnp.where(id_part[None, :, None] == seq_ids[None, None, :], scores, -1e30)
            maxima = jnp.max(masked, axis=-1, keepdims=True)
            exp_scores = jnp.exp(masked - maxima)
            totals = jnp.sum(exp_scores, axis=-1, keepdims=True)
            weights_low = (exp_scores / totals).astype(jnp.bfloat16)
            context = jnp.einsum(
                "hqk,khd->qhd", weights_low, value_heads, preferred_element_type=jnp.float32
            )
            return (
                context.astype(jnp.bfloat16).reshape(block_len, local_width),
                (maxima + jnp.log(totals))[..., 0],
            )

        contexts, logsums = lax.map(
            per_block, (queries.reshape(3, block_len, local_width), seq_ids.reshape(3, block_len))
        )
        return (contexts.reshape(length, local_width), logsums)

    return lax.map(per_sequence, (query_all, key_all, value_all, segments))


def attention_backward(query_all, key_all, value_all, segments, logsums, grad_all, head_dim):
    length, local_width = (query_all.shape[1], query_all.shape[2])
    head_count = local_width // head_dim
    block_len = length // 3
    score_scale = head_dim ** (-0.5)

    def per_sequence(pieces):
        queries, key_rows, value_rows, seq_ids, sum_rows, grad_rows = pieces
        key_heads = key_rows.reshape(length, head_count, head_dim)
        value_heads = value_rows.reshape(length, head_count, head_dim)

        def per_block(carry, block_pieces):
            key_total, value_total = carry
            query_part, id_part, sum_part, grad_part = block_pieces
            query_heads = query_part.reshape(block_len, head_count, head_dim)
            grad_heads = grad_part.reshape(block_len, head_count, head_dim)
            scores = (
                jnp.einsum(
                    "qhd,khd->hqk", query_heads, key_heads, preferred_element_type=jnp.float32
                )
                * score_scale
            )
            allowed = id_part[None, :, None] == seq_ids[None, None, :]
            prob_weights = jnp.where(allowed, jnp.exp(scores - sum_part[:, :, None]), 0.0)
            grad_probs = jnp.einsum(
                "qhd,khd->hqk", grad_heads, value_heads, preferred_element_type=jnp.float32
            )
            delta = jnp.sum(prob_weights * grad_probs, axis=-1, keepdims=True)
            grad_scores = (prob_weights * (grad_probs - delta)).astype(jnp.bfloat16)
            query_grad = (
                jnp.einsum(
                    "hqk,khd->qhd", grad_scores, key_heads, preferred_element_type=jnp.float32
                )
                * score_scale
            )
            key_total = (
                key_total
                + jnp.einsum(
                    "hqk,qhd->khd", grad_scores, query_heads, preferred_element_type=jnp.float32
                )
                * score_scale
            )
            value_total = value_total + jnp.einsum(
                "hqk,qhd->khd",
                prob_weights.astype(jnp.bfloat16),
                grad_heads,
                preferred_element_type=jnp.float32,
            )
            return (
                (key_total, value_total),
                query_grad.astype(jnp.bfloat16).reshape(block_len, local_width),
            )

        zero_heads = jnp.zeros((length, head_count, head_dim), jnp.float32)
        (key_total, value_total), query_grads = lax.scan(
            per_block,
            (zero_heads, zero_heads),
            (
                queries.reshape(3, block_len, local_width),
                seq_ids.reshape(3, block_len),
                sum_rows,
                grad_rows.reshape(3, block_len, local_width),
            ),
        )
        return (
            query_grads.reshape(length, local_width),
            key_total.astype(jnp.bfloat16).reshape(length, local_width),
            value_total.astype(jnp.bfloat16).reshape(length, local_width),
        )

    return lax.map(per_sequence, (query_all, key_all, value_all, segments, logsums, grad_all))


def per_device(
    inputs,
    timesteps,
    segments,
    cotangent,
    w_qkv,
    b_query,
    b_value,
    w_out,
    b_out,
    ln1_gain,
    ln1_bias,
    w_up,
    b_up,
    w_down,
    b_down,
    ln2_gain,
    ln2_bias,
    w_time,
    b_time,
):
    groups, local_len, model_width = inputs.shape
    row_count = groups * local_len
    head_dim = D // HEADS
    fraction = timesteps.astype(jnp.float32) / TSTEPS
    start_sum = (
        inputs.astype(jnp.float32)
        + fraction[:, None, None] * w_time.astype(jnp.float32)
        + b_time.astype(jnp.float32)
    )
    start_low = start_sum.astype(jnp.bfloat16)
    projected = jnp.einsum("bld,de->ble", start_low, w_qkv, preferred_element_type=jnp.float32)
    query_low = (projected[..., :model_width] + b_query.astype(jnp.float32)).astype(jnp.bfloat16)
    key_low = projected[..., model_width : 2 * model_width].astype(jnp.bfloat16)
    value_low = (projected[..., 2 * model_width :] + b_value.astype(jnp.float32)).astype(
        jnp.bfloat16
    )
    query_all, key_all, value_all = (
        lax.all_to_all(query_low, "seq", split_axis=2, concat_axis=1, tiled=True),
        lax.all_to_all(key_low, "seq", split_axis=2, concat_axis=1, tiled=True),
        lax.all_to_all(value_low, "seq", split_axis=2, concat_axis=1, tiled=True),
    )
    context_heads, logsums = attention_forward(query_all, key_all, value_all, segments, head_dim)
    context = lax.all_to_all(context_heads, "seq", split_axis=1, concat_axis=2, tiled=True)
    context_rows = context.reshape(row_count, model_width)
    start_rows = start_sum.reshape(row_count, model_width)
    residual_one = (
        start_rows
        + jnp.dot(context_rows, w_out, preferred_element_type=jnp.float32)
        + b_out.astype(jnp.float32)
    )
    normed, unit_one, inverse_one = norm_forward(
        residual_one, ln1_gain.astype(jnp.float32), ln1_bias.astype(jnp.float32)
    )
    normed_low = normed.astype(jnp.bfloat16)
    hidden_pre = jnp.dot(normed_low, w_up, preferred_element_type=jnp.float32) + b_up.astype(
        jnp.float32
    )
    activated, gelu_pull = jax.vjp(gelu_exact, hidden_pre)
    activated_low = activated.astype(jnp.bfloat16)
    residual_two = (
        normed
        + jnp.dot(activated_low, w_down, preferred_element_type=jnp.float32)
        + b_down.astype(jnp.float32)
    )
    result, unit_two, inverse_two = norm_forward(
        residual_two, ln2_gain.astype(jnp.float32), ln2_bias.astype(jnp.float32)
    )
    output = result.astype(jnp.bfloat16).reshape(groups, local_len, model_width)
    grad_result = cotangent.reshape(row_count, model_width).astype(jnp.float32)
    grad_two, grad_ln2_gain, grad_ln2_bias = norm_backward(
        grad_result, unit_two, inverse_two, ln2_gain.astype(jnp.float32)
    )
    grad_b_down = jnp.sum(grad_two, axis=0)
    grad_two_low = grad_two.astype(jnp.bfloat16)
    grad_w_down = jnp.einsum(
        "rf,rd->fd", activated_low, grad_two_low, preferred_element_type=jnp.float32
    )
    grad_activated = jnp.einsum(
        "rd,fd->rf", grad_two_low, w_down, preferred_element_type=jnp.float32
    )
    grad_hidden = gelu_pull(grad_activated)[0]
    grad_b_up = jnp.sum(grad_hidden, axis=0)
    grad_hidden_low = grad_hidden.astype(jnp.bfloat16)
    grad_w_up = jnp.einsum(
        "rd,rf->df", normed_low, grad_hidden_low, preferred_element_type=jnp.float32
    )
    grad_normed = grad_two + jnp.einsum(
        "rf,df->rd", grad_hidden_low, w_up, preferred_element_type=jnp.float32
    )
    grad_one, grad_ln1_gain, grad_ln1_bias = norm_backward(
        grad_normed, unit_one, inverse_one, ln1_gain.astype(jnp.float32)
    )
    grad_b_out = jnp.sum(grad_one, axis=0)
    grad_one_low = grad_one.astype(jnp.bfloat16)
    grad_w_out = jnp.einsum(
        "rd,re->de", context_rows, grad_one_low, preferred_element_type=jnp.float32
    )
    grad_context = (
        jnp.einsum("re,de->rd", grad_one_low, w_out, preferred_element_type=jnp.float32)
        .astype(jnp.bfloat16)
        .reshape(groups, local_len, model_width)
    )
    grad_context_heads = lax.all_to_all(
        grad_context, "seq", split_axis=2, concat_axis=1, tiled=True
    )
    query_grads, key_grads, value_grads = attention_backward(
        query_all, key_all, value_all, segments, logsums, grad_context_heads, head_dim
    )
    grad_query, grad_key, grad_value = (
        lax.all_to_all(query_grads, "seq", split_axis=1, concat_axis=2, tiled=True),
        lax.all_to_all(key_grads, "seq", split_axis=1, concat_axis=2, tiled=True),
        lax.all_to_all(value_grads, "seq", split_axis=1, concat_axis=2, tiled=True),
    )
    grad_projected = jnp.concatenate((grad_query, grad_key, grad_value), axis=2).reshape(
        row_count, 3 * model_width
    )
    grad_w_qkv = jnp.einsum(
        "rd,re->de",
        start_low.reshape(row_count, model_width),
        grad_projected,
        preferred_element_type=jnp.float32,
    )
    grad_b_query = jnp.sum(grad_query.astype(jnp.float32), axis=(0, 1))
    grad_b_value = jnp.sum(grad_value.astype(jnp.float32), axis=(0, 1))
    grad_start = grad_one + jnp.einsum(
        "re,de->rd", grad_projected, w_qkv, preferred_element_type=jnp.float32
    )
    grad_inputs = grad_start.astype(jnp.bfloat16).reshape(groups, local_len, model_width)
    per_sequence_grad = jnp.sum(grad_start.reshape(groups, local_len, model_width), axis=1)
    grad_w_time = jnp.einsum("g,gd->d", fraction, per_sequence_grad)
    grad_b_time = jnp.sum(per_sequence_grad, axis=0)
    (
        sum_w_qkv,
        sum_b_query,
        sum_b_value,
        sum_w_out,
        sum_b_out,
        sum_ln1_gain,
        sum_ln1_bias,
        sum_w_up,
        sum_b_up,
        sum_w_down,
        sum_b_down,
        sum_ln2_gain,
        sum_ln2_bias,
        sum_w_time,
        sum_b_time,
    ) = (
        lax.psum_scatter(grad_w_qkv, ("batch", "seq"), scatter_dimension=0, tiled=True),
        lax.psum_scatter(grad_b_query, ("batch", "seq"), scatter_dimension=0, tiled=True),
        lax.psum_scatter(grad_b_value, ("batch", "seq"), scatter_dimension=0, tiled=True),
        lax.psum_scatter(grad_w_out, ("batch", "seq"), scatter_dimension=0, tiled=True),
        lax.psum_scatter(grad_b_out, ("batch", "seq"), scatter_dimension=0, tiled=True),
        lax.psum_scatter(grad_ln1_gain, ("batch", "seq"), scatter_dimension=0, tiled=True),
        lax.psum_scatter(grad_ln1_bias, ("batch", "seq"), scatter_dimension=0, tiled=True),
        lax.psum_scatter(grad_w_up, ("batch", "seq"), scatter_dimension=0, tiled=True),
        lax.psum_scatter(grad_b_up, ("batch", "seq"), scatter_dimension=0, tiled=True),
        lax.psum_scatter(grad_w_down, ("batch", "seq"), scatter_dimension=0, tiled=True),
        lax.psum_scatter(grad_b_down, ("batch", "seq"), scatter_dimension=0, tiled=True),
        lax.psum_scatter(grad_ln2_gain, ("batch", "seq"), scatter_dimension=0, tiled=True),
        lax.psum_scatter(grad_ln2_bias, ("batch", "seq"), scatter_dimension=0, tiled=True),
        lax.psum_scatter(grad_w_time, ("batch", "seq"), scatter_dimension=0, tiled=True),
        lax.psum_scatter(grad_b_time, ("batch", "seq"), scatter_dimension=0, tiled=True),
    )
    return (
        output,
        grad_inputs,
        sum_w_qkv,
        sum_b_query,
        sum_b_value,
        sum_w_out,
        sum_b_out,
        sum_ln1_gain,
        sum_ln1_bias,
        sum_w_up,
        sum_b_up,
        sum_w_down,
        sum_b_down,
        sum_ln2_gain,
        sum_ln2_bias,
        sum_w_time,
        sum_b_time,
    )


SLOPE = F32
PIECES = 8
LOG2E = 1.4426950408889634


def layer_norm(values):
    centered = values - jnp.mean(values, axis=1, keepdims=True)
    inverse = lax.rsqrt(jnp.mean(centered * centered, axis=1, keepdims=True) + 1e-05)
    return centered * inverse, inverse


def layer_norm_back(scaled, unit_part, inverse):
    return inverse * (
        scaled
        - jnp.mean(scaled, axis=1, keepdims=True)
        - unit_part * jnp.mean(scaled * unit_part, axis=1, keepdims=True)
    )


def gelu_pair(v):
    bell = jnp.exp2(v * v * (-0.5 * LOG2E))
    base = 1.0 + 0.2316418882663604 * jnp.abs(v)
    t = pltpu.reciprocal(base, approx=True)
    t = t * (2.0 - base * t)
    tail = t * (
        0.127414796
        + t * (-0.142248368 + t * (0.7107068705 + t * (-0.7265760135 + t * 0.5307027145)))
    )
    tail = tail * bell
    cover = jnp.where(v >= 0, 1.0 - tail, tail)
    return v * cover, cover + v * bell * 0.3989422804014327


def middle_kernel(
    fc,
    sel_ref,
    frac_ref,
    inp_ref,
    ctx_a0_ref,
    ctx_a1_ref,
    ctx_b0_ref,
    ctx_b1_ref,
    cot_ref,
    vec_ref,
    b_up_ref,
    wo_a_ref,
    wo_b_ref,
    w_up_hbm,
    w_down_hbm,
    out_ref,
    norm_ref,
    act_ref,
    two_ref,
    hid_ref,
    one_ref,
    onel_ref,
    small_ref,
    smallup_ref,
    w_up,
    w_down,
    slope,
    sems,
):
    step = pl.program_id(0)
    def pieces(i, source, target):
        size = source.shape[0] // PIECES
        return [
            pltpu.make_async_copy(
                source.at[pl.ds(j * size, size)],
                target.at[pl.ds(j * size, size)],
                sems.at[i * PIECES + j],
            )
            for j in range(PIECES)
        ]

    copies = pieces(0, w_up_hbm, w_up) + pieces(1, w_down_hbm, w_down)

    @pl.when(step == 0)
    def _():
        for copy in copies:
            copy.start()
        small_ref[...] = jnp.zeros_like(small_ref)
        smallup_ref[...] = jnp.zeros_like(smallup_ref)

    vec = lambda i: vec_ref[i : i + 1, :]
    start = inp_ref[...].astype(F32) + (frac_ref[0] * vec(0) + vec(1))
    residual = (
        start
        + dot(jnp.concatenate([ctx_a0_ref[...], ctx_a1_ref[...]], axis=1), wo_a_ref[...].reshape(-1, wo_a_ref.shape[-1]), NN)
        + dot(jnp.concatenate([ctx_b0_ref[...], ctx_b1_ref[...]], axis=1), wo_b_ref[...].reshape(-1, wo_b_ref.shape[-1]), NN)
        + vec(2)
    )
    unit_one, inverse_one = layer_norm(residual)
    normed = unit_one * vec(3) + vec(4)
    low = normed.astype(BF)
    norm_ref[...] = low

    @pl.when(step == 0)
    def _():
        for copy in copies:
            copy.wait()

    width = w_up.shape[1]
    total = normed + vec(5)
    for f in range(0, width, fc):
        cols = slice(f, f + fc)
        v = dot(low, w_up[:, cols], NN) + b_up_ref[:, cols]
        a, g = gelu_pair(v)
        a = a.astype(BF)
        act_ref[:, cols] = a
        slope[:, cols] = g.astype(slope.dtype)
        total = total + dot(a, w_down[cols, :], NN)
    unit_two, inverse_two = layer_norm(total)
    out_ref[...] = (unit_two * vec(6) + vec(7)).astype(BF)
    cot = cot_ref[...].astype(F32)
    two = layer_norm_back(cot * vec(6), unit_two, inverse_two)
    add = lambda v: jnp.sum(v, axis=0, keepdims=True)
    small_ref[3:4, :] += add(two)
    small_ref[4:5, :] += add(cot * unit_two)
    small_ref[5:6, :] += add(cot)
    two_low = two.astype(BF)
    two_ref[...] = two_low
    total = two
    for f in range(0, width, fc):
        cols = slice(f, f + fc)
        d = dot(two_low, w_down[cols, :], NT) * slope[:, cols].astype(F32)
        smallup_ref[:, cols] += add(d)
        d = d.astype(BF)
        hid_ref[:, cols] = d
        total = total + dot(d, w_up[:, cols], NT)
    small_ref[1:2, :] += add(total * unit_one)
    small_ref[2:3, :] += add(total)
    one = layer_norm_back(total * vec(3), unit_one, inverse_one)
    small_ref[0:1, :] += add(one)
    one_ref[...] = one
    onel_ref[...] = one.astype(BF)


def middle(core, fraction, inp, ctx_a, ctx_b, cot, vecs, b_up, w_out, w_up, w_down, br=288, fc=2048):
    rows, model = inp.shape
    width = w_up.shape[1]
    half = model // 2
    quads = w_out.shape[0]
    row = lambda w: pl.BlockSpec((br, w), lambda i, s: (i, 0))
    fixed = lambda shape: pl.BlockSpec(shape, lambda i, s: (0,) * len(shape))
    here = pl.BlockSpec((br, half // 2), lambda i, s: (s[0] * (rows // br) + i, 0))
    wo = lambda flip: pl.BlockSpec(
        (quads, 1, model // quads // 2, model),
        (lambda i, s: (0, s[0], 0, 0)) if not flip else (lambda i, s: (0, 1 - s[0], 0, 0)),
    )
    out = lambda w, t: jax.ShapeDtypeStruct((rows, w), t)
    return pl.pallas_call(
        functools.partial(middle_kernel, fc),
        out_shape=(
            out(model, BF),
            out(model, BF),
            out(width, BF),
            out(model, BF),
            out(width, BF),
            out(model, F32),
            out(model, BF),
            jax.ShapeDtypeStruct((8, model), F32),
            jax.ShapeDtypeStruct((1, width), F32),
        ),
        grid_spec=pltpu.PrefetchScalarGridSpec(
            num_scalar_prefetch=1,
            grid=(rows // br,),
            in_specs=[
                pl.BlockSpec(memory_space=pltpu.SMEM),
                row(model),
                here,
                here,
                row(half // 2),
                row(half // 2),
                row(model),
                fixed((8, model)),
                fixed((1, width)),
                wo(False),
                wo(True),
                pl.BlockSpec(memory_space=pl.ANY),
                pl.BlockSpec(memory_space=pl.ANY),
            ],
            out_specs=(
                row(model),
                row(model),
                row(width),
                row(model),
                row(width),
                row(model),
                row(model),
                fixed((8, model)),
                fixed((1, width)),
            ),
            scratch_shapes=[
                pltpu.VMEM(w_up.shape, BF),
                pltpu.VMEM(w_down.shape, BF),
                pltpu.VMEM((br, width), SLOPE),
                pltpu.SemaphoreType.DMA((2 * PIECES,)),
            ],
        ),
        compiler_params=pltpu.CompilerParams(vmem_limit_bytes=60 << 20),
        cost_estimate=pl.CostEstimate(
            flops=4 * rows * model * (model // 2 + 2 * width),
            bytes_accessed=4 * model * width + rows * (16 * model + 4 * width),
            transcendentals=rows * width * 2,
        ),
        name="middle",
    )(core, fraction, inp, *ctx_a, *ctx_b, cot, vecs, b_up, w_out, w_out, w_up, w_down)


def grad_kernel(count, extra, *refs):
    lhs = [r[...] for r in refs[1 : 1 + count]]
    rhs_ref = refs[1 + count]
    out_ref = refs[-1]
    left = lhs[0] if count == 1 else jnp.concatenate(lhs, axis=1)
    right = rhs_ref[0] if len(rhs_ref.shape) == 3 else rhs_ref[...]
    total = dot(left, right, TN)
    if extra:
        total = total + refs[2 + count][...].astype(F32)
    out_ref[...] = total.astype(BF)


def weight_grad(sel, lhs, rhs, add=None, cols=1024, quads=4, pairs=2):
    depth, width = lhs.shape
    three = rhs.ndim == 3
    n = rhs.shape[0] * rhs.shape[2] if three else rhs.shape[1]
    cols = rhs.shape[2] if three else cols
    w = width // (quads * pairs)
    extra = add is not None
    if w >= 512:
        grid, count = (quads,), 1
        ins = [
            pl.BlockSpec((depth, w), lambda i, s: (0, pairs * i + s[0])),
            pl.BlockSpec((depth, n), lambda i, s: (0, 0)),
        ]
        out = pl.BlockSpec((w, n), lambda i, s: (i, 0))
        args = [lhs, rhs]
    else:
        grid, count = (n // cols,), quads
        ins = [
            pl.BlockSpec((depth, w), lambda i, s, q=q: (0, pairs * q + s[0])) for q in range(quads)
        ] + [
            pl.BlockSpec((1, depth, cols), lambda i, s: (i, 0, 0))
            if three
            else pl.BlockSpec((depth, cols), lambda i, s: (0, i))
        ]
        out = pl.BlockSpec((quads * w, cols), lambda i, s: (0, i))
        args = [lhs] * quads + [rhs]
    if extra:
        ins.append(out)
        args.append(add)
    total = quads * w
    return pl.pallas_call(
        functools.partial(grad_kernel, count, extra),
        out_shape=jax.ShapeDtypeStruct((total, n), BF),
        grid_spec=pltpu.PrefetchScalarGridSpec(
            num_scalar_prefetch=1, grid=grid, in_specs=ins, out_specs=out
        ),
        compiler_params=pltpu.CompilerParams(vmem_limit_bytes=48 << 20),
        cost_estimate=pl.CostEstimate(
            flops=2 * depth * total * n,
            bytes_accessed=2 * depth * (total + n) + (4 if extra else 2) * total * n,
            transcendentals=0,
        ),
        name="weight_grad",
    )(sel, *args)


def columns_kernel(sel_ref, a_ref, b_ref, own_ref, oth_ref):
    own_ref[...] = a_ref[...]
    oth_ref[...] = b_ref[...]


def split_columns(core, w, quads):
    model, wide = w.shape
    width = wide // 6 // quads
    at = lambda flip: lambda i, s: (
        0,
        (i // quads) * 2 * quads + 2 * (i % quads) + (1 - s[0] if flip else s[0]),
    )
    out = pl.BlockSpec((model, width), lambda i, s: (0, i))
    return pl.pallas_call(
        columns_kernel,
        out_shape=(jax.ShapeDtypeStruct((model, wide // 2), BF),) * 2,
        grid_spec=pltpu.PrefetchScalarGridSpec(
            num_scalar_prefetch=1,
            grid=(3 * quads,),
            in_specs=[pl.BlockSpec((model, width), at(False)), pl.BlockSpec((model, width), at(True))],
            out_specs=(out, out),
        ),
        compiler_params=pltpu.CompilerParams(vmem_limit_bytes=8 << 20),
        cost_estimate=pl.CostEstimate(flops=0, bytes_accessed=4 * model * wide, transcendentals=0),
        name="split_columns",
    )(core, w, w)


def chosen(sel_ref, own_ref, oth_ref):
    mine = pl.program_id(0) // 2 == sel_ref[0]
    return jnp.where(mine, own_ref[...].astype(F32), oth_ref[...].astype(F32))


def project_kernel(sel_ref, frac_ref, own_ref, oth_ref, vec_ref, w_ref, bias_ref, qkv_ref, start_ref):
    start = chosen(sel_ref, own_ref, oth_ref) + (frac_ref[0] * vec_ref[0:1, :] + vec_ref[1:2, :])
    start = start.astype(BF)
    start_ref[...] = start
    half = w_ref.shape[1] // 3
    out = dot(start, w_ref[...], NN) + bias_ref[...]
    qkv_ref[:, :half] = (out[:, :half] * (0.125 * LOG2E)).astype(BF)
    qkv_ref[:, half:] = out[:, half:].astype(BF)


def project(core, fraction, own, oth, vecs, w, bias):
    rows, model = own.shape
    br = rows // 2
    fixed = lambda shape: pl.BlockSpec(shape, lambda i, s: (0, 0))
    part = pl.BlockSpec((br, model), lambda i, s: (i % 2, 0))
    out = lambda w: pl.BlockSpec((br, w), lambda i, s: (i, 0))
    return pl.pallas_call(
        project_kernel,
        out_shape=(
            jax.ShapeDtypeStruct((2 * rows, w.shape[1]), BF),
            jax.ShapeDtypeStruct((2 * rows, model), BF),
        ),
        grid_spec=pltpu.PrefetchScalarGridSpec(
            num_scalar_prefetch=1,
            grid=(4,),
            in_specs=[
                pl.BlockSpec(memory_space=pltpu.SMEM),
                part,
                part,
                fixed(vecs.shape),
                fixed(w.shape),
                fixed(bias.shape),
            ],
            out_specs=(out(w.shape[1]), out(model)),
        ),
        compiler_params=pltpu.CompilerParams(vmem_limit_bytes=40 << 20),
        cost_estimate=pl.CostEstimate(
            flops=4 * rows * model * w.shape[1],
            bytes_accessed=4 * rows * (2 * model + w.shape[1]) + 2 * model * w.shape[1],
            transcendentals=0,
        ),
        name="project",
    )(core, fraction, own, oth, vecs, w, bias)


def context_grad_kernel(sel_ref, own_ref, oth_ref, w_ref, out_ref):
    rows = chosen(sel_ref, own_ref, oth_ref).astype(BF)
    out_ref[...] = dot(rows, w_ref[...].reshape(-1, w_ref.shape[-1]), NT).astype(BF)


def context_grad(core, own, oth, w_out):
    rows, model = own.shape
    br = rows // 2
    quads, _, w, _ = w_out.shape
    part = pl.BlockSpec((br, model), lambda i, s: (i % 2, 0))
    return pl.pallas_call(
        context_grad_kernel,
        out_shape=jax.ShapeDtypeStruct((2 * rows, quads * w), BF),
        grid_spec=pltpu.PrefetchScalarGridSpec(
            num_scalar_prefetch=1,
            grid=(4,),
            in_specs=[
                part,
                part,
                pl.BlockSpec((quads, 1, w, model), lambda i, s: (0, s[0], 0, 0)),
            ],
            out_specs=pl.BlockSpec((br, quads * w), lambda i, s: (i, 0)),
        ),
        compiler_params=pltpu.CompilerParams(vmem_limit_bytes=32 << 20),
        cost_estimate=pl.CostEstimate(
            flops=4 * rows * model * quads * w,
            bytes_accessed=4 * rows * (model + quads * w) + 2 * quads * w * model,
            transcendentals=0,
        ),
        name="context_grad",
    )(core, own, oth, w_out)


def out_grad_kernel(sel_ref, a0, b0, a1, b1, own_ref, oth_ref, out_ref):
    w = a0.shape[1]
    out_ref[:w, :] = (dot(a0[...], own_ref[...], TN) + dot(b0[...], oth_ref[...], TN)).astype(BF)
    out_ref[w:, :] = (dot(a1[...], own_ref[...], TN) + dot(b1[...], oth_ref[...], TN)).astype(BF)


def out_grad(core, contexts, own, oth):
    rows, model = own.shape
    w = contexts[0].shape[1]
    here = pl.BlockSpec((rows, w), lambda i, s: (s[0], 0))
    there = pl.BlockSpec((rows, w), lambda i, s: (1 - s[0], 0))
    full = pl.BlockSpec((rows, model), lambda i, s: (0, 0))
    return pl.pallas_call(
        out_grad_kernel,
        out_shape=jax.ShapeDtypeStruct((2 * w, model), BF),
        grid_spec=pltpu.PrefetchScalarGridSpec(
            num_scalar_prefetch=1,
            grid=(1,),
            in_specs=[here, there, here, there, full, full],
            out_specs=pl.BlockSpec((2 * w, model), lambda i, s: (0, 0)),
        ),
        compiler_params=pltpu.CompilerParams(vmem_limit_bytes=40 << 20),
        cost_estimate=pl.CostEstimate(
            flops=8 * rows * model * w, bytes_accessed=8 * rows * (model + w), transcendentals=0
        ),
        name="out_grad",
    )(core, contexts[0], contexts[0], contexts[1], contexts[1], own, oth)


def finish_kernel(sel_ref, base_ref, mine_ref, got_ref, wm0, wm1, wm2, wg0, wg1, wg2, out_ref, *rest):
    total = base_ref[...]
    for t, (wm, wg) in enumerate(((wm0, wg0), (wm1, wg1), (wm2, wg2))):
        total = total + dot(mine_ref[t], wm[...], NT)
        total = total + dot(got_ref[t], wg[...], NT)
    out_ref[...] = total.astype(out_ref.dtype)
    if rest:
        step = pl.program_id(0)

        @pl.when(step == 0)
        def _():
            rest[0][...] = jnp.zeros_like(rest[0])

        rest[0][...] += jnp.sum(total, axis=0, keepdims=True)


def add_start(core, base, grads, got, w_mine, w_got, group, last, br=288):
    rows, model = base.shape
    n = got.shape[2]
    steps = rows // br
    every = w_mine.shape[1] // (3 * n)
    cols = [pl.BlockSpec((model, n), lambda i, s, t=t: (0, t * every + group)) for t in range(3)]
    row = pl.BlockSpec((br, model), lambda i, s: (i, 0))
    outs = [jax.ShapeDtypeStruct((rows, model), BF if last else F32)]
    specs = [row]
    if last:
        outs.append(jax.ShapeDtypeStruct((1, model), F32))
        specs.append(pl.BlockSpec((1, model), lambda i, s: (0, 0)))
    return pl.pallas_call(
        finish_kernel,
        out_shape=tuple(outs),
        grid_spec=pltpu.PrefetchScalarGridSpec(
            num_scalar_prefetch=1,
            grid=(steps,),
            in_specs=[
                row,
                pl.BlockSpec((3, br, n), lambda i, s: (0, s[0] * steps + i, 0)),
                pl.BlockSpec((3, br, n), lambda i, s: (0, i, 0)),
                *cols,
                *cols,
            ],
            out_specs=tuple(specs),
        ),
        compiler_params=pltpu.CompilerParams(vmem_limit_bytes=40 << 20),
        cost_estimate=pl.CostEstimate(
            flops=12 * rows * n * model,
            bytes_accessed=8 * rows * model + 12 * n * (rows + model),
            transcendentals=0,
        ),
        name="add_start",
    )(core, base, grads, got, *(w_mine,) * 3, *(w_got,) * 3)


class Plan:
    def __init__(self, mesh):
        sizes = dict(mesh.shape)
        self.batch, self.depth = sizes["batch"], sizes["seq"]
        chips = self.batch // 2
        side = 1
        while side * side < chips:
            side *= 2
        self.nx, self.ny = side, chips // side

    def perm(self, target):
        pairs = []
        for y in range(self.ny):
            for x in range(self.nx):
                for c in range(2):
                    for z in range(self.depth):
                        to = target(y, x, c, z)
                        if to != (y, x, c, z):
                            pairs.append((self.index(y, x, c, z), self.index(*to)))
        return pairs

    def index(self, y, x, c, z):
        return ((y * self.nx + x) * 2 + c) * self.depth + z

    def send(self, value, target):
        return lax.ppermute(value, AXES, self.perm(target))

    def sibling(self, value):
        return self.send(value, lambda y, x, c, z: (y, x, 1 - c, z))


def pick(array, index, axis):
    return lax.dynamic_index_in_dim(array, index, axis, keepdims=False)


def tie(*values):
    return lax.optimization_barrier(values)


class Sum:
    def __init__(self, plan, terms, where, axes="yxhl"):
        self.plan, self.terms, self.axes = plan, terms, axes
        y, x, z = where
        self.where = {"y": y, "x": x, "h": z // 2, "l": z % 2}

    def send(self, axis):
        plan, terms = self.plan, self.terms
        self.axis, self.at = axis, self.axes.index(axis)
        self.axes = self.axes.replace(axis, "")
        size = {"x": plan.nx, "y": plan.ny}.get(axis, 2)
        here = self.where[axis]
        self.got = []
        for r in range(1, size):

            def target(y, x, c, z, r=r):
                at = {"y": y, "x": x, "h": z // 2, "l": z % 2}
                at[axis] = (at[axis] + r) % size
                return at["y"], at["x"], c, 2 * at["h"] + at["l"]

            self.got.append(plan.send(pick(terms, (here + r) % size, self.at), target))
        return self

    def add(self):
        total = pick(self.terms, self.where[self.axis], self.at).astype(F32)
        for got in self.got:
            total = total + got.astype(F32)
        self.terms = total.astype(self.terms.dtype) if self.axes else total
        return self.terms

    def hold(self, *others):
        self.terms, *rest = tie(self.terms, *others)
        return rest


def per_chip(
    plan,
    inputs,
    timesteps,
    segments,
    cotangent,
    w_qkv,
    b_query,
    b_value,
    w_out,
    b_out,
    ln1_gain,
    ln1_bias,
    w_up,
    b_up,
    w_down,
    b_down,
    ln2_gain,
    ln2_bias,
    w_time,
    b_time,
):
    local_len = inputs.shape[1]
    rows = 2 * local_len
    length = segments.shape[1]
    b = lax.axis_index("batch")
    z = lax.axis_index("seq")
    c, x, y = b % 2, (b // 2) % plan.nx, b // 2 // plan.nx
    part = z % 2
    where = (y, x, z)
    first = (segments[1, 0] == segments[1, 128 * 12]).astype(jnp.int32)
    which = lambda s: (first + s) % 2
    facts = jnp.concatenate(
        [segments[:, : 128 * 13 : 128], timesteps[:, None], jnp.zeros((2, 2), jnp.int32)], axis=1
    )
    facts = jnp.stack([pick(facts, which(0), 0), pick(facts, which(1), 0)])
    other_facts = plan.sibling(facts)
    facts = jnp.where(z // 2 == c, facts, other_facts)
    mine = pick(facts, z % 2, 0)
    marks = mine[:13]
    info = jnp.concatenate(
        [
            jnp.where(marks[:1] == marks[12:], 1, jnp.where(marks[12:] == marks[:1] + 12, 2, 0)),
            jnp.sum((marks[None, :] < marks[:, None]).astype(jnp.int32), axis=1),
            jnp.sum((marks[None, :] <= marks[:, None]).astype(jnp.int32), axis=1),
        ]
    )
    fraction = mine[13].astype(F32) / TSTEPS

    stays = z // 2 == c

    def exchange(parts):
        got = [
            plan.send(v, lambda y, x, c, z, j=j: (y, x, z // 2, 2 * c + (z + j) % 2))
            for j, v in enumerate(parts)
        ]
        return [(got[0], parts[0]), (got[1], None)]

    def arrived(got):
        return [jnp.where(stays, got[0][1], got[0][0]), got[1][0]]

    def gather_parts(array):
        return [pick(array, which((part + j) % 2), 0) for j in (0, 1)]

    def gather_end(got):
        got = arrived(got)
        return jnp.concatenate(
            [jnp.where(part == 0, got[0], got[1]), jnp.where(part == 0, got[1], got[0])], axis=0
        )

    def spread_parts(array):
        array = array.reshape(2, local_len, array.shape[-1])
        return [pick(array, (part + j) % 2, 0) for j in (0, 1)]

    def spread_end(got):
        got = arrived(got)
        swap = (part + first) % 2
        return jnp.stack(
            [jnp.where(swap == 0, got[0], got[1]), jnp.where(swap == 0, got[1], got[0])], axis=0
        )

    def whole(own, other):
        return jnp.where(c == 0, jnp.concatenate([own, other]), jnp.concatenate([other, own]))

    def halves(array, axis):
        shape = array.shape
        cut = shape[:axis] + (plan.ny * plan.nx, 2, -1) + shape[axis + 1 :]
        flat = shape[:axis] + (-1,) + shape[axis + 1 :]
        split = array.reshape(cut)
        return (
            pick(split, c, axis + 1).reshape(flat),
            pick(split, 1 - c, axis + 1).reshape(flat),
        )

    def blocks(array):
        return array.reshape(plan.ny, plan.nx, 2, 2, -1, array.shape[-1])

    model = inputs.shape[-1]
    half = model // 2
    quads = plan.ny * plan.nx
    core = jnp.stack([c]).astype(jnp.int32)
    away = 1 - core
    w_own, w_oth = split_columns(core, w_qkv, quads)
    bias = jnp.concatenate(
        [
            halves(b_query.astype(F32), 0)[0],
            jnp.zeros((half,), F32),
            halves(b_value.astype(F32), 0)[0],
        ]
    )
    w_out_four = w_out.reshape(quads, 2, -1, model)
    ahead = [range(0, quads // 2), range(quads // 2, quads)]
    groups = ahead
    own_inputs = gather_end(exchange(gather_parts(inputs)))
    vecs = jnp.stack(
        [v.astype(F32) for v in (w_time, b_time, b_out, ln1_gain, ln1_bias, b_down, ln2_gain, ln2_bias)]
    )
    cot_parts = gather_parts(cotangent)
    bias = bias[None]
    own_inputs, w_own, w_oth, vecs, info, bias, cot_parts = tie(
        own_inputs, w_own, w_oth, vecs, info, bias, cot_parts
    )
    sib_inputs = plan.sibling(own_inputs)
    cot_parts, sib_inputs = tie(cot_parts, sib_inputs)
    own_cotangent = gather_end(exchange(cot_parts))
    qkv, start_full = project(core, fraction[None], own_inputs, sib_inputs, vecs, w_own, bias)
    fwd = [attn_fwd(info, qkv, g.start, len(g)) for g in ahead]
    away_of = [
        plan.sibling(pick(f[0].reshape(2, rows, -1), 1 - c, 0)) for f in fwd
    ]
    result, normed_low, act, two_low, hid, grad_one, one_low, small_sums, up_sums = middle(
        core,
        fraction[None],
        own_inputs,
        [f[0] for f in fwd],
        away_of,
        own_cotangent,
        vecs,
        b_up.astype(F32)[None],
        w_out_four,
        w_up,
        w_down,
    )
    one_sib = plan.sibling(one_low)
    output_got = exchange(spread_parts(result))
    down_part = weight_grad(away, act, two_low, quads=quads)
    normed_low, down_part = tie(normed_low, down_part)
    down_got = plan.sibling(down_part)
    up_part = weight_grad(away, normed_low, hid, quads=quads)
    act, up_part = tie(act, up_part)
    up_got = plan.sibling(up_part)
    down_sum = weight_grad(core, act, two_low, down_got, quads=quads)
    normed_low, down_sum = tie(normed_low, down_sum)
    down = Sum(plan, blocks(down_sum), where).send("x")
    up_sum = weight_grad(core, normed_low, hid, up_got, quads=quads)
    one_low, one_sib, up_sum = tie(one_low, one_sib, up_sum)
    up = Sum(plan, blocks(up_sum), where).send("y")
    out_sum = out_grad(core, [f[0] for f in fwd], one_low, one_sib)
    one_low, one_sib, out_sum = tie(one_low, one_sib, out_sum)
    out = Sum(plan, blocks(out_sum), where).send("x")
    grad_context = context_grad(core, one_low, one_sib, w_out_four)

    def back(first, count, into=None):
        f = first // (quads // 2)
        start = ahead[f].start
        return attn_bwd(
            info,
            fwd[f][2],
            qkv,
            fwd[f][0],
            fwd[f][1],
            grad_context,
            first,
            count,
            first - start,
            quads // 2,
            first - start,
            into,
        )

    def away_rows(grads):
        return plan.sibling(pick(grads.reshape(3, 2, rows, -1), 1 - c, 1))

    def products(grads):
        cross_part = weight_grad(away, start_full, grads, quads=quads)
        grads, cross_part = tie(grads, cross_part)
        cross = plan.sibling(cross_part)
        keep = weight_grad(core, start_full, grads, quads=quads)
        return Sum(plan, blocks(cross), where), Sum(plan, blocks(keep), where)

    def settle(items, other):
        for item in items:
            item.got, other = tie(item.got, other)
            item.add()
            item.terms, other = tie(item.terms, other)
        return other

    grads0, b_sum0 = back(0, quads // 2)
    got0 = away_rows(grads0)
    output_got, grads0 = tie(output_got, grads0)
    grads0 = settle([down, up, out], grads0)
    grad_context, grads0 = tie(grad_context, grads0)
    down.send("y")
    up.send("x")
    out.send("y")
    grads, b_sum1 = back(quads // 2, quads // 4)
    grads, grads0, got0 = tie(grads, grads0, got0)
    grads0 = settle([down, up, out], grads0)
    wide_rows = up.terms.shape[-2]
    slabs = [up.terms[..., i * model : (i + 1) * model] for i in range(up.terms.shape[-1] // model)]
    ffn = jnp.concatenate([down.terms, *slabs, out.terms], axis=2)
    ffn, grads0 = tie(ffn, grads0)
    ffn = Sum(plan, ffn, where, "hl").send("l")
    cross0, keep0 = products(grads0)
    got0, cross0.terms, keep0.terms = tie(got0, cross0.terms, keep0.terms)
    keep0.send("x")
    cross0.send("y")
    (grad_start,) = add_start(core, grad_one, grads0, got0, w_own, w_oth, 0, False)
    grads, grad_start = tie(grads, grad_start)
    grads, b_sum2 = back(quads // 2 + quads // 4, quads // 4, grads)
    got = away_rows(grads)
    grads = settle([ffn, keep0, cross0], grads)
    ffn.send("h")
    keep0.send("y")
    cross0.send("x")
    cross1, keep1 = products(grads)
    got, keep1.terms = tie(got, keep1.terms)
    keep1.send("x")
    cross1.send("y")
    grad_low, b_time_sum = add_start(core, grad_start, grads, got, w_own, w_oth, 1, True)
    in_parts, b_time_sum = tie(spread_parts(grad_low), b_time_sum)
    grad_inputs_got = exchange(in_parts)
    b_time_sum = settle([keep0, cross0, keep1, cross1], b_time_sum)
    ffn.got, b_time_sum = tie(ffn.got, b_time_sum)
    keep1.send("y")
    cross1.send("x")
    small_sums, up_sums, b_time_sum = tie(small_sums, up_sums, b_time_sum)
    b_sum = jnp.concatenate([b_sum0, b_sum1, b_sum2], axis=1)
    zero = jnp.zeros((quads, 2, half // quads), F32)

    def placed(v):
        return lax.dynamic_update_index_in_dim(zero, v.reshape(quads, half // quads), c, 1).reshape(-1)

    vectors = [small_sums[i] for i in range(6)]
    vectors += [placed(b_sum[0]), placed(b_sum[1]), fraction * b_time_sum[0], b_time_sum[0]]
    small = jnp.concatenate([v[:, None] for v in vectors] + [up_sums.reshape(model, -1)], axis=1)
    small_own, small_oth = halves(small, 0)
    small = Sum(plan, blocks(small_own + plan.sibling(small_oth)), where)
    small.send("x").add()
    small.send("y")
    keep1.got, cross1.got, small.got, grad_inputs_got = tie(
        keep1.got, cross1.got, small.got, grad_inputs_got
    )
    keep1.add()
    cross1.add()
    small.add()
    late = jnp.concatenate([i.terms for i in (keep0, cross0, keep1, cross1)], axis=3)
    late = Sum(plan, late, where, "hl").send("l")
    small.send("l")
    late.got, small.got = tie(late.got, small.got)
    late.add()
    small.add()
    late.send("h")
    small.send("h")
    small.add()
    small = small.terms
    late = late.add()
    wide = 3 * half // 2
    keeps = [late[:, :wide], late[:, 2 * wide : 3 * wide]]
    crosses = [late[:, wide : 2 * wide], late[:, 3 * wide : 4 * wide]]
    ffn = ffn.add()
    count = ffn.shape[0] - wide_rows * (len(slabs) + 1)
    sum_w_down, sum_w_out = ffn[:count], ffn[count + wide_rows * len(slabs) :]
    sum_w_up = jnp.concatenate(
        [ffn[count + i * wide_rows : count + (i + 1) * wide_rows] for i in range(len(slabs))], axis=1
    )
    output = spread_end(output_got)
    grad_inputs = spread_end(grad_inputs_got)
    split3 = lambda parts: jnp.concatenate(
        [p.reshape(p.shape[0], 3, len(g), -1) for p, g in zip(parts, groups)], axis=2
    )
    sum_own, sum_oth = split3(keeps), split3(crosses)
    pair = jnp.where(c == 0, jnp.stack([sum_own, sum_oth]), jnp.stack([sum_oth, sum_own]))
    sum_w_qkv = (
        pair.transpose(1, 2, 3, 0, 4).reshape(-1, 3 * model)
    )
    v = [small[:, i] for i in (6, 7, 0, 1, 2, 3, 4, 5, 8, 9)]
    return (
        output,
        grad_inputs,
        sum_w_qkv,
        v[0],
        v[1],
        sum_w_out,
        v[2],
        v[3],
        v[4],
        sum_w_up,
        small[:, 10:].reshape(-1),
        sum_w_down,
        v[5],
        v[6],
        v[7],
        v[8],
        v[9],
    )


def solution(mesh):
    placed = (
        P("batch", "seq", None),
        P("batch"),
        P("batch", None),
        P("batch", "seq", None),
        P(),
        P(),
        P(),
        P(),
        P(),
        P(),
        P(),
        P(),
        P(),
        P(),
        P(),
        P(),
        P(),
        P(),
        P(),
    )
    sizes = dict(mesh.shape)
    body = per_device
    if sizes["seq"] == 4 and sizes["batch"] % 2 == 0:
        body = functools.partial(per_chip, Plan(mesh))
    return jax.shard_map(
        body,
        mesh=mesh,
        in_specs=placed,
        out_specs=(
            P("batch", "seq", None),
            P("batch", "seq", None),
            P(("batch", "seq"), None),
            P(("batch", "seq")),
            P(("batch", "seq")),
            P(("batch", "seq"), None),
            P(("batch", "seq")),
            P(("batch", "seq")),
            P(("batch", "seq")),
            P(("batch", "seq"), None),
            P(("batch", "seq")),
            P(("batch", "seq"), None),
            P(("batch", "seq")),
            P(("batch", "seq")),
            P(("batch", "seq")),
            P(("batch", "seq")),
            P(("batch", "seq")),
        ),
        check_vma=False,
    )
```
